512 devices in a mesh: sfc: 512 (over x, y, z, core).
Axes of the slice: x: 4, y: 4, z: 16, core: 2. Of those that a mesh axis runs over, the one named last changes fastest.
Arguments:
- fields: float32 [6, 64, 65536], P(None, None, 'sfc'), may hold values from -6 to 6
- material: float32 [2, 65536], P(None, 'sfc'), may hold values from 0.25 to 1
- refinement: int32 [65536], P('sfc'), may hold values from 0 to 2
- face_source: int32 [6, 65536], P(None, 'sfc'), may hold values from 0 to 2303, as said below
- face_code: int32 [6, 65536], P(None, 'sfc'), may hold values from 0 to 48, as said below
- send_face: int32 [8, 98304], P(None, 'sfc'), may hold values from 0 to 767, as said below
- mortar_source: int32 [4, 32768], P(None, 'sfc'), may hold values from 0 to 2303, as said below
- mortar_code: int32 [4, 32768], P(None, 'sfc'), may hold values from 0 to 7
- mortar_target: int32 [32768], P('sfc'), may hold values from -1 to 767, as said below
Outputs:
- new_fields: float32 [6, 64, 65536], P(None, None, 'sfc')
- register: float32 [6, 64, 65536], P(None, None, 'sfc')
The draws below stay inside these ranges and needn't reach their ends.
Inputs may be any that keep to these rules, and one draw needn't show every extreme that they name: `face_source`: A value below 768 names a local face of the same block; a larger value 6 * 128 + k * 192 + s names slot s of list k of the block o_k places before, with o_k = k - 4 for k < 4, else k - 3, and that block exists. Boundary faces and coarse faces name themselves. face_code // 8 is the kind: 0 conforming, 1 boundary, 2 + q the fine face on quarter q of a coarse face, 6 a coarse face with four fine neighbours; face_code % 8 is the orientation code, 0 on boundary and coarse faces. A face has kind 6 exactly when a mortar row of its block targets it. `send_face`: local faces of the listing block. `mortar_source`: encoded as face_source, for the block that holds the row. `mortar_target`: A local face of the row's block, each one at most once; -1 marks a padding row, and padding rows follow the live rows of their block. Every block has 12 or more live rows, and some block has no padding row.
All inputs are finite; a program needn't handle non-finite values.
Results may differ from the reference program's by a relative error of at most 0.0003.
Values sent between devices are 32-bit elements; how exact they have to be, the bound alone decides.
No kernel may reach another device: no remote copies, remote signals or barrier semaphores. Data moves between devices by JAX's collectives and lax.ppermute only.
A program may use at most 64 MiB of HBM per device.

```python
import math
import jax
import jax.numpy as jnp
import numpy as np
from jax import lax

E_DEV = 128
SLOTS = 192
MORTAR = 64
REACH = 4
FIELDS = 6
NODES = 64
NE = 65536
N_SFC = 512


def source_codes(key, block_index, shape):
    faces_local = 6 * E_DEV
    subkeys = jax.random.split(key, 4)
    local_face = jax.random.randint(subkeys[0], shape, 0, faces_local, dtype=jnp.int32)
    direction = jax.random.randint(subkeys[1], shape, 0, 2 * REACH, dtype=jnp.int32)
    slot_index = jax.random.randint(subkeys[2], shape, 0, SLOTS, dtype=jnp.int32)
    offset = jnp.where(direction < REACH, direction - REACH, direction - REACH + 1)
    sender = block_index - offset
    exists = (sender >= 0) & (sender < N_SFC)
    remote = jax.random.randint(subkeys[3], shape, 0, 3, dtype=jnp.int32) == 0
    return jnp.where(remote & exists, faces_local + direction * SLOTS + slot_index, local_face)


def mesh_lists(key):
    faces_local = 6 * E_DEV
    elements = E_DEV * N_SFC
    subkeys = jax.random.split(key, 10)
    send_face = jax.random.randint(subkeys[0], (2 * REACH, N_SFC * SLOTS), 0, faces_local, dtype=jnp.int32)
    order_keys = jax.random.split(subkeys[1], N_SFC)
    chosen = jax.vmap(lambda one_key: jax.random.permutation(one_key, faces_local)[:MORTAR])(order_keys).astype(jnp.int32)
    divisor = 1 + jax.random.randint(subkeys[2], (N_SFC,), 0, 5, dtype=jnp.int32)
    full_block = jax.random.randint(subkeys[3], (), 0, N_SFC, dtype=jnp.int32)
    block_ids = jnp.arange(N_SFC, dtype=jnp.int32)
    live_rows = jnp.where(block_ids == full_block, MORTAR, MORTAR // divisor)
    row_index = jnp.arange(MORTAR, dtype=jnp.int32)
    targets = jnp.where(row_index[None, :] < live_rows[:, None], chosen, -1)
    marked = jnp.zeros((N_SFC, faces_local + 1), jnp.int32)
    marked = marked.at[block_ids[:, None], jnp.where(targets >= 0, targets, faces_local)].set(1)
    coarse = marked[:, :faces_local].reshape(N_SFC, 6, E_DEV).transpose(1, 0, 2).reshape(6, elements) == 1
    element_ids = jnp.arange(elements, dtype=jnp.int32)
    face_block = jnp.broadcast_to(element_ids // E_DEV, (6, elements))
    own_face = jnp.arange(6, dtype=jnp.int32)[:, None] * E_DEV + (element_ids % E_DEV)[None, :]
    chance = jax.random.randint(subkeys[4], (6, elements), 0, 100, dtype=jnp.int32)
    quarter = jax.random.randint(subkeys[5], (6, elements), 0, 4, dtype=jnp.int32)
    base_kind = jnp.where(chance < 5, 1, jnp.where(chance < 17, 2 + quarter, 0))
    face_kind = jnp.where(coarse, 6, base_kind)
    orientation = jax.random.randint(subkeys[6], (6, elements), 0, 8, dtype=jnp.int32)
    own_only = (face_kind == 1) | (face_kind == 6)
    face_code = (face_kind * 8 + jnp.where(own_only, 0, orientation)).astype(jnp.int32)
    face_source = jnp.where(own_only, own_face, source_codes(subkeys[7], face_block, (6, elements))).astype(jnp.int32)
    mortar_block = jnp.broadcast_to(jnp.arange(N_SFC * MORTAR, dtype=jnp.int32) // MORTAR, (4, N_SFC * MORTAR))
    mortar_source = source_codes(subkeys[8], mortar_block, (4, N_SFC * MORTAR)).astype(jnp.int32)
    mortar_code = jax.random.randint(subkeys[9], (4, N_SFC * MORTAR), 0, 8, dtype=jnp.int32)
    return (face_source, face_code, send_face, mortar_source, mortar_code, targets.reshape(N_SFC * MORTAR).astype(jnp.int32))


def draw_face_source(key, part):
    lists = mesh_lists(key)
    return lists[0]


def draw_face_code(key, part):
    lists = mesh_lists(key)
    return lists[1]


def draw_send_face(key, part):
    lists = mesh_lists(key)
    return lists[2]


def draw_mortar_source(key, part):
    lists = mesh_lists(key)
    return lists[3]


def draw_mortar_code(key, part):
    lists = mesh_lists(key)
    return lists[4]


def draw_mortar_target(key, part):
    lists = mesh_lists(key)
    return lists[5]


def set_ends(entries, rng, least, largest):
    longest = entries.shape.index(max(entries.shape))
    spots = []
    for shift in (0, 1):
        where = [jax.random.randint(jax.random.fold_in(rng, axis), (), 0, length) for axis, length in enumerate(entries.shape)]
        where[longest] = (where[longest] + shift) % entries.shape[longest]
        spots.append(tuple(where))
    return entries.at[spots[0]].set(least).at[spots[1]].set(largest)


def block_scale(stream_key, shape, cuts, low, largest):
    factor_of, own = 1.0, jax.random.fold_in(stream_key, 6)
    for axis_at, blocks in cuts:
        steps = jnp.exp(jax.random.uniform(jax.random.fold_in(own, axis_at), (blocks,), jnp.float32, low / len(cuts), largest / len(cuts)))
        factor_of = factor_of * jnp.repeat(steps, shape[axis_at] // blocks).reshape([-1 if axis == axis_at else 1 for axis in range(len(shape))])
    return factor_of


def scatter_about(rng, shape, width, most, cuts=(), kind=jnp.bfloat16):
    gain = block_scale(rng, shape, cuts, -0.22, 0.18) if cuts else 1.0
    entries = jax.random.normal(rng, shape, jnp.float32) * width * gain
    return jnp.minimum(jnp.maximum(entries, -most), most).astype(kind)


def setup_inputs(seed: int = 0) -> dict:
    arg_keys = jax.random.split(jax.random.key(seed), 10)
    return {
        "fields": scatter_about(arg_keys[0], (FIELDS, NODES, NE), 1.0, 6.0, ((2, 512),), jnp.float32),
        "material": jnp.clip(jnp.exp(math.log(1.0) - 1.3862944 * jax.random.uniform(arg_keys[1], (2, NE), jnp.float32) ** block_scale(arg_keys[1], (2, NE), ((1, 512),), -0.2, 0.2)), 0.25, 1.0),
        "refinement": set_ends(jax.random.randint(arg_keys[2], (NE,), 0, 3), jax.random.fold_in(arg_keys[2], 1), 0, 2).astype(jnp.int32),
        "face_source": draw_face_source(jax.random.fold_in(arg_keys[9], 71), 0),
        "face_code": draw_face_code(jax.random.fold_in(arg_keys[9], 71), 0),
        "send_face": draw_send_face(jax.random.fold_in(arg_keys[9], 71), 0),
        "mortar_source": draw_mortar_source(jax.random.fold_in(arg_keys[9], 71), 0),
        "mortar_code": draw_mortar_code(jax.random.fold_in(arg_keys[9], 71), 0),
        "mortar_target": draw_mortar_target(jax.random.fold_in(arg_keys[9], 71), 0),
    }


STEP_SIZE = 0.02
SECTION_A = (0.0, -567301805773.0 / 1357537059087.0)
SECTION_B = (1432997174477.0 / 9575080441755.0, 5161836677717.0 / 13612068292357.0)

def gll_tables():
    points = np.array([-1.0, -1.0 / math.sqrt(5.0), 1.0 / math.sqrt(5.0), 1.0])
    weights = np.array([1.0, 5.0, 5.0, 1.0]) / 6.0

    def lagrange(where_at):
        values = np.ones((where_at.shape[0], 4))
        for column in range(4):
            for another in range(4):
                if another != column:
                    values[:, column] *= (where_at - points[another]) / (points[column] - points[another])
        return values
    derivative = np.zeros((4, 4))
    for row_at in range(4):
        for column in range(4):
            summed = 0.0
            for another in range(4):
                if another == column:
                    continue
                factor = 1.0 / (points[column] - points[another])
                for further in range(4):
                    if further != column and further != another:
                        factor *= (points[row_at] - points[further]) / (points[column] - points[further])
                summed += factor
            derivative[row_at, column] = summed
    halves = [lagrange((points - 1.0) / 2.0), lagrange((points + 1.0) / 2.0)]
    adjoint = [0.5 * halfway.T * weights[None, :] / weights[:, None] for halfway in halves]
    interpolate = [np.kron(halves[quarter % 2], halves[quarter // 2]) for quarter in range(4)] + [np.eye(16)]
    projection = [np.kron(adjoint[quarter % 2], adjoint[quarter // 2]) for quarter in range(4)]
    normals = np.zeros((3, 6))
    for facing in range(6):
        normals[facing // 2, facing] = 1.0 if facing % 2 == 1 else -1.0
    return (jnp.asarray(derivative, jnp.float32), jnp.asarray(np.stack(interpolate), jnp.float32), jnp.asarray(np.stack(projection), jnp.float32), jnp.asarray(normals, jnp.float32))

def face_traces(nodal_grid):
    elements = nodal_grid.shape[-1]
    sides = [nodal_grid[:, 0], nodal_grid[:, 3], nodal_grid[:, :, 0], nodal_grid[:, :, 3], nodal_grid[:, :, :, 0], nodal_grid[:, :, :, 3]]
    return jnp.stack([facing.reshape(6, 16, elements) for facing in sides], axis=2)

def oriented(trace_table, columns, orient_codes):
    corners = jnp.arange(16, dtype=jnp.int32)[:, None, None]
    first_axis = corners // 4
    second = corners % 4
    orient_codes = orient_codes[None]
    along_a = jnp.where(orient_codes % 2 == 1, 3 - first_axis, first_axis)
    along_b = jnp.where(orient_codes // 2 % 2 == 1, 3 - second, second)
    source = jnp.where(orient_codes >= 4, 4 * along_b + along_a, 4 * along_a + along_b)
    return trace_table[:, source, columns[None]]

def cross_product(normal, vector):
    return jnp.stack([normal[1] * vector[2] - normal[2] * vector[1], normal[2] * vector[0] - normal[0] * vector[2], normal[0] * vector[1] - normal[1] * vector[0]])

def lifted(flux, metric):
    elements = flux.shape[-1]
    weight = 3.0 * metric
    volume = jnp.zeros((3, 4, 4, 4, elements), flux.dtype)
    volume = volume.at[:, 0].add(flux[:, :, 0].reshape(3, 4, 4, elements) * weight)
    volume = volume.at[:, 3].add(flux[:, :, 1].reshape(3, 4, 4, elements) * weight)
    volume = volume.at[:, :, 0].add(flux[:, :, 2].reshape(3, 4, 4, elements) * weight)
    volume = volume.at[:, :, 3].add(flux[:, :, 3].reshape(3, 4, 4, elements) * weight)
    volume = volume.at[:, :, :, 0].add(flux[:, :, 4].reshape(3, 4, 4, elements) * weight)
    volume = volume.at[:, :, :, 3].add(flux[:, :, 5].reshape(3, 4, 4, elements) * weight)
    return volume

def curl_of(vector, derivative, metric):
    highest = lax.Precision.HIGHEST
    along_x = jnp.einsum('ia,fajke->fijke', derivative, vector[1:3], precision=highest) * metric
    along_y = jnp.einsum('ja,fiake->fijke', derivative, vector[0::2], precision=highest) * metric
    along_z = jnp.einsum('ka,fijae->fijke', derivative, vector[0:2], precision=highest) * metric
    return jnp.stack([along_y[1] - along_z[1], along_z[0] - along_x[1], along_x[0] - along_y[0]])

def block_rates(solution, material, metric, inside, face_columns, face_code, mortar_columns, mortar_code, mortar_target, trace_table, tables):
    derivative, interpolate, projection, normals = tables
    highest = lax.Precision.HIGHEST
    elements = solution.shape[-1]
    nodal_grid = solution.reshape(6, 4, 4, 4, elements)
    face_kind = face_code // 8
    raw_trace = oriented(trace_table, face_columns, face_code % 8)
    exterior = raw_trace
    for quarter in range(4):
        refined = jnp.einsum('mn,fnge->fmge', interpolate[quarter], raw_trace, precision=highest)
        exterior = jnp.where(face_kind[None, None] == 2 + quarter, refined, exterior)
    field_ids = jnp.arange(6, dtype=jnp.int32)[:, None, None, None]
    exterior = jnp.where((face_kind[None, None] == 1) & (field_ids < 3), -exterior, exterior)
    pieces = oriented(trace_table, mortar_columns, mortar_code)
    mortar_value = jnp.einsum('qmn,fnqr->fmr', projection, pieces, precision=highest)
    target_column = jnp.where(mortar_target >= 0, mortar_target, 6 * elements)
    placed = jnp.zeros((6, 16, 6 * elements + 1), jnp.float32).at[:, :, target_column].set(mortar_value)
    placed = placed[:, :, :6 * elements].reshape(6, 16, 6, elements)
    exterior = jnp.where(face_kind[None, None] == 6, placed, exterior)
    jump_e = exterior[0:3] - inside[0:3]
    jump_h = exterior[3:6] - inside[3:6]
    normal = normals[:, None, :, None]
    flux_e = cross_product(normal, jump_h) - (jump_e - lax.optimization_barrier(jnp.sum(normal * jump_e, axis=0)) * normal)
    flux_h = -cross_product(normal, jump_e) - (jump_h - lax.optimization_barrier(jnp.sum(normal * jump_h, axis=0)) * normal)
    curl_e = curl_of(nodal_grid[0:3], derivative, metric)
    curl_h = curl_of(nodal_grid[3:6], derivative, metric)
    rate_e = material[0] * (curl_h + lifted(flux_e, metric))
    rate_h = material[1] * (lifted(flux_h, metric) - curl_e)
    return jnp.concatenate([rate_e, rate_h], axis=0).reshape(6, 64, elements)

def resolve(values, block_index, send_face):
    faces_local = 6 * E_DEV
    remote = jnp.maximum(values - faces_local, 0)
    direction = remote // SLOTS
    offset = jnp.where(direction < REACH, direction - REACH, direction - REACH + 1)
    sender = jnp.clip(block_index - offset, 0, N_SFC - 1)
    sent_face = send_face[direction, sender * SLOTS + remote % SLOTS]
    is_local = values < faces_local
    owner_block = jnp.where(is_local, block_index, sender)
    face_local = jnp.where(is_local, values, sent_face)
    return face_local // E_DEV * NE + owner_block * E_DEV + face_local % E_DEV

def reference(fields, material, refinement, face_source, face_code, send_face, mortar_source, mortar_code, mortar_target):
    tables = gll_tables()
    metric = jnp.left_shift(jnp.ones_like(refinement), refinement).astype(jnp.float32)
    solution = fields
    register = jnp.zeros_like(fields)
    for section_index in range(2):
        trace_table = face_traces(solution.reshape(6, 4, 4, 4, NE)).reshape(6, 16, 6 * NE)

        def per_block(block_index):
            first_element = block_index * E_DEV
            first_row = block_index * MORTAR

            def element_slice(array):
                return lax.dynamic_slice_in_dim(array, first_element, E_DEV, array.ndim - 1)

            def mortar_slice(array):
                return lax.dynamic_slice_in_dim(array, first_row, MORTAR, array.ndim - 1)
            block_state = element_slice(solution)
            inside = face_traces(block_state.reshape(6, 4, 4, 4, E_DEV))
            face_columns = resolve(element_slice(face_source), block_index, send_face)
            mortar_columns = resolve(mortar_slice(mortar_source), block_index, send_face)
            return block_rates(block_state, element_slice(material), element_slice(metric), inside, face_columns, element_slice(face_code), mortar_columns, mortar_slice(mortar_code), mortar_slice(mortar_target), trace_table, tables)
        section_rates = lax.map(per_block, jnp.arange(N_SFC, dtype=jnp.int32))
        section_rates = jnp.transpose(section_rates, (1, 2, 0, 3)).reshape(6, 64, NE)
        register = SECTION_A[section_index] * register + STEP_SIZE * section_rates
        solution = solution + SECTION_B[section_index] * register
    return (solution, register)
```

```python
import math

import jax
import jax.numpy as jnp
import numpy as np
from jax import lax
from jax.experimental import pallas as pl
from jax.experimental.pallas import tpu as pltpu
from jax.sharding import PartitionSpec as P

STEP_SIZE = 0.02
SECTION_A = (0.0, -567301805773.0 / 1357537059087.0)
SECTION_B = (1432997174477.0 / 9575080441755.0, 5161836677717.0 / 13612068292357.0)
UNIT = 144
LANES = 128
VMEM_LIMIT = 32 * 1024 * 1024


def gll_tables():
    points = np.array([-1.0, -1.0 / math.sqrt(5.0), 1.0 / math.sqrt(5.0), 1.0])
    weights = np.array([1.0, 5.0, 5.0, 1.0]) / 6.0

    def lagrange(where_at):
        values = np.ones((where_at.shape[0], 4))
        for column in range(4):
            for another in range(4):
                if another != column:
                    values[:, column] *= (where_at - points[another]) / (
                        points[column] - points[another]
                    )
        return values

    derivative = np.zeros((4, 4))
    for row_at in range(4):
        for column in range(4):
            summed = 0.0
            for another in range(4):
                if another == column:
                    continue
                factor = 1.0 / (points[column] - points[another])
                for further in range(4):
                    if further != column and further != another:
                        factor *= (points[row_at] - points[further]) / (
                            points[column] - points[further]
                        )
                summed += factor
            derivative[row_at, column] = summed
    halves = [lagrange((points - 1.0) / 2.0), lagrange((points + 1.0) / 2.0)]
    adjoint = [0.5 * halfway.T * weights[None, :] / weights[:, None] for halfway in halves]
    return derivative, halves, adjoint


def face_nodes(face):
    grid = np.arange(64).reshape(4, 4, 4)
    at = 3 if face % 2 else 0
    return [grid[at], grid[:, at], grid[:, :, at]][face // 2].reshape(16)


def volume_map():
    derivative, _, _ = gll_tables()
    eye = np.eye(4)
    along = [
        np.kron(np.kron(derivative, eye), eye),
        np.kron(np.kron(eye, derivative), eye),
        np.kron(np.kron(eye, eye), derivative),
    ]
    whole = np.zeros((6, 64, 6, 64))
    for a in range(3):
        b, c = (a + 1) % 3, (a + 2) % 3
        whole[a, :, 3 + c] += along[b]
        whole[a, :, 3 + b] -= along[c]
        whole[3 + a, :, c] -= along[b]
        whole[3 + a, :, b] += along[c]
    for face in range(6):
        a = face // 2
        b, c = (a + 1) % 3, (a + 2) % 3
        s = 1.0 if face % 2 else -1.0
        for n in face_nodes(face):
            whole[b, n, b, n] += 3.0
            whole[b, n, 3 + c, n] += 3.0 * s
            whole[c, n, c, n] += 3.0
            whole[c, n, 3 + b, n] -= 3.0 * s
            whole[3 + b, n, 3 + b, n] += 3.0
            whole[3 + b, n, c, n] -= 3.0 * s
            whole[3 + c, n, 3 + c, n] += 3.0
            whole[3 + c, n, b, n] += 3.0 * s
    return whole.reshape(384, 384)


def volume_operand():
    whole = volume_map().astype(np.float32)
    high = whole.astype(jnp.bfloat16)
    low = (whole - high.astype(np.float32)).astype(jnp.bfloat16)
    return np.concatenate([high, high, low], axis=1)


def halves_of(value):
    high = value.astype(jnp.bfloat16)
    low = (value - high.astype(jnp.float32)).astype(jnp.bfloat16)
    return high, low


def one_hot(rows, columns):
    at = lax.broadcasted_iota(jnp.int32, (rows, columns.shape[1]), 0)
    return jnp.where(at == columns, 1.0, 0.0).astype(jnp.bfloat16)


def picked(table, columns):
    rows = table.shape[0]
    both = jnp.concatenate(halves_of(table), axis=0)
    out = jnp.dot(both, columns, preferred_element_type=jnp.float32)
    return out[:rows] + out[rows:]


def write_table(u_ref, t_ref):
    for f in range(6):
        base = 64 * f
        rows = slice(16 * f, 16 * f + 16)
        t_ref[rows, 0:128] = u_ref[base : base + 16, :]
        t_ref[rows, 128:256] = u_ref[base + 48 : base + 64, :]
        for side, at in ((2, 0), (3, 12)):
            for i in range(4):
                start = base + 16 * i + at
                t_ref[16 * f + 4 * i : 16 * f + 4 * i + 4, 128 * side : 128 * side + 128] = u_ref[
                    start : start + 4, :
                ]
        t_ref[rows, 512:640] = u_ref[pl.ds(base, 16, stride=4), :]
        t_ref[rows, 640:768] = u_ref[pl.ds(base + 3, 16, stride=4), :]


def write_lists(core, t_ref, send_ref, swap_ref, own_ref):
    def listed(k, lanes):
        return jnp.where(core == 0, send_ref[k : k + 1, lanes], send_ref[7 - k : 8 - k, lanes])

    columns = [listed(k, slice(0, 128)) for k in range(8)]
    for pair in range(4):
        columns.append(
            jnp.concatenate(
                [listed(2 * pair, slice(128, 192)), listed(2 * pair + 1, slice(128, 192))], axis=1
            )
        )
    spread = jnp.concatenate([one_hot(768, column) for column in columns], axis=1)
    out = picked(t_ref[...], spread)
    first = lax.broadcasted_iota(jnp.int32, (48, LANES), 1) < 64
    places = {4 - d: (swap_ref, d - 1) for d in range(1, 5)}
    places[4] = (swap_ref, 4)
    places.update({3 + d: (own_ref, d - 2) for d in range(2, 5)})
    for k in range(8):
        ref, place = places[k]
        ref[UNIT * place : UNIT * place + 96, :] = out[:, 128 * k : 128 * k + 128]
        at = 1024 + 128 * (k // 2)
        upper, lower = out[0:48, at : at + 128], out[48:96, at : at + 128]
        if k % 2 == 0:
            packed = jnp.where(first, upper, pltpu.roll(lower, 64, 1))
        else:
            packed = jnp.where(first, pltpu.roll(upper, 64, 1), lower)
        ref[UNIT * place + 96 : UNIT * place + UNIT, :] = packed


def lists_kernel(core_ref, u_ref, send_ref, swap_ref, own_ref, t_ref):
    write_table(u_ref, t_ref)
    write_lists(core_ref[0], t_ref, send_ref, swap_ref, own_ref)


def mortar_row(ref):
    return jnp.concatenate([ref[q : q + 1, :] for q in range(4)], axis=1)


def local_kernel(u_ref, volume_ref, face_ref, mortar_ref, rate_ref, part_ref, t_ref):
    high, low = halves_of(u_ref[...])
    rate_ref[...] = jnp.dot(
        volume_ref[...],
        jnp.concatenate([high, low, high], axis=0),
        preferred_element_type=jnp.float32,
    )
    write_table(u_ref, t_ref)
    columns = [face_ref[face : face + 1, :] for face in range(6)] + [mortar_row(mortar_ref)]
    spread = jnp.concatenate([one_hot(768, column) for column in columns], axis=1)
    part_ref[...] = picked(t_ref[...], spread)


def write_received(core, swapped_ref, near_ref, far_ref, shared_ref, r_ref):
    other = 1 - core
    swapped = pl.multiple_of(other * (5 * UNIT) + 4 * UNIT, 8)
    shared = [pl.multiple_of(other * (3 * UNIT) + UNIT * place, 8) for place in range(3)]
    sources = [
        (shared_ref, shared[2]),
        (shared_ref, shared[0]),
        (shared_ref, shared[1]),
        (swapped_ref, swapped),
        (near_ref, UNIT),
        (near_ref, 0),
        (far_ref, UNIT),
        (far_ref, 0),
    ]
    first = lax.broadcasted_iota(jnp.int32, (48, LANES), 1) < 64
    rests = []
    for k, (ref, start) in enumerate(sources):
        r_ref[:, 128 * k : 128 * k + 128] = ref[pl.ds(start, 96), :]
        rests.append(ref[pl.ds(start + 96, 48), :])
    for pair in range(4):
        even, odd = rests[2 * pair], rests[2 * pair + 1]
        at = 1024 + 128 * pair
        r_ref[0:48, at : at + 128] = jnp.where(first, even, pltpu.roll(odd, 64, 1))
        r_ref[48:96, at : at + 128] = jnp.where(first, pltpu.roll(even, 64, 1), odd)


def received_column(core, source):
    remote = source - 768
    list_at = jnp.zeros_like(source)
    for k in range(1, 8):
        list_at = list_at + jnp.where(remote >= 192 * k, 1, 0)
    slot = remote - 192 * list_at
    seen = list_at + core * (7 - 2 * list_at)
    rest = 1024 + 64 * seen + slot - 128
    return jnp.where(remote < 0, -1, jnp.where(slot < 128, 128 * seen + slot, rest))


def turned(nodes, code):
    swap = code >= 4
    flip_a = (code & 1) == 1
    flip_b = (code & 2) == 2
    out = [
        [nodes[a][b] if a == b else jnp.where(swap, nodes[b][a], nodes[a][b]) for b in range(4)]
        for a in range(4)
    ]
    out = [[jnp.where(flip_a, out[3 - a][b], out[a][b]) for b in range(4)] for a in range(4)]
    return [[jnp.where(flip_b, out[a][3 - b], out[a][b]) for b in range(4)] for a in range(4)]


def applied(nodes, along_a, along_b):
    def summed(terms):
        return (terms[0] + terms[1]) + (terms[2] + terms[3])

    half = [
        [summed([along_a[a][x] * nodes[x][b] for x in range(4)]) for b in range(4)]
        for a in range(4)
    ]
    return [
        [summed([along_b[b][y] * half[a][y] for y in range(4)]) for b in range(4)]
        for a in range(4)
    ]


def exterior(core, gathered, code_ref, mortar_code_ref, target_ref, g_ref, m_ref):
    _, halves, adjoint = gll_tables()
    for face in range(6):
        a = face // 2
        b, c = (a + 1) % 3, (a + 2) % 3
        s = 1.0 if face % 2 else -1.0
        boundary = (code_ref[face : face + 1, :] >> 3) == 1
        sign = jnp.where(boundary, -1.0, 1.0)

        def field(index):
            return gathered[16 * index : 16 * index + 16, 128 * face : 128 * face + 128]

        g_ref[16 * face : 16 * face + 16, :] = sign * field(b) + s * field(3 + c)
        g_ref[96 + 16 * face : 96 + 16 * face + 16, :] = sign * field(c) - s * field(3 + b)
    code = code_ref[...]
    kind = code >> 3
    quarter = kind - 2
    plain = kind < 2
    live = kind < 6

    def chosen(which, row, column):
        refined = jnp.where(
            which == 1, float(halves[1][row, column]), float(halves[0][row, column])
        )
        kept = jnp.where(plain, 1.0 if row == column else 0.0, refined)
        return jnp.where(live, kept, 0.0)

    along_a = [[chosen(quarter & 1, i, j) for j in range(4)] for i in range(4)]
    along_b = [[chosen(quarter >> 1, i, j) for j in range(4)] for i in range(4)]
    for w in range(2):
        nodes = [
            [g_ref[pl.ds(96 * w + 4 * a + b, 6, stride=16), :] for b in range(4)] for a in range(4)
        ]
        out = applied(turned(nodes, code & 7), along_a, along_b)
        for a in range(4):
            for b in range(4):
                g_ref[pl.ds(96 * w + 4 * a + b, 6, stride=16), :] = out[a][b]

    target = jnp.concatenate([target_ref[...]] * 4, axis=1)
    face = jnp.zeros_like(target)
    for k in range(1, 6):
        face = face + jnp.where(target >= 128 * k, 1, 0)
    axis = face >> 1
    s = jnp.where((face & 1) == 1, 1.0, -1.0)

    def tangential(base, first):
        parts = [gathered[16 * (base + f) : 16 * (base + f) + 16, 768:1024] for f in range(3)]
        x, y, z = (parts[(first + k) % 3] for k in range(3))
        return jnp.where(axis == 0, x, jnp.where(axis == 1, y, z))

    for w, value in enumerate(
        (tangential(0, 1) + s * tangential(3, 2), tangential(0, 2) - s * tangential(3, 1))
    ):
        for half in range(2):
            rows = slice(32 * half + 16 * w, 32 * half + 16 * w + 16)
            m_ref[rows, :] = value[:, 128 * half : 128 * half + 128]
    lane = lax.broadcasted_iota(jnp.int32, (4, LANES), 1)
    row = lax.broadcasted_iota(jnp.int32, (4, LANES), 0)

    def weight(second, i, j):
        return jnp.where(second, float(adjoint[1][i, j]), float(adjoint[0][i, j]))

    project_a = [[weight(lane >= 64, i, j) for j in range(4)] for i in range(4)]
    project_b = [[weight(row >= 2, i, j) for j in range(4)] for i in range(4)]
    nodes = [[m_ref[pl.ds(4 * a + b, 4, stride=16), :] for b in range(4)] for a in range(4)]
    codes = mortar_row(mortar_code_ref)
    codes = jnp.where(row >= 2, codes[:, 128:256], codes[:, 0:128])
    out = applied(turned(nodes, codes), project_a, project_b)
    for a in range(4):
        for b in range(4):
            m_ref[pl.ds(4 * a + b, 4, stride=16), :] = out[a][b]
    pieces = jnp.concatenate([m_ref[0:32, :], m_ref[32:64, :]], axis=1)
    both = jnp.concatenate(halves_of(pieces), axis=0)
    placed = lax.dot_general(
        both, one_hot(768, target), (((1,), (1,)), ((), ())), preferred_element_type=jnp.float32
    )
    placed = placed[0:32] + placed[32:64]
    for w in range(2):
        for at in range(6):
            rows = slice(96 * w + 16 * at, 96 * w + 16 * at + 16)
            g_ref[rows, :] = (
                g_ref[rows, :] + placed[16 * w : 16 * w + 16, 128 * at : 128 * at + 128]
            )


def add_lift(rate_ref, g_ref):
    for face in range(6):
        a = face // 2
        b, c = (a + 1) % 3, (a + 2) % 3
        s = 3.0 if face % 2 else -3.0
        p = g_ref[16 * face : 16 * face + 16, :]
        q = g_ref[96 + 16 * face : 96 + 16 * face + 16, :]
        for f, value in ((b, -3.0 * p), (c, -3.0 * q), (3 + b, s * q), (3 + c, -s * p)):
            base = 64 * f
            if a == 0:
                at = base + (48 if face % 2 else 0)
                rate_ref[at : at + 16, :] = rate_ref[at : at + 16, :] + value
            elif a == 1:
                for i in range(4):
                    at = base + 16 * i + (12 if face % 2 else 0)
                    rate_ref[at : at + 4, :] = rate_ref[at : at + 4, :] + value[4 * i : 4 * i + 4]
            else:
                at = pl.ds(base + (3 if face % 2 else 0), 16, stride=4)
                rate_ref[at, :] = rate_ref[at, :] + value


def section_kernel(section, *refs):
    refs = list(refs)
    core_ref, u_ref = refs[0:2]
    del refs[0:2]
    register_ref = refs.pop(0) if section else None
    (
        rate_in_ref,
        part_ref,
        swapped_ref,
        near_ref,
        far_ref,
        shared_ref,
        material_ref,
        refinement_ref,
        face_ref,
        code_ref,
        mortar_ref,
        mortar_code_ref,
        target_ref,
    ) = refs[0:13]
    del refs[0:13]
    send_ref = None if section else refs.pop(0)
    new_u_ref, new_register_ref = refs[0:2]
    del refs[0:2]
    if section == 0:
        swap_ref, own_ref = refs[0:2]
        del refs[0:2]
    r_ref, g_ref, m_ref, rate_ref, t_ref = refs
    core = core_ref[0]
    write_received(core, swapped_ref, near_ref, far_ref, shared_ref, r_ref)
    at = received_column(core, face_ref[...])
    columns = [at[face : face + 1, :] for face in range(6)]
    columns.append(received_column(core, mortar_row(mortar_ref)))
    spread = jnp.concatenate([one_hot(1536, column) for column in columns], axis=1)
    gathered = part_ref[...] + picked(r_ref[...], spread)
    exterior(core, gathered, code_ref, mortar_code_ref, target_ref, g_ref, m_ref)
    rate_ref[...] = rate_in_ref[...]
    add_lift(rate_ref, g_ref)
    metric = jnp.where(
        refinement_ref[...] == 0, 1.0, jnp.where(refinement_ref[...] == 1, 2.0, 4.0)
    )
    for half in range(2):
        rows = slice(192 * half, 192 * half + 192)
        scale = STEP_SIZE * metric * material_ref[half : half + 1, :]
        register = scale * rate_ref[rows, :]
        if section:
            register = register + SECTION_A[section] * register_ref[rows, :]
        new_register_ref[rows, :] = register
        new_u_ref[rows, :] = u_ref[rows, :] + SECTION_B[section] * register
    if section == 0:
        write_table(new_u_ref, t_ref)
        write_lists(core, t_ref, send_ref, swap_ref, own_ref)


def vmem(count):
    return [pl.BlockSpec(memory_space=pltpu.VMEM)] * count


def floats(rows, columns=LANES):
    return jax.ShapeDtypeStruct((rows, columns), jnp.float32)


def called(kernel, core, operands, outputs, scratch):
    first = [] if core is None else [pl.BlockSpec(memory_space=pltpu.SMEM)]
    given = list(operands) if core is None else [core, *operands]
    return pl.pallas_call(
        kernel,
        in_specs=first + vmem(len(operands)),
        out_specs=vmem(len(outputs)),
        out_shape=outputs,
        scratch_shapes=[pltpu.VMEM(shape, jnp.float32) for shape in scratch],
        compiler_params=pltpu.CompilerParams(vmem_limit_bytes=VMEM_LIMIT),
    )(*given)


LIST_OUTPUTS = [floats(5 * UNIT), floats(3 * UNIT)]


def exchanged(core, swap, own):
    count = lax.axis_size("sfc")
    pairs = [[2 * chip, 2 * chip + 1] for chip in range(count // 2)]

    def ahead(chips):
        ends = [(i, i + 2 * chips if i % 2 == 0 else i - 2 * chips) for i in range(count)]
        return [(source, end) for source, end in ends if 0 <= end < count]

    swapped = lax.all_gather(swap, "sfc", axis_index_groups=pairs, tiled=True)
    theirs = lax.dynamic_slice_in_dim(swapped, (1 - core) * (5 * UNIT), 4 * UNIT)
    u = UNIT
    near = jnp.concatenate([own[0:u], theirs[0:u], own[u : 2 * u], theirs[u : 2 * u]])
    far = jnp.concatenate([own[2 * u : 3 * u], theirs[2 * u : 4 * u]])
    near = lax.ppermute(near, "sfc", ahead(1))
    far = lax.ppermute(far, "sfc", ahead(2))
    shared = jnp.concatenate([near[2 * u : 4 * u], far[2 * u : 3 * u]])
    shared = lax.all_gather(shared, "sfc", axis_index_groups=pairs, tiled=True)
    return swapped, near, far, shared


def local(
    fields,
    material,
    refinement,
    face_source,
    face_code,
    send_face,
    mortar_source,
    mortar_code,
    mortar_target,
):
    core = lax.rem(lax.axis_index("sfc"), 2).astype(jnp.int32)
    core_at = core.reshape(1)
    volume = jnp.asarray(volume_operand())
    solution = fields.reshape(384, LANES)
    refinement = refinement.reshape(1, LANES)
    target = mortar_target.reshape(1, 64)
    table = (96, 768)
    swap, own = called(lists_kernel, core_at, [solution, send_face], LIST_OUTPUTS, [table])
    register = None
    for section in range(2):
        received = exchanged(core, swap, own)
        rate, part = called(
            local_kernel,
            None,
            [solution, volume, face_source, mortar_source],
            [floats(384), floats(96, 1024)],
            [table],
        )
        operands = [solution] + ([register] if section else [])
        operands += [rate, part, *received, material, refinement]
        operands += [face_source, face_code, mortar_source, mortar_code, target]
        outputs = [floats(384), floats(384)]
        if section == 0:
            operands.append(send_face)
            outputs = outputs + LIST_OUTPUTS

        def kernel(*refs, section=section):
            section_kernel(section, *refs)

        results = called(
            kernel,
            core_at,
            operands,
            outputs,
            [(96, 1536), (192, LANES), (64, LANES), (384, LANES), table],
        )
        solution, register = results[0:2]
        if section == 0:
            swap, own = results[2:4]
    return (solution.reshape(6, 64, LANES), register.reshape(6, 64, LANES))


def solution(mesh):
    return jax.shard_map(
        local,
        mesh=mesh,
        in_specs=(
            P(None, None, "sfc"),
            P(None, "sfc"),
            P("sfc"),
            P(None, "sfc"),
            P(None, "sfc"),
            P(None, "sfc"),
            P(None, "sfc"),
            P(None, "sfc"),
            P("sfc"),
        ),
        out_specs=(P(None, None, "sfc"), P(None, None, "sfc")),
        check_vma=False,
    )
```

```python
import math

import jax
import jax.numpy as jnp
import numpy as np
from jax import lax
from jax.experimental import pallas as pl
from jax.experimental.pallas import tpu as pltpu
from jax.sharding import PartitionSpec as P

STEP_SIZE = 0.02
SECTION_A = (0.0, -567301805773.0 / 1357537059087.0)
SECTION_B = (1432997174477.0 / 9575080441755.0, 5161836677717.0 / 13612068292357.0)
UNIT = 144
LANES = 128
VMEM_LIMIT = 24 * 1024 * 1024


def gll_tables():
    points = np.array([-1.0, -1.0 / math.sqrt(5.0), 1.0 / math.sqrt(5.0), 1.0])
    weights = np.array([1.0, 5.0, 5.0, 1.0]) / 6.0

    def lagrange(where_at):
        values = np.ones((where_at.shape[0], 4))
        for column in range(4):
            for another in range(4):
                if another != column:
                    values[:, column] *= (where_at - points[another]) / (
                        points[column] - points[another]
                    )
        return values

    derivative = np.zeros((4, 4))
    for row_at in range(4):
        for column in range(4):
            summed = 0.0
            for another in range(4):
                if another == column:
                    continue
                factor = 1.0 / (points[column] - points[another])
                for further in range(4):
                    if further != column and further != another:
                        factor *= (points[row_at] - points[further]) / (
                            points[column] - points[further]
                        )
                summed += factor
            derivative[row_at, column] = summed
    halves = [lagrange((points - 1.0) / 2.0), lagrange((points + 1.0) / 2.0)]
    adjoint = [0.5 * halfway.T * weights[None, :] / weights[:, None] for halfway in halves]
    return derivative, halves, adjoint


def face_nodes(face):
    grid = np.arange(64).reshape(4, 4, 4)
    at = 3 if face % 2 else 0
    return [grid[at], grid[:, at], grid[:, :, at]][face // 2].reshape(16)


def volume_map():
    derivative, _, _ = gll_tables()
    eye = np.eye(4)
    along = [
        np.kron(np.kron(derivative, eye), eye),
        np.kron(np.kron(eye, derivative), eye),
        np.kron(np.kron(eye, eye), derivative),
    ]
    whole = np.zeros((6, 64, 6, 64))
    for a in range(3):
        b, c = (a + 1) % 3, (a + 2) % 3
        whole[a, :, 3 + c] += along[b]
        whole[a, :, 3 + b] -= along[c]
        whole[3 + a, :, c] -= along[b]
        whole[3 + a, :, b] += along[c]
    for face in range(6):
        a = face // 2
        b, c = (a + 1) % 3, (a + 2) % 3
        s = 1.0 if face % 2 else -1.0
        for n in face_nodes(face):
            whole[b, n, b, n] += 3.0
            whole[b, n, 3 + c, n] += 3.0 * s
            whole[c, n, c, n] += 3.0
            whole[c, n, 3 + b, n] -= 3.0 * s
            whole[3 + b, n, 3 + b, n] += 3.0
            whole[3 + b, n, c, n] -= 3.0 * s
            whole[3 + c, n, 3 + c, n] += 3.0
            whole[3 + c, n, b, n] += 3.0 * s
    return whole.reshape(384, 384)


def volume_operand():
    whole = volume_map().astype(np.float32)
    high = whole.astype(jnp.bfloat16)
    low = (whole - high.astype(np.float32)).astype(jnp.bfloat16)
    return np.concatenate([high, high, low], axis=1)


def halves_of(value):
    high = value.astype(jnp.bfloat16)
    low = (value - high.astype(jnp.float32)).astype(jnp.bfloat16)
    return high, low


def one_hot(rows, columns):
    at = lax.broadcasted_iota(jnp.int32, (rows, columns.shape[1]), 0)
    return jnp.where(at == columns, 1.0, 0.0).astype(jnp.bfloat16)


def picked(table, columns):
    rows = table.shape[0]
    both = jnp.concatenate(halves_of(table), axis=0)
    out = jnp.dot(both, columns, preferred_element_type=jnp.float32)
    return out[:rows] + out[rows:]


def write_table(u_ref, t_ref):
    for f in range(6):
        base = 64 * f
        rows = slice(16 * f, 16 * f + 16)
        t_ref[rows, 0:128] = u_ref[base : base + 16, :]
        t_ref[rows, 128:256] = u_ref[base + 48 : base + 64, :]
        for side, at in ((2, 0), (3, 12)):
            for i in range(4):
                start = base + 16 * i + at
                t_ref[16 * f + 4 * i : 16 * f + 4 * i + 4, 128 * side : 128 * side + 128] = u_ref[
                    start : start + 4, :
                ]
        t_ref[rows, 512:640] = u_ref[pl.ds(base, 16, stride=4), :]
        t_ref[rows, 640:768] = u_ref[pl.ds(base + 3, 16, stride=4), :]


def list_spread(core, send_ref):
    def listed(k, lanes):
        return jnp.where(core == 0, send_ref[k : k + 1, lanes], send_ref[7 - k : 8 - k, lanes])

    columns = [listed(k, slice(0, 128)) for k in range(8)]
    for pair in range(4):
        rests = [listed(2 * pair + k, slice(128, 192)) for k in range(2)]
        columns.append(jnp.concatenate(rests, axis=1))
    return jnp.concatenate([one_hot(768, column) for column in columns], axis=1)


def write_lists(t_ref, spread, swap_ref, own_ref):
    out = picked(t_ref[...], spread)
    first = lax.broadcasted_iota(jnp.int32, (48, LANES), 1) < 64
    places = {4 - d: (swap_ref, d - 1) for d in range(1, 5)}
    places[4] = (swap_ref, 4)
    places.update({3 + d: (own_ref, d - 2) for d in range(2, 5)})
    for k in range(8):
        ref, place = places[k]
        ref[UNIT * place : UNIT * place + 96, :] = out[:, 128 * k : 128 * k + 128]
        at = 1024 + 128 * (k // 2)
        upper, lower = out[0:48, at : at + 128], out[48:96, at : at + 128]
        if k % 2 == 0:
            packed = jnp.where(first, upper, pltpu.roll(lower, 64, 1))
        else:
            packed = jnp.where(first, pltpu.roll(upper, 64, 1), lower)
        ref[UNIT * place + 96 : UNIT * place + UNIT, :] = packed


def lists_kernel(core_ref, u_ref, send_ref, swap_ref, own_ref, t_ref):
    write_table(u_ref, t_ref)
    write_lists(t_ref, list_spread(core_ref[0], send_ref), swap_ref, own_ref)


def mortar_row(ref):
    return jnp.concatenate([ref[q : q + 1, :] for q in range(4)], axis=1)


def local_part(u_ref, volume_ref, face_ref, mortar_ref, rate_ref, part_ref, t_ref):
    high, low = halves_of(u_ref[...])
    rate_ref[...] = jnp.dot(
        volume_ref[...],
        jnp.concatenate([high, low, high], axis=0),
        preferred_element_type=jnp.float32,
    )
    write_table(u_ref, t_ref)
    columns = [face_ref[face : face + 1, :] for face in range(6)] + [mortar_row(mortar_ref)]
    spread = jnp.concatenate([one_hot(768, column) for column in columns], axis=1)
    part_ref[...] = picked(t_ref[...], spread)


def first_kernel(
    core_ref,
    u_ref,
    volume_ref,
    face_ref,
    mortar_ref,
    code_ref,
    mortar_code_ref,
    target_ref,
    material_ref,
    refinement_ref,
    send_ref,
    rate_ref,
    part_ref,
    list_spread_ref,
    spread_ref,
    place_ref,
    codes_ref,
    scale_ref,
    t_ref,
):
    local_part(u_ref, volume_ref, face_ref, mortar_ref, rate_ref, part_ref, t_ref)
    core = core_ref[0]
    list_spread_ref[...] = list_spread(core, send_ref)
    at = received_column(core, face_ref[...])
    columns = [at[face : face + 1, :] for face in range(6)]
    columns.append(received_column(core, mortar_row(mortar_ref)))
    spread_ref[...] = jnp.concatenate([one_hot(1536, column) for column in columns], axis=1)
    target = jnp.concatenate([target_ref[...]] * 4, axis=1)
    place_ref[...] = one_hot(768, target)
    face = jnp.zeros_like(target)
    for k in range(1, 6):
        face = face + jnp.where(target >= 128 * k, 1, 0)
    row = lax.broadcasted_iota(jnp.int32, (4, LANES), 0)
    codes = mortar_row(mortar_code_ref)
    codes_ref[0:6, :] = code_ref[...]
    codes_ref[6:8, :] = jnp.zeros((2, LANES), jnp.int32)
    codes_ref[8:12, :] = jnp.where(row >= 2, codes[:, 128:256], codes[:, 0:128])
    codes_ref[12:16, :] = jnp.where(row >= 2, face[:, 128:256], face[:, 0:128])
    level = refinement_ref[...]
    metric = jnp.where(level == 0, 1.0, jnp.where(level == 1, 2.0, 4.0))
    scale_ref[...] = STEP_SIZE * metric * material_ref[...]


def write_received(core, swapped_ref, near_ref, far_ref, shared_ref, r_ref):
    other = 1 - core
    swapped = pl.multiple_of(other * (5 * UNIT) + 4 * UNIT, 8)
    shared = [pl.multiple_of(other * (3 * UNIT) + UNIT * place, 8) for place in range(3)]
    sources = [
        (shared_ref, shared[2]),
        (shared_ref, shared[0]),
        (shared_ref, shared[1]),
        (swapped_ref, swapped),
        (near_ref, UNIT),
        (near_ref, 0),
        (far_ref, UNIT),
        (far_ref, 0),
    ]
    first = lax.broadcasted_iota(jnp.int32, (48, LANES), 1) < 64
    rests = []
    for k, (ref, start) in enumerate(sources):
        r_ref[:, 128 * k : 128 * k + 128] = ref[pl.ds(start, 96), :]
        rests.append(ref[pl.ds(start + 96, 48), :])
    for pair in range(4):
        even, odd = rests[2 * pair], rests[2 * pair + 1]
        at = 1024 + 128 * pair
        r_ref[0:48, at : at + 128] = jnp.where(first, even, pltpu.roll(odd, 64, 1))
        r_ref[48:96, at : at + 128] = jnp.where(first, pltpu.roll(even, 64, 1), odd)


def received_column(core, source):
    remote = source - 768
    list_at = jnp.zeros_like(source)
    for k in range(1, 8):
        list_at = list_at + jnp.where(remote >= 192 * k, 1, 0)
    slot = remote - 192 * list_at
    seen = list_at + core * (7 - 2 * list_at)
    rest = 1024 + 64 * seen + slot - 128
    return jnp.where(remote < 0, -1, jnp.where(slot < 128, 128 * seen + slot, rest))


def turned(nodes, code):
    swap = code >= 4
    flip_a = (code & 1) == 1
    flip_b = (code & 2) == 2
    out = [
        [nodes[a][b] if a == b else jnp.where(swap, nodes[b][a], nodes[a][b]) for b in range(4)]
        for a in range(4)
    ]
    out = [[jnp.where(flip_a, out[3 - a][b], out[a][b]) for b in range(4)] for a in range(4)]
    return [[jnp.where(flip_b, out[a][3 - b], out[a][b]) for b in range(4)] for a in range(4)]


def applied(nodes, along_a, along_b):
    def summed(terms):
        return (terms[0] + terms[1]) + (terms[2] + terms[3])

    half = [
        [summed([along_a[a][x] * nodes[x][b] for x in range(4)]) for b in range(4)]
        for a in range(4)
    ]
    return [
        [summed([along_b[b][y] * half[a][y] for y in range(4)]) for b in range(4)]
        for a in range(4)
    ]


def exterior(gathered, codes_ref, place_ref, g_ref, m_ref):
    _, halves, adjoint = gll_tables()
    for face in range(6):
        a = face // 2
        b, c = (a + 1) % 3, (a + 2) % 3
        s = 1.0 if face % 2 else -1.0
        boundary = (codes_ref[face : face + 1, :] >> 3) == 1
        sign = jnp.where(boundary, -1.0, 1.0)

        def field(index):
            return gathered[16 * index : 16 * index + 16, 128 * face : 128 * face + 128]

        g_ref[16 * face : 16 * face + 16, :] = sign * field(b) + s * field(3 + c)
        g_ref[96 + 16 * face : 96 + 16 * face + 16, :] = sign * field(c) - s * field(3 + b)
    code = codes_ref[0:6, :]
    kind = code >> 3
    quarter = kind - 2
    plain = kind < 2
    live = kind < 6

    def chosen(which, row, column):
        refined = jnp.where(
            which == 1, float(halves[1][row, column]), float(halves[0][row, column])
        )
        kept = jnp.where(plain, 1.0 if row == column else 0.0, refined)
        return jnp.where(live, kept, 0.0)

    along_a = [[chosen(quarter & 1, i, j) for j in range(4)] for i in range(4)]
    along_b = [[chosen(quarter >> 1, i, j) for j in range(4)] for i in range(4)]
    for w in range(2):
        nodes = [
            [g_ref[pl.ds(96 * w + 4 * a + b, 6, stride=16), :] for b in range(4)] for a in range(4)
        ]
        out = applied(turned(nodes, code & 7), along_a, along_b)
        for a in range(4):
            for b in range(4):
                g_ref[pl.ds(96 * w + 4 * a + b, 6, stride=16), :] = out[a][b]

    for half in range(2):
        face = codes_ref[13 + half : 14 + half, :]
        axis = face >> 1
        s = jnp.where((face & 1) == 1, 1.0, -1.0)
        lanes = slice(768 + 128 * half, 896 + 128 * half)

        def tangential(base, first):
            x, y, z = (
                gathered[16 * f : 16 * f + 16, lanes]
                for f in (base + (first + k) % 3 for k in range(3))
            )
            return jnp.where(axis == 0, x, jnp.where(axis == 1, y, z))

        m_ref[32 * half : 32 * half + 16, :] = tangential(0, 1) + s * tangential(3, 2)
        m_ref[32 * half + 16 : 32 * half + 32, :] = tangential(0, 2) - s * tangential(3, 1)
    lane = lax.broadcasted_iota(jnp.int32, (4, LANES), 1)
    row = lax.broadcasted_iota(jnp.int32, (4, LANES), 0)

    def weight(second, i, j):
        return jnp.where(second, float(adjoint[1][i, j]), float(adjoint[0][i, j]))

    project_a = [[weight(lane >= 64, i, j) for j in range(4)] for i in range(4)]
    project_b = [[weight(row >= 2, i, j) for j in range(4)] for i in range(4)]
    nodes = [[m_ref[pl.ds(4 * a + b, 4, stride=16), :] for b in range(4)] for a in range(4)]
    out = applied(turned(nodes, codes_ref[8:12, :]), project_a, project_b)
    for a in range(4):
        for b in range(4):
            m_ref[pl.ds(4 * a + b, 4, stride=16), :] = out[a][b]
    pieces = jnp.concatenate([m_ref[0:32, :], m_ref[32:64, :]], axis=1)
    both = jnp.concatenate(halves_of(pieces), axis=0)
    placed = lax.dot_general(
        both, place_ref[...], (((1,), (1,)), ((), ())), preferred_element_type=jnp.float32
    )
    placed = placed[0:32] + placed[32:64]
    for w in range(2):
        for at in range(6):
            rows = slice(96 * w + 16 * at, 96 * w + 16 * at + 16)
            g_ref[rows, :] = (
                g_ref[rows, :] + placed[16 * w : 16 * w + 16, 128 * at : 128 * at + 128]
            )


def add_lift(rate_ref, g_ref):
    for face in range(6):
        a = face // 2
        b, c = (a + 1) % 3, (a + 2) % 3
        s = 3.0 if face % 2 else -3.0
        p = g_ref[16 * face : 16 * face + 16, :]
        q = g_ref[96 + 16 * face : 96 + 16 * face + 16, :]
        for f, value in ((b, -3.0 * p), (c, -3.0 * q), (3 + b, s * q), (3 + c, -s * p)):
            base = 64 * f
            if a == 0:
                at = base + (48 if face % 2 else 0)
                rate_ref[at : at + 16, :] = rate_ref[at : at + 16, :] + value
            elif a == 1:
                for i in range(4):
                    at = base + 16 * i + (12 if face % 2 else 0)
                    rate_ref[at : at + 4, :] = rate_ref[at : at + 4, :] + value[4 * i : 4 * i + 4]
            else:
                at = pl.ds(base + (3 if face % 2 else 0), 16, stride=4)
                rate_ref[at, :] = rate_ref[at, :] + value


def section_kernel(section, *refs):
    refs = list(refs)
    core_ref, u_ref = refs[0:2]
    del refs[0:2]
    register_ref = refs.pop(0) if section else None
    rate_in_ref, part_ref, swapped_ref, near_ref, far_ref, shared_ref = refs[0:6]
    spread_ref, place_ref, codes_ref, scale_ref = refs[6:10]
    del refs[0:10]
    list_spread_ref = None if section else refs.pop(0)
    new_u_ref, new_register_ref = refs[0:2]
    del refs[0:2]
    if section == 0:
        swap_ref, own_ref = refs[0:2]
        del refs[0:2]
    r_ref, g_ref, m_ref, rate_ref, t_ref = refs
    core = core_ref[0]
    write_received(core, swapped_ref, near_ref, far_ref, shared_ref, r_ref)
    gathered = part_ref[...] + picked(r_ref[...], spread_ref[...])
    exterior(gathered, codes_ref, place_ref, g_ref, m_ref)
    rate_ref[...] = rate_in_ref[...]
    add_lift(rate_ref, g_ref)
    for half in range(2):
        rows = slice(192 * half, 192 * half + 192)
        register = scale_ref[half : half + 1, :] * rate_ref[rows, :]
        if section:
            register = register + SECTION_A[section] * register_ref[rows, :]
        new_register_ref[rows, :] = register
        new_u_ref[rows, :] = u_ref[rows, :] + SECTION_B[section] * register
    if section == 0:
        write_table(new_u_ref, t_ref)
        write_lists(t_ref, list_spread_ref[...], swap_ref, own_ref)


def shaped(rows, columns=LANES, dtype=jnp.float32):
    return jax.ShapeDtypeStruct((rows, columns), dtype)


def called(kernel, core, operands, outputs, scratch):
    first = [] if core is None else [pl.BlockSpec(memory_space=pltpu.SMEM)]
    given = list(operands) if core is None else [core, *operands]
    return pl.pallas_call(
        kernel,
        in_specs=first + [pl.BlockSpec(memory_space=pltpu.VMEM)] * len(operands),
        out_specs=[pl.BlockSpec(memory_space=pltpu.VMEM)] * len(outputs),
        out_shape=outputs,
        scratch_shapes=[pltpu.VMEM(shape, jnp.float32) for shape in scratch],
        compiler_params=pltpu.CompilerParams(vmem_limit_bytes=VMEM_LIMIT),
    )(*given)


LIST_OUTPUTS = [shaped(5 * UNIT), shaped(3 * UNIT)]


def exchanged(core, swap, own):
    count = lax.axis_size("sfc")
    pairs = [[2 * chip, 2 * chip + 1] for chip in range(count // 2)]

    def ahead(chips):
        ends = [(i, i + 2 * chips if i % 2 == 0 else i - 2 * chips) for i in range(count)]
        return [(source, end) for source, end in ends if 0 <= end < count]

    swapped = lax.all_gather(swap, "sfc", axis_index_groups=pairs, tiled=True)
    theirs = lax.dynamic_slice_in_dim(swapped, (1 - core) * (5 * UNIT), 4 * UNIT)
    u = UNIT
    near = jnp.concatenate([own[0:u], theirs[0:u], own[u : 2 * u], theirs[u : 2 * u]])
    far = jnp.concatenate([own[2 * u : 3 * u], theirs[2 * u : 4 * u]])
    near = lax.ppermute(near, "sfc", ahead(1))
    far = lax.ppermute(far, "sfc", ahead(2))
    shared = jnp.concatenate([near[2 * u : 4 * u], far[2 * u : 3 * u]])
    shared = lax.all_gather(shared, "sfc", axis_index_groups=pairs, tiled=True)
    return swapped, near, far, shared


def local(
    fields,
    material,
    refinement,
    face_source,
    face_code,
    send_face,
    mortar_source,
    mortar_code,
    mortar_target,
):
    core = lax.rem(lax.axis_index("sfc"), 2).astype(jnp.int32)
    core_at = core.reshape(1)
    volume = jnp.asarray(volume_operand())
    solution = fields.reshape(384, LANES)
    refinement = refinement.reshape(1, LANES)
    target = mortar_target.reshape(1, 64)
    table = (96, 768)
    swap, own = called(
        lists_kernel,
        core_at,
        [solution, send_face],
        LIST_OUTPUTS,
        [table],
    )
    register = None
    for section in range(2):
        received = exchanged(core, swap, own)
        if section == 0:
            rate, part, list_spread_made, *made = called(
                first_kernel,
                core_at,
                [
                    solution,
                    volume,
                    face_source,
                    mortar_source,
                    face_code,
                    mortar_code,
                    target,
                    material,
                    refinement,
                    send_face,
                ],
                [
                    shaped(384),
                    shaped(96, 1024),
                    shaped(768, 1536, jnp.bfloat16),
                    shaped(1536, 1024, jnp.bfloat16),
                    shaped(768, 256, jnp.bfloat16),
                    shaped(16, LANES, jnp.int32),
                    shaped(2, LANES),
                ],
                [table],
            )
        else:
            rate, part = called(
                local_part,
                None,
                [solution, volume, face_source, mortar_source],
                [shaped(384), shaped(96, 1024)],
                [table],
            )
        operands = [solution] + ([register] if section else [])
        operands += [rate, part, *received, *made]
        outputs = [shaped(384), shaped(384)]
        if section == 0:
            operands.append(list_spread_made)
            outputs = outputs + LIST_OUTPUTS

        def kernel(*refs, section=section):
            section_kernel(section, *refs)

        results = called(
            kernel,
            core_at,
            operands,
            outputs,
            [(96, 1536), (192, LANES), (64, LANES), (384, LANES), table],
        )
        solution, register = results[0:2]
        if section == 0:
            swap, own = results[2:4]
    return (solution.reshape(6, 64, LANES), register.reshape(6, 64, LANES))


def solution(mesh):
    return jax.shard_map(
        local,
        mesh=mesh,
        in_specs=(
            P(None, None, "sfc"),
            P(None, "sfc"),
            P("sfc"),
            P(None, "sfc"),
            P(None, "sfc"),
            P(None, "sfc"),
            P(None, "sfc"),
            P(None, "sfc"),
            P("sfc"),
        ),
        out_specs=(P(None, None, "sfc"), P(None, None, "sfc")),
        check_vma=False,
    )
```

```python
import math

import jax
import jax.numpy as jnp
import numpy as np
from jax import lax
from jax.experimental import pallas as pl
from jax.experimental.pallas import tpu as pltpu
from jax.sharding import PartitionSpec as P

STEP_SIZE = 0.02
SECTION_A = (0.0, -567301805773.0 / 1357537059087.0)
SECTION_B = (1432997174477.0 / 9575080441755.0, 5161836677717.0 / 13612068292357.0)
UNIT = 144
LANES = 128
VMEM_LIMIT = 24 * 1024 * 1024


def gll_tables():
    points = np.array([-1.0, -1.0 / math.sqrt(5.0), 1.0 / math.sqrt(5.0), 1.0])
    weights = np.array([1.0, 5.0, 5.0, 1.0]) / 6.0

    def lagrange(where_at):
        values = np.ones((where_at.shape[0], 4))
        for column in range(4):
            for another in range(4):
                if another != column:
                    values[:, column] *= (where_at - points[another]) / (
                        points[column] - points[another]
                    )
        return values

    derivative = np.zeros((4, 4))
    for row_at in range(4):
        for column in range(4):
            summed = 0.0
            for another in range(4):
                if another == column:
                    continue
                factor = 1.0 / (points[column] - points[another])
                for further in range(4):
                    if further != column and further != another:
                        factor *= (points[row_at] - points[further]) / (
                            points[column] - points[further]
                        )
                summed += factor
            derivative[row_at, column] = summed
    halves = [lagrange((points - 1.0) / 2.0), lagrange((points + 1.0) / 2.0)]
    adjoint = [0.5 * halfway.T * weights[None, :] / weights[:, None] for halfway in halves]
    return derivative, halves, adjoint


def face_nodes(face):
    grid = np.arange(64).reshape(4, 4, 4)
    at = 3 if face % 2 else 0
    return [grid[at], grid[:, at], grid[:, :, at]][face // 2].reshape(16)


def volume_map():
    derivative, _, _ = gll_tables()
    eye = np.eye(4)
    along = [
        np.kron(np.kron(derivative, eye), eye),
        np.kron(np.kron(eye, derivative), eye),
        np.kron(np.kron(eye, eye), derivative),
    ]
    whole = np.zeros((6, 64, 6, 64))
    for a in range(3):
        b, c = (a + 1) % 3, (a + 2) % 3
        whole[a, :, 3 + c] += along[b]
        whole[a, :, 3 + b] -= along[c]
        whole[3 + a, :, c] -= along[b]
        whole[3 + a, :, b] += along[c]
    for face in range(6):
        a = face // 2
        b, c = (a + 1) % 3, (a + 2) % 3
        s = 1.0 if face % 2 else -1.0
        for n in face_nodes(face):
            whole[b, n, b, n] += 3.0
            whole[b, n, 3 + c, n] += 3.0 * s
            whole[c, n, c, n] += 3.0
            whole[c, n, 3 + b, n] -= 3.0 * s
            whole[3 + b, n, 3 + b, n] += 3.0
            whole[3 + b, n, c, n] -= 3.0 * s
            whole[3 + c, n, 3 + c, n] += 3.0
            whole[3 + c, n, b, n] += 3.0 * s
    return whole.reshape(384, 384)


def volume_operand():
    whole = volume_map().astype(np.float32)
    high = whole.astype(jnp.bfloat16)
    low = (whole - high.astype(np.float32)).astype(jnp.bfloat16)
    return np.concatenate([high, high, low], axis=1)


def halves_of(value):
    high = value.astype(jnp.bfloat16)
    low = (value - high.astype(jnp.float32)).astype(jnp.bfloat16)
    return high, low


def one_hot(rows, columns):
    at = lax.broadcasted_iota(jnp.int32, (rows, columns.shape[1]), 0)
    return jnp.where(at == columns, 1.0, 0.0).astype(jnp.bfloat16)


def picked(table, columns):
    rows = table.shape[0]
    both = jnp.concatenate(halves_of(table), axis=0)
    out = jnp.dot(both, columns, preferred_element_type=jnp.float32)
    return out[:rows] + out[rows:]


def write_table(u_ref, t_ref):
    for f in range(6):
        base = 64 * f
        rows = slice(16 * f, 16 * f + 16)
        t_ref[rows, 0:128] = u_ref[base : base + 16, :]
        t_ref[rows, 128:256] = u_ref[base + 48 : base + 64, :]
        for side, at in ((2, 0), (3, 12)):
            for i in range(4):
                start = base + 16 * i + at
                t_ref[16 * f + 4 * i : 16 * f + 4 * i + 4, 128 * side : 128 * side + 128] = u_ref[
                    start : start + 4, :
                ]
        t_ref[rows, 512:640] = u_ref[pl.ds(base, 16, stride=4), :]
        t_ref[rows, 640:768] = u_ref[pl.ds(base + 3, 16, stride=4), :]


def list_spread(core, send_ref):
    def listed(k, lanes):
        return jnp.where(core == 0, send_ref[k : k + 1, lanes], send_ref[7 - k : 8 - k, lanes])

    columns = [listed(k, slice(0, 128)) for k in range(8)]
    for pair in range(4):
        rests = [listed(2 * pair + k, slice(128, 192)) for k in range(2)]
        columns.append(jnp.concatenate(rests, axis=1))
    return jnp.concatenate([one_hot(768, column) for column in columns], axis=1)


def write_lists(t_ref, spread, swap_ref, *own_refs):
    out = picked(t_ref[...], spread)
    first = lax.broadcasted_iota(jnp.int32, (48, LANES), 1) < 64
    places = {4 - d: (swap_ref, d - 1) for d in range(1, 4)}
    places[4] = (swap_ref, 3)
    places.update({3 + d: (own_refs[d - 2], 0) for d in range(2, 5)})
    places[0] = (own_refs[3], 0)
    for k in range(8):
        ref, place = places[k]
        ref[UNIT * place : UNIT * place + 96, :] = out[:, 128 * k : 128 * k + 128]
        at = 1024 + 128 * (k // 2)
        upper, lower = out[0:48, at : at + 128], out[48:96, at : at + 128]
        if k % 2 == 0:
            packed = jnp.where(first, upper, pltpu.roll(lower, 64, 1))
        else:
            packed = jnp.where(first, pltpu.roll(upper, 64, 1), lower)
        ref[UNIT * place + 96 : UNIT * place + UNIT, :] = packed


def lists_kernel(core_ref, u_ref, send_ref, *refs):
    t_ref = refs[-1]
    write_table(u_ref, t_ref)
    write_lists(t_ref, list_spread(core_ref[0], send_ref), *refs[:-1])


def mortar_row(ref):
    return jnp.concatenate([ref[q : q + 1, :] for q in range(4)], axis=1)


def local_part(u_ref, volume_ref, face_ref, mortar_ref, rate_ref, part_ref, t_ref):
    high, low = halves_of(u_ref[...])
    rate_ref[...] = jnp.dot(
        volume_ref[...],
        jnp.concatenate([high, low, high], axis=0),
        preferred_element_type=jnp.float32,
    )
    write_table(u_ref, t_ref)
    columns = [face_ref[face : face + 1, :] for face in range(6)] + [mortar_row(mortar_ref)]
    spread = jnp.concatenate([one_hot(768, column) for column in columns], axis=1)
    part_ref[...] = picked(t_ref[...], spread)


def first_kernel(
    core_ref,
    u_ref,
    volume_ref,
    face_ref,
    mortar_ref,
    code_ref,
    mortar_code_ref,
    target_ref,
    material_ref,
    refinement_ref,
    send_ref,
    rate_ref,
    part_ref,
    list_spread_ref,
    spread_ref,
    place_ref,
    codes_ref,
    scale_ref,
    t_ref,
):
    local_part(u_ref, volume_ref, face_ref, mortar_ref, rate_ref, part_ref, t_ref)
    core = core_ref[0]
    list_spread_ref[...] = list_spread(core, send_ref)
    at = received_column(core, face_ref[...])
    columns = [at[face : face + 1, :] for face in range(6)]
    columns.append(received_column(core, mortar_row(mortar_ref)))
    spread_ref[...] = jnp.concatenate([one_hot(1536, column) for column in columns], axis=1)
    target = jnp.concatenate([target_ref[...]] * 4, axis=1)
    place_ref[...] = one_hot(768, target)
    face = jnp.zeros_like(target)
    for k in range(1, 6):
        face = face + jnp.where(target >= 128 * k, 1, 0)
    row = lax.broadcasted_iota(jnp.int32, (4, LANES), 0)
    codes = mortar_row(mortar_code_ref)
    codes_ref[0:6, :] = code_ref[...]
    codes_ref[6:8, :] = jnp.zeros((2, LANES), jnp.int32)
    codes_ref[8:12, :] = jnp.where(row >= 2, codes[:, 128:256], codes[:, 0:128])
    codes_ref[12:16, :] = jnp.where(row >= 2, face[:, 128:256], face[:, 0:128])
    level = refinement_ref[...]
    metric = jnp.where(level == 0, 1.0, jnp.where(level == 1, 2.0, 4.0))
    scale_ref[...] = STEP_SIZE * metric * material_ref[...]


def write_received(core, swapped_ref, near_ref, far_ref, across_ref, shared_ref, r_ref):
    other = 1 - core
    swapped = pl.multiple_of(other * (4 * UNIT) + 3 * UNIT, 8)
    shared = [pl.multiple_of(other * (2 * UNIT) + UNIT * place, 8) for place in range(2)]
    sources = [
        (across_ref, 0),
        (shared_ref, shared[0]),
        (shared_ref, shared[1]),
        (swapped_ref, swapped),
        (near_ref, UNIT),
        (near_ref, 0),
        (far_ref, UNIT),
        (far_ref, 0),
    ]
    first = lax.broadcasted_iota(jnp.int32, (48, LANES), 1) < 64
    rests = []
    for k, (ref, start) in enumerate(sources):
        r_ref[:, 128 * k : 128 * k + 128] = ref[pl.ds(start, 96), :]
        rests.append(ref[pl.ds(start + 96, 48), :])
    for pair in range(4):
        even, odd = rests[2 * pair], rests[2 * pair + 1]
        at = 1024 + 128 * pair
        r_ref[0:48, at : at + 128] = jnp.where(first, even, pltpu.roll(odd, 64, 1))
        r_ref[48:96, at : at + 128] = jnp.where(first, pltpu.roll(even, 64, 1), odd)


def received_column(core, source):
    remote = source - 768
    list_at = jnp.zeros_like(source)
    for k in range(1, 8):
        list_at = list_at + jnp.where(remote >= 192 * k, 1, 0)
    slot = remote - 192 * list_at
    seen = list_at + core * (7 - 2 * list_at)
    rest = 1024 + 64 * seen + slot - 128
    return jnp.where(remote < 0, -1, jnp.where(slot < 128, 128 * seen + slot, rest))


def turned(nodes, code):
    swap = code >= 4
    flip_a = (code & 1) == 1
    flip_b = (code & 2) == 2
    out = [
        [nodes[a][b] if a == b else jnp.where(swap, nodes[b][a], nodes[a][b]) for b in range(4)]
        for a in range(4)
    ]
    out = [[jnp.where(flip_a, out[3 - a][b], out[a][b]) for b in range(4)] for a in range(4)]
    return [[jnp.where(flip_b, out[a][3 - b], out[a][b]) for b in range(4)] for a in range(4)]


def applied(nodes, along_a, along_b):
    def summed(terms):
        return (terms[0] + terms[1]) + (terms[2] + terms[3])

    half = [
        [summed([along_a[a][x] * nodes[x][b] for x in range(4)]) for b in range(4)]
        for a in range(4)
    ]
    return [
        [summed([along_b[b][y] * half[a][y] for y in range(4)]) for b in range(4)]
        for a in range(4)
    ]


def exterior(gathered, codes_ref, place_ref, g_ref, m_ref):
    _, halves, adjoint = gll_tables()
    for face in range(6):
        a = face // 2
        b, c = (a + 1) % 3, (a + 2) % 3
        s = 1.0 if face % 2 else -1.0
        boundary = (codes_ref[face : face + 1, :] >> 3) == 1
        sign = jnp.where(boundary, -1.0, 1.0)

        def field(index):
            return gathered[16 * index : 16 * index + 16, 128 * face : 128 * face + 128]

        g_ref[16 * face : 16 * face + 16, :] = sign * field(b) + s * field(3 + c)
        g_ref[96 + 16 * face : 96 + 16 * face + 16, :] = sign * field(c) - s * field(3 + b)
    code = codes_ref[0:6, :]
    kind = code >> 3
    quarter = kind - 2
    plain = kind < 2
    live = kind < 6

    def chosen(which, row, column):
        refined = jnp.where(
            which == 1, float(halves[1][row, column]), float(halves[0][row, column])
        )
        kept = jnp.where(plain, 1.0 if row == column else 0.0, refined)
        return jnp.where(live, kept, 0.0)

    along_a = [[chosen(quarter & 1, i, j) for j in range(4)] for i in range(4)]
    along_b = [[chosen(quarter >> 1, i, j) for j in range(4)] for i in range(4)]
    for w in range(2):
        nodes = [
            [g_ref[pl.ds(96 * w + 4 * a + b, 6, stride=16), :] for b in range(4)] for a in range(4)
        ]
        out = applied(turned(nodes, code & 7), along_a, along_b)
        for a in range(4):
            for b in range(4):
                g_ref[pl.ds(96 * w + 4 * a + b, 6, stride=16), :] = out[a][b]

    for half in range(2):
        face = codes_ref[13 + half : 14 + half, :]
        axis = face >> 1
        s = jnp.where((face & 1) == 1, 1.0, -1.0)
        lanes = slice(768 + 128 * half, 896 + 128 * half)

        def tangential(base, first):
            x, y, z = (
                gathered[16 * f : 16 * f + 16, lanes]
                for f in (base + (first + k) % 3 for k in range(3))
            )
            return jnp.where(axis == 0, x, jnp.where(axis == 1, y, z))

        m_ref[32 * half : 32 * half + 16, :] = tangential(0, 1) + s * tangential(3, 2)
        m_ref[32 * half + 16 : 32 * half + 32, :] = tangential(0, 2) - s * tangential(3, 1)
    lane = lax.broadcasted_iota(jnp.int32, (4, LANES), 1)
    row = lax.broadcasted_iota(jnp.int32, (4, LANES), 0)

    def weight(second, i, j):
        return jnp.where(second, float(adjoint[1][i, j]), float(adjoint[0][i, j]))

    project_a = [[weight(lane >= 64, i, j) for j in range(4)] for i in range(4)]
    project_b = [[weight(row >= 2, i, j) for j in range(4)] for i in range(4)]
    nodes = [[m_ref[pl.ds(4 * a + b, 4, stride=16), :] for b in range(4)] for a in range(4)]
    out = applied(turned(nodes, codes_ref[8:12, :]), project_a, project_b)
    for a in range(4):
        for b in range(4):
            m_ref[pl.ds(4 * a + b, 4, stride=16), :] = out[a][b]
    pieces = jnp.concatenate([m_ref[0:32, :], m_ref[32:64, :]], axis=1)
    both = jnp.concatenate(halves_of(pieces), axis=0)
    placed = lax.dot_general(
        both, place_ref[...], (((1,), (1,)), ((), ())), preferred_element_type=jnp.float32
    )
    placed = placed[0:32] + placed[32:64]
    for w in range(2):
        for at in range(6):
            rows = slice(96 * w + 16 * at, 96 * w + 16 * at + 16)
            g_ref[rows, :] = (
                g_ref[rows, :] + placed[16 * w : 16 * w + 16, 128 * at : 128 * at + 128]
            )


def add_lift(rate_ref, g_ref):
    for face in range(6):
        a = face // 2
        b, c = (a + 1) % 3, (a + 2) % 3
        s = 3.0 if face % 2 else -3.0
        p = g_ref[16 * face : 16 * face + 16, :]
        q = g_ref[96 + 16 * face : 96 + 16 * face + 16, :]
        for f, value in ((b, -3.0 * p), (c, -3.0 * q), (3 + b, s * q), (3 + c, -s * p)):
            base = 64 * f
            if a == 0:
                at = base + (48 if face % 2 else 0)
                rate_ref[at : at + 16, :] = rate_ref[at : at + 16, :] + value
            elif a == 1:
                for i in range(4):
                    at = base + 16 * i + (12 if face % 2 else 0)
                    rate_ref[at : at + 4, :] = rate_ref[at : at + 4, :] + value[4 * i : 4 * i + 4]
            else:
                at = pl.ds(base + (3 if face % 2 else 0), 16, stride=4)
                rate_ref[at, :] = rate_ref[at, :] + value


def section_kernel(section, *refs):
    refs = list(refs)
    core_ref, u_ref = refs[0:2]
    del refs[0:2]
    register_ref = refs.pop(0) if section else None
    rate_in_ref, part_ref = refs[0:2]
    received = refs[2:7]
    spread_ref, place_ref, codes_ref, scale_ref = refs[7:11]
    del refs[0:11]
    list_spread_ref = None if section else refs.pop(0)
    new_u_ref, new_register_ref = refs[0:2]
    del refs[0:2]
    list_refs = [] if section else refs[0:5]
    del refs[0 : len(list_refs)]
    r_ref, g_ref, m_ref, rate_ref, t_ref = refs
    core = core_ref[0]
    write_received(core, *received, r_ref)
    gathered = part_ref[...] + picked(r_ref[...], spread_ref[...])
    exterior(gathered, codes_ref, place_ref, g_ref, m_ref)
    rate_ref[...] = rate_in_ref[...]
    add_lift(rate_ref, g_ref)
    for half in range(2):
        rows = slice(192 * half, 192 * half + 192)
        register = scale_ref[half : half + 1, :] * rate_ref[rows, :]
        if section:
            register = register + SECTION_A[section] * register_ref[rows, :]
        new_register_ref[rows, :] = register
        new_u_ref[rows, :] = u_ref[rows, :] + SECTION_B[section] * register
    if section == 0:
        write_table(new_u_ref, t_ref)
        write_lists(t_ref, list_spread_ref[...], *list_refs)


def shaped(rows, columns=LANES, dtype=jnp.float32):
    return jax.ShapeDtypeStruct((rows, columns), dtype)


def called(kernel, core, operands, outputs, scratch):
    first = [] if core is None else [pl.BlockSpec(memory_space=pltpu.SMEM)]
    given = list(operands) if core is None else [core, *operands]
    return pl.pallas_call(
        kernel,
        in_specs=first + [pl.BlockSpec(memory_space=pltpu.VMEM)] * len(operands),
        out_specs=[pl.BlockSpec(memory_space=pltpu.VMEM)] * len(outputs),
        out_shape=outputs,
        scratch_shapes=[pltpu.VMEM(shape, jnp.float32) for shape in scratch],
        compiler_params=pltpu.CompilerParams(vmem_limit_bytes=VMEM_LIMIT),
    )(*given)


LIST_OUTPUTS = [shaped(4 * UNIT)] + [shaped(UNIT)] * 4


def exchanged(core, swap, own_2, own_3, own_4, far_4):
    count = lax.axis_size("sfc")
    pairs = [[2 * chip, 2 * chip + 1] for chip in range(count // 2)]

    def ahead(chips):
        ends = [(i, i + 2 * chips if i % 2 == 0 else i - 2 * chips) for i in range(count)]
        return [(source, end) for source, end in ends if 0 <= end < count]

    across = lax.ppermute(far_4, "sfc", ahead(-2))
    swapped = lax.all_gather(swap, "sfc", axis_index_groups=pairs, tiled=True)
    theirs = lax.dynamic_slice_in_dim(swapped, (1 - core) * (4 * UNIT), 3 * UNIT)
    u = UNIT
    near = jnp.concatenate([own_2, theirs[0:u], own_3, theirs[u : 2 * u]])
    far = jnp.concatenate([own_4, theirs[2 * u : 3 * u]])
    near = lax.ppermute(near, "sfc", ahead(1))
    far = lax.ppermute(far, "sfc", ahead(2))
    shared = lax.all_gather(near[2 * u : 4 * u], "sfc", axis_index_groups=pairs, tiled=True)
    return swapped, near, far, across, shared


def local(
    fields,
    material,
    refinement,
    face_source,
    face_code,
    send_face,
    mortar_source,
    mortar_code,
    mortar_target,
):
    core = lax.rem(lax.axis_index("sfc"), 2).astype(jnp.int32)
    core_at = core.reshape(1)
    volume = jnp.asarray(volume_operand())
    solution = fields.reshape(384, LANES)
    refinement = refinement.reshape(1, LANES)
    target = mortar_target.reshape(1, 64)
    table = (96, 768)
    lists = called(
        lists_kernel,
        core_at,
        [solution, send_face],
        LIST_OUTPUTS,
        [table],
    )
    register = None
    for section in range(2):
        received = exchanged(core, *lists)
        if section == 0:
            rate, part, list_spread_made, *made = called(
                first_kernel,
                core_at,
                [
                    solution,
                    volume,
                    face_source,
                    mortar_source,
                    face_code,
                    mortar_code,
                    target,
                    material,
                    refinement,
                    send_face,
                ],
                [
                    shaped(384),
                    shaped(96, 1024),
                    shaped(768, 1536, jnp.bfloat16),
                    shaped(1536, 1024, jnp.bfloat16),
                    shaped(768, 256, jnp.bfloat16),
                    shaped(16, LANES, jnp.int32),
                    shaped(2, LANES),
                ],
                [table],
            )
        else:
            rate, part = called(
                local_part,
                None,
                [solution, volume, face_source, mortar_source],
                [shaped(384), shaped(96, 1024)],
                [table],
            )
        operands = [solution] + ([register] if section else [])
        operands += [rate, part, *received, *made]
        outputs = [shaped(384), shaped(384)]
        if section == 0:
            operands.append(list_spread_made)
            outputs = outputs + LIST_OUTPUTS

        def kernel(*refs, section=section):
            section_kernel(section, *refs)

        results = called(
            kernel,
            core_at,
            operands,
            outputs,
            [(96, 1536), (192, LANES), (64, LANES), (384, LANES), table],
        )
        solution, register = results[0:2]
        if section == 0:
            lists = results[2:7]
    return (solution.reshape(6, 64, LANES), register.reshape(6, 64, LANES))


def solution(mesh):
    return jax.shard_map(
        local,
        mesh=mesh,
        in_specs=(
            P(None, None, "sfc"),
            P(None, "sfc"),
            P("sfc"),
            P(None, "sfc"),
            P(None, "sfc"),
            P(None, "sfc"),
            P(None, "sfc"),
            P(None, "sfc"),
            P("sfc"),
        ),
        out_specs=(P(None, None, "sfc"), P(None, None, "sfc")),
        check_vma=False,
    )
```

```python
import math

import jax
import jax.numpy as jnp
import numpy as np
from jax import lax
from jax.experimental import pallas as pl
from jax.experimental.pallas import tpu as pltpu
from jax.sharding import PartitionSpec as P

STEP_SIZE = 0.02
SECTION_A = (0.0, -567301805773.0 / 1357537059087.0)
SECTION_B = (1432997174477.0 / 9575080441755.0, 5161836677717.0 / 13612068292357.0)
UNIT = 144
LANES = 128
VMEM_LIMIT = 24 * 1024 * 1024


def gll_tables():
    points = np.array([-1.0, -1.0 / math.sqrt(5.0), 1.0 / math.sqrt(5.0), 1.0])
    weights = np.array([1.0, 5.0, 5.0, 1.0]) / 6.0

    def lagrange(where_at):
        values = np.ones((where_at.shape[0], 4))
        for column in range(4):
            for another in range(4):
                if another != column:
                    values[:, column] *= (where_at - points[another]) / (
                        points[column] - points[another]
                    )
        return values

    derivative = np.zeros((4, 4))
    for row_at in range(4):
        for column in range(4):
            summed = 0.0
            for another in range(4):
                if another == column:
                    continue
                factor = 1.0 / (points[column] - points[another])
                for further in range(4):
                    if further != column and further != another:
                        factor *= (points[row_at] - points[further]) / (
                            points[column] - points[further]
                        )
                summed += factor
            derivative[row_at, column] = summed
    halves = [lagrange((points - 1.0) / 2.0), lagrange((points + 1.0) / 2.0)]
    adjoint = [0.5 * halfway.T * weights[None, :] / weights[:, None] for halfway in halves]
    return derivative, halves, adjoint


def face_nodes(face):
    grid = np.arange(64).reshape(4, 4, 4)
    at = 3 if face % 2 else 0
    return [grid[at], grid[:, at], grid[:, :, at]][face // 2].reshape(16)


def volume_map():
    derivative, _, _ = gll_tables()
    eye = np.eye(4)
    along = [
        np.kron(np.kron(derivative, eye), eye),
        np.kron(np.kron(eye, derivative), eye),
        np.kron(np.kron(eye, eye), derivative),
    ]
    whole = np.zeros((6, 64, 6, 64))
    for a in range(3):
        b, c = (a + 1) % 3, (a + 2) % 3
        whole[a, :, 3 + c] += along[b]
        whole[a, :, 3 + b] -= along[c]
        whole[3 + a, :, c] -= along[b]
        whole[3 + a, :, b] += along[c]
    for face in range(6):
        a = face // 2
        b, c = (a + 1) % 3, (a + 2) % 3
        s = 1.0 if face % 2 else -1.0
        for n in face_nodes(face):
            whole[b, n, b, n] += 3.0
            whole[b, n, 3 + c, n] += 3.0 * s
            whole[c, n, c, n] += 3.0
            whole[c, n, 3 + b, n] -= 3.0 * s
            whole[3 + b, n, 3 + b, n] += 3.0
            whole[3 + b, n, c, n] -= 3.0 * s
            whole[3 + c, n, 3 + c, n] += 3.0
            whole[3 + c, n, b, n] += 3.0 * s
    return whole.reshape(384, 384)


def volume_operand():
    whole = volume_map().astype(np.float32)
    high = whole.astype(jnp.bfloat16)
    low = (whole - high.astype(np.float32)).astype(jnp.bfloat16)
    return np.concatenate([high, high, low], axis=1)


def halves_of(value):
    high = value.astype(jnp.bfloat16)
    low = (value - high.astype(jnp.float32)).astype(jnp.bfloat16)
    return high, low


def one_hot(rows, columns):
    at = lax.broadcasted_iota(jnp.int32, (rows, columns.shape[1]), 0)
    return jnp.where(at == columns, 1.0, 0.0).astype(jnp.bfloat16)


def picked(table, columns):
    rows = table.shape[0]
    both = jnp.concatenate(halves_of(table), axis=0)
    out = jnp.dot(both, columns, preferred_element_type=jnp.float32)
    return out[:rows] + out[rows:]


def write_table(u_ref, t_ref):
    for f in range(6):
        base = 64 * f
        rows = slice(16 * f, 16 * f + 16)
        t_ref[rows, 0:128] = u_ref[base : base + 16, :]
        t_ref[rows, 128:256] = u_ref[base + 48 : base + 64, :]
        for side, at in ((2, 0), (3, 12)):
            for i in range(4):
                start = base + 16 * i + at
                t_ref[16 * f + 4 * i : 16 * f + 4 * i + 4, 128 * side : 128 * side + 128] = u_ref[
                    start : start + 4, :
                ]
        t_ref[rows, 512:640] = u_ref[pl.ds(base, 16, stride=4), :]
        t_ref[rows, 640:768] = u_ref[pl.ds(base + 3, 16, stride=4), :]


def list_spread(core, send_ref):
    def listed(k, lanes):
        return jnp.where(core == 0, send_ref[k : k + 1, lanes], send_ref[7 - k : 8 - k, lanes])

    columns = [listed(k, slice(0, 128)) for k in range(8)]
    for pair in range(4):
        rests = [listed(2 * pair + k, slice(128, 192)) for k in range(2)]
        columns.append(jnp.concatenate(rests, axis=1))
    return jnp.concatenate([one_hot(768, column) for column in columns], axis=1)


def write_lists(t_ref, spread, swap_ref, *own_refs):
    out = picked(t_ref[...], spread)
    first = lax.broadcasted_iota(jnp.int32, (48, LANES), 1) < 64
    places = {4 - d: (swap_ref, d - 1) for d in range(1, 4)}
    places[4] = (swap_ref, 3)
    places.update({3 + d: (own_refs[d - 2], 0) for d in range(2, 5)})
    places[0] = (own_refs[3], 0)
    for k in range(8):
        ref, place = places[k]
        ref[UNIT * place : UNIT * place + 96, :] = out[:, 128 * k : 128 * k + 128]
        at = 1024 + 128 * (k // 2)
        upper, lower = out[0:48, at : at + 128], out[48:96, at : at + 128]
        if k % 2 == 0:
            packed = jnp.where(first, upper, pltpu.roll(lower, 64, 1))
        else:
            packed = jnp.where(first, pltpu.roll(upper, 64, 1), lower)
        ref[UNIT * place + 96 : UNIT * place + UNIT, :] = packed


def lists_kernel(core_ref, u_ref, send_ref, *refs):
    u_out_ref, send_out_ref, t_ref = refs[5:8]
    write_table(u_ref, t_ref)
    write_lists(t_ref, list_spread(core_ref[0], send_ref), *refs[0:5])
    u_out_ref[...] = u_ref[...]
    send_out_ref[...] = send_ref[...]


def mortar_row(index_ref, base):
    return jnp.concatenate([index_ref[base + q : base + q + 1, 0:64] for q in range(4)], axis=1)


def source_columns(index_ref):
    return [index_ref[face : face + 1, :] for face in range(6)] + [mortar_row(index_ref, 12)]


def local_kernel(u_ref, volume_ref, index_ref, rate_ref, part_ref, t_ref):
    high, low = halves_of(u_ref[...])
    rate_ref[...] = jnp.dot(
        volume_ref[...],
        jnp.concatenate([high, low, high], axis=0),
        preferred_element_type=jnp.float32,
    )
    write_table(u_ref, t_ref)
    spread = [one_hot(768, column) for column in source_columns(index_ref)]
    spread = jnp.concatenate(spread, axis=1)
    part_ref[...] = picked(t_ref[...], spread)


def write_received(core, swapped_ref, near_ref, far_ref, across_ref, shared_ref, r_ref):
    other = 1 - core
    swapped = pl.multiple_of(other * (4 * UNIT) + 3 * UNIT, 8)
    shared = [pl.multiple_of(other * (2 * UNIT) + UNIT * place, 8) for place in range(2)]
    sources = [
        (across_ref, 0),
        (shared_ref, shared[0]),
        (shared_ref, shared[1]),
        (swapped_ref, swapped),
        (near_ref, UNIT),
        (near_ref, 0),
        (far_ref, UNIT),
        (far_ref, 0),
    ]
    first = lax.broadcasted_iota(jnp.int32, (48, LANES), 1) < 64
    rests = []
    for k, (ref, start) in enumerate(sources):
        r_ref[:, 128 * k : 128 * k + 128] = ref[pl.ds(start, 96), :]
        rests.append(ref[pl.ds(start + 96, 48), :])
    for pair in range(4):
        even, odd = rests[2 * pair], rests[2 * pair + 1]
        at = 1024 + 128 * pair
        r_ref[0:48, at : at + 128] = jnp.where(first, even, pltpu.roll(odd, 64, 1))
        r_ref[48:96, at : at + 128] = jnp.where(first, pltpu.roll(even, 64, 1), odd)


def received_column(core, source):
    remote = source - 768
    list_at = jnp.zeros_like(source)
    for k in range(1, 8):
        list_at = list_at + jnp.where(remote >= 192 * k, 1, 0)
    slot = remote - 192 * list_at
    seen = list_at + core * (7 - 2 * list_at)
    rest = 1024 + 64 * seen + slot - 128
    return jnp.where(remote < 0, -1, jnp.where(slot < 128, 128 * seen + slot, rest))


def turned(nodes, code):
    swap = code >= 4
    flip_a = (code & 1) == 1
    flip_b = (code & 2) == 2
    out = [
        [nodes[a][b] if a == b else jnp.where(swap, nodes[b][a], nodes[a][b]) for b in range(4)]
        for a in range(4)
    ]
    out = [[jnp.where(flip_a, out[3 - a][b], out[a][b]) for b in range(4)] for a in range(4)]
    return [[jnp.where(flip_b, out[a][3 - b], out[a][b]) for b in range(4)] for a in range(4)]


def applied(nodes, along_a, along_b):
    def summed(terms):
        return (terms[0] + terms[1]) + (terms[2] + terms[3])

    half = [
        [summed([along_a[a][x] * nodes[x][b] for x in range(4)]) for b in range(4)]
        for a in range(4)
    ]
    return [
        [summed([along_b[b][y] * half[a][y] for y in range(4)]) for b in range(4)]
        for a in range(4)
    ]


def exterior(gathered, index_ref, g_ref, m_ref):
    _, halves, adjoint = gll_tables()
    for face in range(6):
        a = face // 2
        b, c = (a + 1) % 3, (a + 2) % 3
        s = 1.0 if face % 2 else -1.0
        boundary = (index_ref[6 + face : 7 + face, :] >> 3) == 1
        sign = jnp.where(boundary, -1.0, 1.0)

        def field(index):
            return gathered[16 * index : 16 * index + 16, 128 * face : 128 * face + 128]

        g_ref[16 * face : 16 * face + 16, :] = sign * field(b) + s * field(3 + c)
        g_ref[96 + 16 * face : 96 + 16 * face + 16, :] = sign * field(c) - s * field(3 + b)
    code = index_ref[6:12, :]
    kind = code >> 3
    quarter = kind - 2
    plain = kind < 2
    live = kind < 6

    def chosen(which, row, column):
        refined = jnp.where(
            which == 1, float(halves[1][row, column]), float(halves[0][row, column])
        )
        kept = jnp.where(plain, 1.0 if row == column else 0.0, refined)
        return jnp.where(live, kept, 0.0)

    along_a = [[chosen(quarter & 1, i, j) for j in range(4)] for i in range(4)]
    along_b = [[chosen(quarter >> 1, i, j) for j in range(4)] for i in range(4)]
    for w in range(2):
        nodes = [
            [g_ref[pl.ds(96 * w + 4 * a + b, 6, stride=16), :] for b in range(4)] for a in range(4)
        ]
        out = applied(turned(nodes, code & 7), along_a, along_b)
        for a in range(4):
            for b in range(4):
                g_ref[pl.ds(96 * w + 4 * a + b, 6, stride=16), :] = out[a][b]

    target = jnp.concatenate([index_ref[20:21, 0:64]] * 4, axis=1)
    face = jnp.zeros_like(target[:, 0:128])
    for k in range(1, 6):
        face = face + jnp.where(target[:, 0:128] >= 128 * k, 1, 0)
    for half in range(2):
        axis = face >> 1
        s = jnp.where((face & 1) == 1, 1.0, -1.0)
        lanes = slice(768 + 128 * half, 896 + 128 * half)

        def tangential(base, first):
            x, y, z = (
                gathered[16 * f : 16 * f + 16, lanes]
                for f in (base + (first + k) % 3 for k in range(3))
            )
            return jnp.where(axis == 0, x, jnp.where(axis == 1, y, z))

        m_ref[32 * half : 32 * half + 16, :] = tangential(0, 1) + s * tangential(3, 2)
        m_ref[32 * half + 16 : 32 * half + 32, :] = tangential(0, 2) - s * tangential(3, 1)
    lane = lax.broadcasted_iota(jnp.int32, (4, LANES), 1)
    row = lax.broadcasted_iota(jnp.int32, (4, LANES), 0)

    def weight(second, i, j):
        return jnp.where(second, float(adjoint[1][i, j]), float(adjoint[0][i, j]))

    project_a = [[weight(lane >= 64, i, j) for j in range(4)] for i in range(4)]
    project_b = [[weight(row >= 2, i, j) for j in range(4)] for i in range(4)]
    nodes = [[m_ref[pl.ds(4 * a + b, 4, stride=16), :] for b in range(4)] for a in range(4)]
    codes = mortar_row(index_ref, 16)
    codes = jnp.where(row >= 2, codes[:, 128:256], codes[:, 0:128])
    out = applied(turned(nodes, codes), project_a, project_b)
    for a in range(4):
        for b in range(4):
            m_ref[pl.ds(4 * a + b, 4, stride=16), :] = out[a][b]
    pieces = jnp.concatenate([m_ref[0:32, :], m_ref[32:64, :]], axis=1)
    both = jnp.concatenate(halves_of(pieces), axis=0)
    placed = lax.dot_general(
        both, one_hot(768, target), (((1,), (1,)), ((), ())), preferred_element_type=jnp.float32
    )
    placed = placed[0:32] + placed[32:64]
    for w in range(2):
        for at in range(6):
            rows = slice(96 * w + 16 * at, 96 * w + 16 * at + 16)
            g_ref[rows, :] = (
                g_ref[rows, :] + placed[16 * w : 16 * w + 16, 128 * at : 128 * at + 128]
            )


def add_lift(rate_ref, g_ref):
    for face in range(6):
        a = face // 2
        b, c = (a + 1) % 3, (a + 2) % 3
        s = 3.0 if face % 2 else -3.0
        p = g_ref[16 * face : 16 * face + 16, :]
        q = g_ref[96 + 16 * face : 96 + 16 * face + 16, :]
        for f, value in ((b, -3.0 * p), (c, -3.0 * q), (3 + b, s * q), (3 + c, -s * p)):
            base = 64 * f
            if a == 0:
                at = base + (48 if face % 2 else 0)
                rate_ref[at : at + 16, :] = rate_ref[at : at + 16, :] + value
            elif a == 1:
                for i in range(4):
                    at = base + 16 * i + (12 if face % 2 else 0)
                    rate_ref[at : at + 4, :] = rate_ref[at : at + 4, :] + value[4 * i : 4 * i + 4]
            else:
                at = pl.ds(base + (3 if face % 2 else 0), 16, stride=4)
                rate_ref[at, :] = rate_ref[at, :] + value


def section_kernel(section, *refs):
    refs = list(refs)
    core_ref, u_ref = refs[0:2]
    del refs[0:2]
    register_ref = refs.pop(0) if section else None
    rate_in_ref, part_ref = refs[0:2]
    received = refs[2:7]
    index_ref, scale_ref = refs[7:9]
    del refs[0:9]
    send_ref = None if section else refs.pop(0)
    new_u_ref, new_register_ref = refs[0:2]
    del refs[0:2]
    list_refs = [] if section else refs[0:5]
    del refs[0 : len(list_refs)]
    r_ref, g_ref, m_ref, rate_ref, t_ref = refs
    core = core_ref[0]
    write_received(core, *received, r_ref)
    columns = [received_column(core, column) for column in source_columns(index_ref)]
    spread = jnp.concatenate([one_hot(1536, column) for column in columns], axis=1)
    gathered = part_ref[...] + picked(r_ref[...], spread)
    exterior(gathered, index_ref, g_ref, m_ref)
    rate_ref[...] = rate_in_ref[...]
    add_lift(rate_ref, g_ref)
    for half in range(2):
        rows = slice(192 * half, 192 * half + 192)
        register = scale_ref[half : half + 1, :] * rate_ref[rows, :]
        if section:
            register = register + SECTION_A[section] * register_ref[rows, :]
        new_register_ref[rows, :] = register
        new_u_ref[rows, :] = u_ref[rows, :] + SECTION_B[section] * register
    if section == 0:
        write_table(new_u_ref, t_ref)
        write_lists(t_ref, list_spread(core, send_ref), *list_refs)


def shaped(rows, columns=LANES, dtype=jnp.float32):
    return jax.ShapeDtypeStruct((rows, columns), dtype)


def called(kernel, core, operands, outputs, scratch):
    first = [] if core is None else [pl.BlockSpec(memory_space=pltpu.SMEM)]
    given = list(operands) if core is None else [core, *operands]
    return pl.pallas_call(
        kernel,
        in_specs=first + [pl.BlockSpec(memory_space=pltpu.VMEM)] * len(operands),
        out_specs=[pl.BlockSpec(memory_space=pltpu.VMEM)] * len(outputs),
        out_shape=outputs,
        scratch_shapes=[pltpu.VMEM(shape, jnp.float32) for shape in scratch],
        compiler_params=pltpu.CompilerParams(vmem_limit_bytes=VMEM_LIMIT),
    )(*given)


LIST_OUTPUTS = [shaped(4 * UNIT)] + [shaped(UNIT)] * 4


def exchanged(core, swap, own_2, own_3, own_4, far_4):
    count = lax.axis_size("sfc")
    pairs = [[2 * chip, 2 * chip + 1] for chip in range(count // 2)]

    def ahead(chips):
        ends = [(i, i + 2 * chips if i % 2 == 0 else i - 2 * chips) for i in range(count)]
        return [(source, end) for source, end in ends if 0 <= end < count]

    across = lax.ppermute(far_4, "sfc", ahead(-2))
    swapped = lax.all_gather(swap, "sfc", axis_index_groups=pairs, tiled=True)
    theirs = lax.dynamic_slice_in_dim(swapped, (1 - core) * (4 * UNIT), 3 * UNIT)
    u = UNIT
    near = jnp.concatenate([own_2, theirs[0:u], own_3, theirs[u : 2 * u]])
    far = jnp.concatenate([own_4, theirs[2 * u : 3 * u]])
    near = lax.ppermute(near, "sfc", ahead(1))
    far = lax.ppermute(far, "sfc", ahead(2))
    shared = lax.all_gather(near[2 * u : 4 * u], "sfc", axis_index_groups=pairs, tiled=True)
    return swapped, near, far, across, shared


def packed(
    face_source, face_code, mortar_source, mortar_code, mortar_target, refinement, material
):
    def wide(rows):
        return jnp.pad(rows, ((0, 0), (0, LANES - rows.shape[1])))

    index = jnp.concatenate(
        [
            face_source,
            face_code,
            wide(mortar_source),
            wide(mortar_code),
            wide(mortar_target[None]),
        ]
    )
    metric = jnp.left_shift(jnp.ones_like(refinement), refinement).astype(jnp.float32)
    return index, STEP_SIZE * metric * material


def local(
    fields,
    material,
    refinement,
    face_source,
    face_code,
    send_face,
    mortar_source,
    mortar_code,
    mortar_target,
):
    core = lax.rem(lax.axis_index("sfc"), 2).astype(jnp.int32)
    core_at = core.reshape(1)
    volume = jnp.asarray(volume_operand())
    solution = fields.reshape(384, LANES)
    table = (96, 768)
    *lists, solution, send_face = called(
        lists_kernel,
        core_at,
        [solution, send_face],
        LIST_OUTPUTS + [shaped(384), shaped(8, 192, jnp.int32)],
        [table],
    )
    register = None
    index = scale = None
    for section in range(2):
        received = exchanged(core, *lists)
        if section == 0:
            arrays = (face_source, face_code, mortar_source, mortar_code)
            arrays = (*arrays, mortar_target, refinement, material)
            arrays, swapped = lax.optimization_barrier((arrays, received[0]))
            received = (swapped, *received[1:])
            index, scale = packed(*arrays)
        rate, part = called(
            local_kernel,
            None,
            [solution, volume, index],
            [shaped(384), shaped(96, 1024)],
            [table],
        )
        operands = [solution] + ([register] if section else [])
        operands += [rate, part, *received, index, scale]
        outputs = [shaped(384), shaped(384)]
        if section == 0:
            operands.append(send_face)
            outputs = outputs + LIST_OUTPUTS

        def kernel(*refs, section=section):
            section_kernel(section, *refs)

        results = called(
            kernel,
            core_at,
            operands,
            outputs,
            [(96, 1536), (192, LANES), (64, LANES), (384, LANES), table],
        )
        solution, register = results[0:2]
        if section == 0:
            lists = results[2:7]
    return (solution.reshape(6, 64, LANES), register.reshape(6, 64, LANES))


def solution(mesh):
    return jax.shard_map(
        local,
        mesh=mesh,
        in_specs=(
            P(None, None, "sfc"),
            P(None, "sfc"),
            P("sfc"),
            P(None, "sfc"),
            P(None, "sfc"),
            P(None, "sfc"),
            P(None, "sfc"),
            P(None, "sfc"),
            P("sfc"),
        ),
        out_specs=(P(None, None, "sfc"), P(None, None, "sfc")),
        check_vma=False,
    )
```

```python
import math

import jax
import jax.numpy as jnp
import numpy as np
from jax import lax
from jax.experimental import pallas as pl
from jax.experimental.pallas import tpu as pltpu
from jax.sharding import PartitionSpec as P

STEP_SIZE = 0.02
SECTION_A = (0.0, -567301805773.0 / 1357537059087.0)
SECTION_B = (1432997174477.0 / 9575080441755.0, 5161836677717.0 / 13612068292357.0)
UNIT = 144
LANES = 128
VMEM_LIMIT = 24 * 1024 * 1024


def gll_tables():
    points = np.array([-1.0, -1.0 / math.sqrt(5.0), 1.0 / math.sqrt(5.0), 1.0])
    weights = np.array([1.0, 5.0, 5.0, 1.0]) / 6.0

    def lagrange(where_at):
        values = np.ones((where_at.shape[0], 4))
        for column in range(4):
            for another in range(4):
                if another != column:
                    values[:, column] *= (where_at - points[another]) / (
                        points[column] - points[another]
                    )
        return values

    derivative = np.zeros((4, 4))
    for row_at in range(4):
        for column in range(4):
            summed = 0.0
            for another in range(4):
                if another == column:
                    continue
                factor = 1.0 / (points[column] - points[another])
                for further in range(4):
                    if further != column and further != another:
                        factor *= (points[row_at] - points[further]) / (
                            points[column] - points[further]
                        )
                summed += factor
            derivative[row_at, column] = summed
    halves = [lagrange((points - 1.0) / 2.0), lagrange((points + 1.0) / 2.0)]
    adjoint = [0.5 * halfway.T * weights[None, :] / weights[:, None] for halfway in halves]
    return derivative, halves, adjoint


def face_nodes(face):
    grid = np.arange(64).reshape(4, 4, 4)
    at = 3 if face % 2 else 0
    return [grid[at], grid[:, at], grid[:, :, at]][face // 2].reshape(16)


def volume_map():
    derivative, _, _ = gll_tables()
    eye = np.eye(4)
    along = [
        np.kron(np.kron(derivative, eye), eye),
        np.kron(np.kron(eye, derivative), eye),
        np.kron(np.kron(eye, eye), derivative),
    ]
    whole = np.zeros((6, 64, 6, 64))
    for a in range(3):
        b, c = (a + 1) % 3, (a + 2) % 3
        whole[a, :, 3 + c] += along[b]
        whole[a, :, 3 + b] -= along[c]
        whole[3 + a, :, c] -= along[b]
        whole[3 + a, :, b] += along[c]
    for face in range(6):
        a = face // 2
        b, c = (a + 1) % 3, (a + 2) % 3
        s = 1.0 if face % 2 else -1.0
        for n in face_nodes(face):
            whole[b, n, b, n] += 3.0
            whole[b, n, 3 + c, n] += 3.0 * s
            whole[c, n, c, n] += 3.0
            whole[c, n, 3 + b, n] -= 3.0 * s
            whole[3 + b, n, 3 + b, n] += 3.0
            whole[3 + b, n, c, n] -= 3.0 * s
            whole[3 + c, n, 3 + c, n] += 3.0
            whole[3 + c, n, b, n] += 3.0 * s
    return whole.reshape(384, 384)


def volume_operand():
    whole = volume_map().astype(np.float32)
    high = whole.astype(jnp.bfloat16)
    low = (whole - high.astype(np.float32)).astype(jnp.bfloat16)
    return np.concatenate([high, high, low], axis=1)


def halves_of(value):
    high = value.astype(jnp.bfloat16)
    low = (value - high.astype(jnp.float32)).astype(jnp.bfloat16)
    return high, low


def one_hot(rows, columns):
    at = lax.broadcasted_iota(jnp.int32, (rows, columns.shape[1]), 0)
    return jnp.where(at == columns, 1.0, 0.0).astype(jnp.bfloat16)


def picked(table, columns):
    rows = table.shape[0]
    both = jnp.concatenate(halves_of(table), axis=0)
    out = jnp.dot(both, columns, preferred_element_type=jnp.float32)
    return out[:rows] + out[rows:]


def write_table(u_ref, t_ref):
    for f in range(6):
        base = 64 * f
        rows = slice(16 * f, 16 * f + 16)
        t_ref[rows, 0:128] = u_ref[base : base + 16, :]
        t_ref[rows, 128:256] = u_ref[base + 48 : base + 64, :]
        for side, at in ((2, 0), (3, 12)):
            for i in range(4):
                start = base + 16 * i + at
                t_ref[16 * f + 4 * i : 16 * f + 4 * i + 4, 128 * side : 128 * side + 128] = u_ref[
                    start : start + 4, :
                ]
        t_ref[rows, 512:640] = u_ref[pl.ds(base, 16, stride=4), :]
        t_ref[rows, 640:768] = u_ref[pl.ds(base + 3, 16, stride=4), :]


def list_spread(core, send_ref):
    def listed(k, lanes):
        return jnp.where(core == 0, send_ref[k : k + 1, lanes], send_ref[7 - k : 8 - k, lanes])

    columns = [listed(k, slice(0, 128)) for k in range(8)]
    for pair in range(4):
        rests = [listed(2 * pair + k, slice(128, 192)) for k in range(2)]
        columns.append(jnp.concatenate(rests, axis=1))
    return jnp.concatenate([one_hot(768, column) for column in columns], axis=1)


def write_lists(t_ref, spread, swap_ref, own_ref):
    out = picked(t_ref[...], spread)
    first = lax.broadcasted_iota(jnp.int32, (48, LANES), 1) < 64
    places = {4 - d: (swap_ref, d - 1) for d in range(1, 5)}
    places[4] = (swap_ref, 4)
    places.update({3 + d: (own_ref, d - 2) for d in range(2, 5)})
    for k in range(8):
        ref, place = places[k]
        ref[UNIT * place : UNIT * place + 96, :] = out[:, 128 * k : 128 * k + 128]
        at = 1024 + 128 * (k // 2)
        upper, lower = out[0:48, at : at + 128], out[48:96, at : at + 128]
        if k % 2 == 0:
            packed = jnp.where(first, upper, pltpu.roll(lower, 64, 1))
        else:
            packed = jnp.where(first, pltpu.roll(upper, 64, 1), lower)
        ref[UNIT * place + 96 : UNIT * place + UNIT, :] = packed


def lists_kernel(
    core_ref, u_hbm, send_hbm, swap_ref, own_ref, t_ref, u_ref, send_ref, send_sem, u_sem
):
    send_copy = pltpu.make_async_copy(send_hbm, send_ref, send_sem)
    u_copy = pltpu.make_async_copy(u_hbm, u_ref, u_sem)
    send_copy.start()
    u_copy.start()
    send_copy.wait()
    spread = list_spread(core_ref[0], send_ref)
    u_copy.wait()
    write_table(u_ref, t_ref)
    write_lists(t_ref, spread, swap_ref, own_ref)


def mortar_row(ref):
    return jnp.concatenate([ref[q : q + 1, :] for q in range(4)], axis=1)


def local_part(u_ref, volume_ref, face_ref, mortar_ref, rate_ref, part_ref, t_ref):
    high, low = halves_of(u_ref[...])
    rate_ref[...] = jnp.dot(
        volume_ref[...],
        jnp.concatenate([high, low, high], axis=0),
        preferred_element_type=jnp.float32,
    )
    write_table(u_ref, t_ref)
    columns = [face_ref[face : face + 1, :] for face in range(6)] + [mortar_row(mortar_ref)]
    spread = jnp.concatenate([one_hot(768, column) for column in columns], axis=1)
    part_ref[...] = picked(t_ref[...], spread)


def first_kernel(
    core_ref,
    u_ref,
    volume_ref,
    face_ref,
    mortar_ref,
    code_ref,
    mortar_code_ref,
    target_ref,
    material_ref,
    refinement_ref,
    send_ref,
    rate_ref,
    part_ref,
    list_spread_ref,
    spread_ref,
    place_ref,
    codes_ref,
    scale_ref,
    t_ref,
):
    local_part(u_ref, volume_ref, face_ref, mortar_ref, rate_ref, part_ref, t_ref)
    core = core_ref[0]
    list_spread_ref[...] = list_spread(core, send_ref)
    at = received_column(core, face_ref[...])
    columns = [at[face : face + 1, :] for face in range(6)]
    columns.append(received_column(core, mortar_row(mortar_ref)))
    spread_ref[...] = jnp.concatenate([one_hot(1536, column) for column in columns], axis=1)
    target = jnp.concatenate([target_ref[...]] * 4, axis=1)
    place_ref[...] = one_hot(768, target)
    face = jnp.zeros_like(target)
    for k in range(1, 6):
        face = face + jnp.where(target >= 128 * k, 1, 0)
    row = lax.broadcasted_iota(jnp.int32, (4, LANES), 0)
    codes = mortar_row(mortar_code_ref)
    codes_ref[0:6, :] = code_ref[...]
    codes_ref[6:8, :] = jnp.zeros((2, LANES), jnp.int32)
    codes_ref[8:12, :] = jnp.where(row >= 2, codes[:, 128:256], codes[:, 0:128])
    codes_ref[12:16, :] = jnp.where(row >= 2, face[:, 128:256], face[:, 0:128])
    level = refinement_ref[...]
    metric = jnp.where(level == 0, 1.0, jnp.where(level == 1, 2.0, 4.0))
    scale_ref[...] = STEP_SIZE * metric * material_ref[...]


def write_received(core, swapped_ref, near_ref, far_ref, shared_ref, r_ref):
    other = 1 - core
    swapped = pl.multiple_of(other * (5 * UNIT) + 4 * UNIT, 8)
    shared = [pl.multiple_of(other * (3 * UNIT) + UNIT * place, 8) for place in range(3)]
    sources = [
        (shared_ref, shared[2]),
        (shared_ref, shared[0]),
        (shared_ref, shared[1]),
        (swapped_ref, swapped),
        (near_ref, UNIT),
        (near_ref, 0),
        (far_ref, UNIT),
        (far_ref, 0),
    ]
    first = lax.broadcasted_iota(jnp.int32, (48, LANES), 1) < 64
    rests = []
    for k, (ref, start) in enumerate(sources):
        r_ref[:, 128 * k : 128 * k + 128] = ref[pl.ds(start, 96), :]
        rests.append(ref[pl.ds(start + 96, 48), :])
    for pair in range(4):
        even, odd = rests[2 * pair], rests[2 * pair + 1]
        at = 1024 + 128 * pair
        r_ref[0:48, at : at + 128] = jnp.where(first, even, pltpu.roll(odd, 64, 1))
        r_ref[48:96, at : at + 128] = jnp.where(first, pltpu.roll(even, 64, 1), odd)


def received_column(core, source):
    remote = source - 768
    list_at = jnp.zeros_like(source)
    for k in range(1, 8):
        list_at = list_at + jnp.where(remote >= 192 * k, 1, 0)
    slot = remote - 192 * list_at
    seen = list_at + core * (7 - 2 * list_at)
    rest = 1024 + 64 * seen + slot - 128
    return jnp.where(remote < 0, -1, jnp.where(slot < 128, 128 * seen + slot, rest))


def turned(nodes, code):
    swap = code >= 4
    flip_a = (code & 1) == 1
    flip_b = (code & 2) == 2
    out = [
        [nodes[a][b] if a == b else jnp.where(swap, nodes[b][a], nodes[a][b]) for b in range(4)]
        for a in range(4)
    ]
    out = [[jnp.where(flip_a, out[3 - a][b], out[a][b]) for b in range(4)] for a in range(4)]
    return [[jnp.where(flip_b, out[a][3 - b], out[a][b]) for b in range(4)] for a in range(4)]


def applied(nodes, along_a, along_b):
    def summed(terms):
        return (terms[0] + terms[1]) + (terms[2] + terms[3])

    half = [
        [summed([along_a[a][x] * nodes[x][b] for x in range(4)]) for b in range(4)]
        for a in range(4)
    ]
    return [
        [summed([along_b[b][y] * half[a][y] for y in range(4)]) for b in range(4)]
        for a in range(4)
    ]


def exterior(gathered, codes_ref, place_ref, g_ref, m_ref):
    _, halves, adjoint = gll_tables()
    for face in range(6):
        a = face // 2
        b, c = (a + 1) % 3, (a + 2) % 3
        s = 1.0 if face % 2 else -1.0
        boundary = (codes_ref[face : face + 1, :] >> 3) == 1
        sign = jnp.where(boundary, -1.0, 1.0)

        def field(index):
            return gathered[16 * index : 16 * index + 16, 128 * face : 128 * face + 128]

        g_ref[16 * face : 16 * face + 16, :] = sign * field(b) + s * field(3 + c)
        g_ref[96 + 16 * face : 96 + 16 * face + 16, :] = sign * field(c) - s * field(3 + b)
    code = codes_ref[0:6, :]
    kind = code >> 3
    quarter = kind - 2
    plain = kind < 2
    live = kind < 6

    def chosen(which, row, column):
        refined = jnp.where(
            which == 1, float(halves[1][row, column]), float(halves[0][row, column])
        )
        kept = jnp.where(plain, 1.0 if row == column else 0.0, refined)
        return jnp.where(live, kept, 0.0)

    along_a = [[chosen(quarter & 1, i, j) for j in range(4)] for i in range(4)]
    along_b = [[chosen(quarter >> 1, i, j) for j in range(4)] for i in range(4)]
    for w in range(2):
        nodes = [
            [g_ref[pl.ds(96 * w + 4 * a + b, 6, stride=16), :] for b in range(4)] for a in range(4)
        ]
        out = applied(turned(nodes, code & 7), along_a, along_b)
        for a in range(4):
            for b in range(4):
                g_ref[pl.ds(96 * w + 4 * a + b, 6, stride=16), :] = out[a][b]

    for half in range(2):
        face = codes_ref[13 + half : 14 + half, :]
        axis = face >> 1
        s = jnp.where((face & 1) == 1, 1.0, -1.0)
        lanes = slice(768 + 128 * half, 896 + 128 * half)

        def tangential(base, first):
            x, y, z = (
                gathered[16 * f : 16 * f + 16, lanes]
                for f in (base + (first + k) % 3 for k in range(3))
            )
            return jnp.where(axis == 0, x, jnp.where(axis == 1, y, z))

        m_ref[32 * half : 32 * half + 16, :] = tangential(0, 1) + s * tangential(3, 2)
        m_ref[32 * half + 16 : 32 * half + 32, :] = tangential(0, 2) - s * tangential(3, 1)
    lane = lax.broadcasted_iota(jnp.int32, (4, LANES), 1)
    row = lax.broadcasted_iota(jnp.int32, (4, LANES), 0)

    def weight(second, i, j):
        return jnp.where(second, float(adjoint[1][i, j]), float(adjoint[0][i, j]))

    project_a = [[weight(lane >= 64, i, j) for j in range(4)] for i in range(4)]
    project_b = [[weight(row >= 2, i, j) for j in range(4)] for i in range(4)]
    nodes = [[m_ref[pl.ds(4 * a + b, 4, stride=16), :] for b in range(4)] for a in range(4)]
    out = applied(turned(nodes, codes_ref[8:12, :]), project_a, project_b)
    for a in range(4):
        for b in range(4):
            m_ref[pl.ds(4 * a + b, 4, stride=16), :] = out[a][b]
    pieces = jnp.concatenate([m_ref[0:32, :], m_ref[32:64, :]], axis=1)
    both = jnp.concatenate(halves_of(pieces), axis=0)
    placed = lax.dot_general(
        both, place_ref[...], (((1,), (1,)), ((), ())), preferred_element_type=jnp.float32
    )
    placed = placed[0:32] + placed[32:64]
    for w in range(2):
        for at in range(6):
            rows = slice(96 * w + 16 * at, 96 * w + 16 * at + 16)
            g_ref[rows, :] = (
                g_ref[rows, :] + placed[16 * w : 16 * w + 16, 128 * at : 128 * at + 128]
            )


def add_lift(rate_ref, g_ref):
    for face in range(6):
        a = face // 2
        b, c = (a + 1) % 3, (a + 2) % 3
        s = 3.0 if face % 2 else -3.0
        p = g_ref[16 * face : 16 * face + 16, :]
        q = g_ref[96 + 16 * face : 96 + 16 * face + 16, :]
        for f, value in ((b, -3.0 * p), (c, -3.0 * q), (3 + b, s * q), (3 + c, -s * p)):
            base = 64 * f
            if a == 0:
                at = base + (48 if face % 2 else 0)
                rate_ref[at : at + 16, :] = rate_ref[at : at + 16, :] + value
            elif a == 1:
                for i in range(4):
                    at = base + 16 * i + (12 if face % 2 else 0)
                    rate_ref[at : at + 4, :] = rate_ref[at : at + 4, :] + value[4 * i : 4 * i + 4]
            else:
                at = pl.ds(base + (3 if face % 2 else 0), 16, stride=4)
                rate_ref[at, :] = rate_ref[at, :] + value


def section_kernel(section, *refs):
    refs = list(refs)
    core_ref, u_ref = refs[0:2]
    del refs[0:2]
    register_ref = refs.pop(0) if section else None
    rate_in_ref, part_ref, swapped_ref, near_ref, far_ref, shared_ref = refs[0:6]
    spread_ref, place_ref, codes_ref, scale_ref = refs[6:10]
    del refs[0:10]
    list_spread_ref = None if section else refs.pop(0)
    new_u_ref, new_register_ref = refs[0:2]
    del refs[0:2]
    if section == 0:
        swap_ref, own_ref = refs[0:2]
        del refs[0:2]
    r_ref, g_ref, m_ref, rate_ref, t_ref = refs
    core = core_ref[0]
    write_received(core, swapped_ref, near_ref, far_ref, shared_ref, r_ref)
    gathered = part_ref[...] + picked(r_ref[...], spread_ref[...])
    exterior(gathered, codes_ref, place_ref, g_ref, m_ref)
    rate_ref[...] = rate_in_ref[...]
    add_lift(rate_ref, g_ref)
    for half in range(2):
        rows = slice(192 * half, 192 * half + 192)
        register = scale_ref[half : half + 1, :] * rate_ref[rows, :]
        if section:
            register = register + SECTION_A[section] * register_ref[rows, :]
        new_register_ref[rows, :] = register
        new_u_ref[rows, :] = u_ref[rows, :] + SECTION_B[section] * register
    if section == 0:
        write_table(new_u_ref, t_ref)
        write_lists(t_ref, list_spread_ref[...], swap_ref, own_ref)


def shaped(rows, columns=LANES, dtype=jnp.float32):
    return jax.ShapeDtypeStruct((rows, columns), dtype)


def called(kernel, core, operands, outputs, scratch, space=pltpu.VMEM):
    first = [] if core is None else [pl.BlockSpec(memory_space=pltpu.SMEM)]
    given = list(operands) if core is None else [core, *operands]
    return pl.pallas_call(
        kernel,
        in_specs=first + [pl.BlockSpec(memory_space=space)] * len(operands),
        out_specs=[pl.BlockSpec(memory_space=pltpu.VMEM)] * len(outputs),
        out_shape=outputs,
        scratch_shapes=[
            pltpu.VMEM(shape, jnp.float32) if isinstance(shape, tuple) else shape
            for shape in scratch
        ],
        compiler_params=pltpu.CompilerParams(vmem_limit_bytes=VMEM_LIMIT),
    )(*given)


LIST_OUTPUTS = [shaped(5 * UNIT), shaped(3 * UNIT)]


def exchanged(core, swap, own):
    count = lax.axis_size("sfc")
    pairs = [[2 * chip, 2 * chip + 1] for chip in range(count // 2)]

    def ahead(chips):
        ends = [(i, i + 2 * chips if i % 2 == 0 else i - 2 * chips) for i in range(count)]
        return [(source, end) for source, end in ends if 0 <= end < count]

    swapped = lax.all_gather(swap, "sfc", axis_index_groups=pairs, tiled=True)
    theirs = lax.dynamic_slice_in_dim(swapped, (1 - core) * (5 * UNIT), 4 * UNIT)
    u = UNIT
    near = jnp.concatenate([own[0:u], theirs[0:u], own[u : 2 * u], theirs[u : 2 * u]])
    far = jnp.concatenate([own[2 * u : 3 * u], theirs[2 * u : 4 * u]])
    near = lax.ppermute(near, "sfc", ahead(1))
    far = lax.ppermute(far, "sfc", ahead(2))
    shared = jnp.concatenate([near[2 * u : 4 * u], far[2 * u : 3 * u]])
    shared = lax.all_gather(shared, "sfc", axis_index_groups=pairs, tiled=True)
    return swapped, near, far, shared


def local(
    fields,
    material,
    refinement,
    face_source,
    face_code,
    send_face,
    mortar_source,
    mortar_code,
    mortar_target,
):
    core = lax.rem(lax.axis_index("sfc"), 2).astype(jnp.int32)
    core_at = core.reshape(1)
    volume = jnp.asarray(volume_operand())
    solution = fields.reshape(384, LANES)
    refinement = refinement.reshape(1, LANES)
    target = mortar_target.reshape(1, 64)
    table = (96, 768)
    swap, own = called(
        lists_kernel,
        core_at,
        [
            pltpu.with_memory_space_constraint(operand, pltpu.HBM)
            for operand in (solution, send_face)
        ],
        LIST_OUTPUTS,
        [
            table,
            (384, LANES),
            pltpu.VMEM((8, 192), jnp.int32),
            pltpu.SemaphoreType.DMA,
            pltpu.SemaphoreType.DMA,
        ],
        space=pltpu.HBM,
    )
    register = None
    for section in range(2):
        received = exchanged(core, swap, own)
        if section == 0:
            rate, part, list_spread_made, *made = called(
                first_kernel,
                core_at,
                [
                    solution,
                    volume,
                    face_source,
                    mortar_source,
                    face_code,
                    mortar_code,
                    target,
                    material,
                    refinement,
                    send_face,
                ],
                [
                    shaped(384),
                    shaped(96, 1024),
                    shaped(768, 1536, jnp.bfloat16),
                    shaped(1536, 1024, jnp.bfloat16),
                    shaped(768, 256, jnp.bfloat16),
                    shaped(16, LANES, jnp.int32),
                    shaped(2, LANES),
                ],
                [table],
            )
        else:
            rate, part = called(
                local_part,
                None,
                [solution, volume, face_source, mortar_source],
                [shaped(384), shaped(96, 1024)],
                [table],
            )
        operands = [solution] + ([register] if section else [])
        operands += [rate, part, *received, *made]
        outputs = [shaped(384), shaped(384)]
        if section == 0:
            operands.append(list_spread_made)
            outputs = outputs + LIST_OUTPUTS

        def kernel(*refs, section=section):
            section_kernel(section, *refs)

        results = called(
            kernel,
            core_at,
            operands,
            outputs,
            [(96, 1536), (192, LANES), (64, LANES), (384, LANES), table],
        )
        solution, register = results[0:2]
        if section == 0:
            swap, own = results[2:4]
    return (solution.reshape(6, 64, LANES), register.reshape(6, 64, LANES))


def solution(mesh):
    return jax.shard_map(
        local,
        mesh=mesh,
        in_specs=(
            P(None, None, "sfc"),
            P(None, "sfc"),
            P("sfc"),
            P(None, "sfc"),
            P(None, "sfc"),
            P(None, "sfc"),
            P(None, "sfc"),
            P(None, "sfc"),
            P("sfc"),
        ),
        out_specs=(P(None, None, "sfc"), P(None, None, "sfc")),
        check_vma=False,
    )
```

```python
import math

import jax
import jax.numpy as jnp
import numpy as np
from jax import lax
from jax.experimental import pallas as pl
from jax.experimental.pallas import tpu as pltpu
from jax.sharding import PartitionSpec as P

STEP_SIZE = 0.02
SECTION_A = (0.0, -567301805773.0 / 1357537059087.0)
SECTION_B = (1432997174477.0 / 9575080441755.0, 5161836677717.0 / 13612068292357.0)
UNIT = 144
LANES = 128
NEAR_ROWS = 640
ALL_ROWS = 1664
VMEM_LIMIT = 24 * 1024 * 1024


def gll_tables():
    points = np.array([-1.0, -1.0 / math.sqrt(5.0), 1.0 / math.sqrt(5.0), 1.0])
    weights = np.array([1.0, 5.0, 5.0, 1.0]) / 6.0

    def lagrange(where_at):
        values = np.ones((where_at.shape[0], 4))
        for column in range(4):
            for another in range(4):
                if another != column:
                    values[:, column] *= (where_at - points[another]) / (
                        points[column] - points[another]
                    )
        return values

    derivative = np.zeros((4, 4))
    for row_at in range(4):
        for column in range(4):
            summed = 0.0
            for another in range(4):
                if another == column:
                    continue
                factor = 1.0 / (points[column] - points[another])
                for further in range(4):
                    if further != column and further != another:
                        factor *= (points[row_at] - points[further]) / (
                            points[column] - points[further]
                        )
                summed += factor
            derivative[row_at, column] = summed
    halves = [lagrange((points - 1.0) / 2.0), lagrange((points + 1.0) / 2.0)]
    adjoint = [0.5 * halfway.T * weights[None, :] / weights[:, None] for halfway in halves]
    return derivative, halves, adjoint


def face_nodes(face):
    grid = np.arange(64).reshape(4, 4, 4)
    at = 3 if face % 2 else 0
    return [grid[at], grid[:, at], grid[:, :, at]][face // 2].reshape(16)


def volume_map():
    derivative, _, _ = gll_tables()
    eye = np.eye(4)
    along = [
        np.kron(np.kron(derivative, eye), eye),
        np.kron(np.kron(eye, derivative), eye),
        np.kron(np.kron(eye, eye), derivative),
    ]
    whole = np.zeros((6, 64, 6, 64))
    for a in range(3):
        b, c = (a + 1) % 3, (a + 2) % 3
        whole[a, :, 3 + c] += along[b]
        whole[a, :, 3 + b] -= along[c]
        whole[3 + a, :, c] -= along[b]
        whole[3 + a, :, b] += along[c]
    for face in range(6):
        a = face // 2
        b, c = (a + 1) % 3, (a + 2) % 3
        s = 1.0 if face % 2 else -1.0
        for n in face_nodes(face):
            whole[b, n, b, n] += 3.0
            whole[b, n, 3 + c, n] += 3.0 * s
            whole[c, n, c, n] += 3.0
            whole[c, n, 3 + b, n] -= 3.0 * s
            whole[3 + b, n, 3 + b, n] += 3.0
            whole[3 + b, n, c, n] -= 3.0 * s
            whole[3 + c, n, 3 + c, n] += 3.0
            whole[3 + c, n, b, n] += 3.0 * s
    return whole.reshape(384, 384)


def volume_operand():
    whole = volume_map().astype(np.float32)
    high = whole.astype(jnp.bfloat16)
    low = (whole - high.astype(np.float32)).astype(jnp.bfloat16)
    return np.concatenate([high, high, low], axis=1)


def halves_of(value):
    high = value.astype(jnp.bfloat16)
    low = (value - high.astype(jnp.float32)).astype(jnp.bfloat16)
    return high, low


def one_hot(rows, columns):
    at = lax.broadcasted_iota(jnp.int32, (rows, columns.shape[1]), 0)
    return jnp.where(at == columns, 1.0, 0.0).astype(jnp.bfloat16)


def picked(table, columns):
    rows = table.shape[0]
    both = jnp.concatenate(halves_of(table), axis=0)
    out = jnp.dot(both, columns, preferred_element_type=jnp.float32)
    return out[:rows] + out[rows:]


def write_table(u_ref, t_ref, fields=range(6)):
    for f in fields:
        base = 64 * f
        rows = slice(16 * f, 16 * f + 16)
        t_ref[rows, 0:128] = u_ref[base : base + 16, :]
        t_ref[rows, 128:256] = u_ref[base + 48 : base + 64, :]
        for side, at in ((2, 0), (3, 12)):
            for i in range(4):
                start = base + 16 * i + at
                t_ref[16 * f + 4 * i : 16 * f + 4 * i + 4, 128 * side : 128 * side + 128] = u_ref[
                    start : start + 4, :
                ]
        t_ref[rows, 512:640] = u_ref[pl.ds(base, 16, stride=4), :]
        t_ref[rows, 640:768] = u_ref[pl.ds(base + 3, 16, stride=4), :]


def list_spread(core, send_ref):
    def listed(k, lanes):
        return jnp.where(core == 0, send_ref[k : k + 1, lanes], send_ref[7 - k : 8 - k, lanes])

    columns = [listed(k, slice(0, 128)) for k in range(8)]
    for pair in range(4):
        rests = [listed(2 * pair + k, slice(128, 192)) for k in range(2)]
        columns.append(jnp.concatenate(rests, axis=1))
    return jnp.concatenate([one_hot(768, column) for column in columns], axis=1)


def write_lists(t_ref, spread, swap_ref, own_ref):
    out = picked(t_ref[...], spread)
    first = lax.broadcasted_iota(jnp.int32, (48, LANES), 1) < 64
    places = {4 - d: (swap_ref, d - 1) for d in range(1, 5)}
    places[4] = (swap_ref, 4)
    places.update({3 + d: (own_ref, d - 2) for d in range(2, 5)})
    for k in range(8):
        ref, place = places[k]
        ref[UNIT * place : UNIT * place + 96, :] = out[:, 128 * k : 128 * k + 128]
        at = 1024 + 128 * (k // 2)
        upper, lower = out[0:48, at : at + 128], out[48:96, at : at + 128]
        if k % 2 == 0:
            packed = jnp.where(first, upper, pltpu.roll(lower, 64, 1))
        else:
            packed = jnp.where(first, pltpu.roll(upper, 64, 1), lower)
        ref[UNIT * place + 96 : UNIT * place + UNIT, :] = packed


def lists_kernel(
    core_ref, u_hbm, send_hbm, swap_ref, own_ref, t_ref, u_ref, send_ref, send_sem, u_sems
):
    send_copy = pltpu.make_async_copy(send_hbm, send_ref, send_sem)
    send_copy.start()
    u_copies = [
        pltpu.make_async_copy(
            u_hbm.at[pl.ds(64 * f, 64)], u_ref.at[pl.ds(64 * f, 64)], u_sems.at[f]
        )
        for f in range(6)
    ]
    for copy in u_copies:
        copy.start()
    send_copy.wait()
    spread = list_spread(core_ref[0], send_ref)
    for f, copy in enumerate(u_copies):
        copy.wait()
        write_table(u_ref, t_ref, [f])
    write_lists(t_ref, spread, swap_ref, own_ref)


def mortar_row(ref):
    return jnp.concatenate([ref[q : q + 1, :] for q in range(4)], axis=1)


def local_part(u_ref, volume_ref, face_ref, mortar_ref, rate_ref, part_ref, t_ref):
    high, low = halves_of(u_ref[...])
    rate_ref[...] = jnp.dot(
        volume_ref[...],
        jnp.concatenate([high, low, high], axis=0),
        preferred_element_type=jnp.float32,
    )
    write_table(u_ref, t_ref)
    columns = [face_ref[face : face + 1, :] for face in range(6)] + [mortar_row(mortar_ref)]
    spread = jnp.concatenate([one_hot(768, column) for column in columns], axis=1)
    part_ref[...] = picked(t_ref[...], spread)


def first_kernel(
    core_ref,
    u_ref,
    volume_ref,
    face_ref,
    mortar_ref,
    code_ref,
    mortar_code_ref,
    target_ref,
    material_ref,
    refinement_ref,
    send_ref,
    rate_ref,
    part_ref,
    list_spread_ref,
    spread_ref,
    place_ref,
    codes_ref,
    scale_ref,
    t_ref,
):
    local_part(u_ref, volume_ref, face_ref, mortar_ref, rate_ref, part_ref, t_ref)
    core = core_ref[0]
    list_spread_ref[...] = list_spread(core, send_ref)
    at = received_column(core, face_ref[...])
    columns = [at[face : face + 1, :] for face in range(6)]
    columns.append(received_column(core, mortar_row(mortar_ref)))
    spread_ref[...] = jnp.concatenate([one_hot(ALL_ROWS, column) for column in columns], axis=1)
    target = jnp.concatenate([target_ref[...]] * 4, axis=1)
    place_ref[...] = one_hot(768, target)
    face = jnp.zeros_like(target)
    for k in range(1, 6):
        face = face + jnp.where(target >= 128 * k, 1, 0)
    row = lax.broadcasted_iota(jnp.int32, (4, LANES), 0)
    codes = mortar_row(mortar_code_ref)
    codes_ref[0:6, :] = code_ref[...]
    codes_ref[6:8, :] = jnp.zeros((2, LANES), jnp.int32)
    codes_ref[8:12, :] = jnp.where(row >= 2, codes[:, 128:256], codes[:, 0:128])
    codes_ref[12:16, :] = jnp.where(row >= 2, face[:, 128:256], face[:, 0:128])
    level = refinement_ref[...]
    metric = jnp.where(level == 0, 1.0, jnp.where(level == 1, 2.0, 4.0))
    scale_ref[...] = STEP_SIZE * metric * material_ref[...]


def write_units(sources, r_ref):
    count = len(sources)
    first = lax.broadcasted_iota(jnp.int32, (48, LANES), 1) < 64
    none = jnp.zeros((48, LANES), jnp.float32)
    rests = []
    for k, (ref, start) in enumerate(sources):
        r_ref[:, 128 * k : 128 * k + 128] = ref[pl.ds(start, 96), :]
        rests.append(ref[pl.ds(start + 96, 48), :])
    for k in range(0, count, 2):
        even, odd = rests[k], rests[k + 1] if k + 1 < count else none
        at = 128 * count + 64 * k
        r_ref[0:48, at : at + 128] = jnp.where(first, even, pltpu.roll(odd, 64, 1))
        r_ref[48:96, at : at + 128] = jnp.where(first, pltpu.roll(even, 64, 1), odd)


def near_kernel(core_ref, part_ref, spread_ref, swapped_ref, near_ref, out_ref, give_ref, r_ref):
    swapped = pl.multiple_of((1 - core_ref[0]) * (5 * UNIT) + 4 * UNIT, 8)
    write_units([(swapped_ref, swapped), (near_ref, UNIT), (near_ref, 0)], r_ref)
    out_ref[...] = part_ref[...] + picked(r_ref[...], spread_ref[0:NEAR_ROWS, :])
    give_ref[...] = near_ref[2 * UNIT : 4 * UNIT, :]


def join_kernel(give_ref, far_ref, out_ref):
    out_ref[0 : 2 * UNIT, :] = give_ref[...]
    out_ref[2 * UNIT : 3 * UNIT, :] = far_ref[2 * UNIT : 3 * UNIT, :]


def write_far(core, far_ref, shared_ref, r_ref):
    shared = [pl.multiple_of((1 - core) * (3 * UNIT) + UNIT * place, 8) for place in range(3)]
    sources = [(shared_ref, shared[place]) for place in (2, 0, 1)]
    write_units(sources + [(far_ref, UNIT), (far_ref, 0)], r_ref)


def received_column(core, source):
    remote = source - 768
    list_at = jnp.zeros_like(source)
    for k in range(1, 8):
        list_at = list_at + jnp.where(remote >= 192 * k, 1, 0)
    slot = remote - 192 * list_at
    seen = list_at + core * (7 - 2 * list_at)
    near = (seen >= 3) & (seen < 6)
    place = jnp.where(seen < 3, seen, seen - 3)
    main = jnp.where(near, 0, NEAR_ROWS) + 128 * place + slot
    rest = jnp.where(near, 384, NEAR_ROWS + 640) + 64 * place + slot - 128
    return jnp.where(remote < 0, -1, jnp.where(slot < 128, main, rest))


def turned(nodes, code):
    swap = code >= 4
    flip_a = (code & 1) == 1
    flip_b = (code & 2) == 2
    out = [
        [nodes[a][b] if a == b else jnp.where(swap, nodes[b][a], nodes[a][b]) for b in range(4)]
        for a in range(4)
    ]
    out = [[jnp.where(flip_a, out[3 - a][b], out[a][b]) for b in range(4)] for a in range(4)]
    return [[jnp.where(flip_b, out[a][3 - b], out[a][b]) for b in range(4)] for a in range(4)]


def applied(nodes, along_a, along_b):
    def summed(terms):
        return (terms[0] + terms[1]) + (terms[2] + terms[3])

    half = [
        [summed([along_a[a][x] * nodes[x][b] for x in range(4)]) for b in range(4)]
        for a in range(4)
    ]
    return [
        [summed([along_b[b][y] * half[a][y] for y in range(4)]) for b in range(4)]
        for a in range(4)
    ]


def exterior(gathered, codes_ref, place_ref, g_ref, m_ref):
    _, halves, adjoint = gll_tables()
    for face in range(6):
        a = face // 2
        b, c = (a + 1) % 3, (a + 2) % 3
        s = 1.0 if face % 2 else -1.0
        boundary = (codes_ref[face : face + 1, :] >> 3) == 1
        sign = jnp.where(boundary, -1.0, 1.0)

        def field(index):
            return gathered[16 * index : 16 * index + 16, 128 * face : 128 * face + 128]

        g_ref[16 * face : 16 * face + 16, :] = sign * field(b) + s * field(3 + c)
        g_ref[96 + 16 * face : 96 + 16 * face + 16, :] = sign * field(c) - s * field(3 + b)
    code = codes_ref[0:6, :]
    kind = code >> 3
    quarter = kind - 2
    plain = kind < 2
    live = kind < 6

    def chosen(which, row, column):
        refined = jnp.where(
            which == 1, float(halves[1][row, column]), float(halves[0][row, column])
        )
        kept = jnp.where(plain, 1.0 if row == column else 0.0, refined)
        return jnp.where(live, kept, 0.0)

    along_a = [[chosen(quarter & 1, i, j) for j in range(4)] for i in range(4)]
    along_b = [[chosen(quarter >> 1, i, j) for j in range(4)] for i in range(4)]
    for w in range(2):
        nodes = [
            [g_ref[pl.ds(96 * w + 4 * a + b, 6, stride=16), :] for b in range(4)] for a in range(4)
        ]
        out = applied(turned(nodes, code & 7), along_a, along_b)
        for a in range(4):
            for b in range(4):
                g_ref[pl.ds(96 * w + 4 * a + b, 6, stride=16), :] = out[a][b]

    for half in range(2):
        face = codes_ref[13 + half : 14 + half, :]
        axis = face >> 1
        s = jnp.where((face & 1) == 1, 1.0, -1.0)
        lanes = slice(768 + 128 * half, 896 + 128 * half)

        def tangential(base, first):
            x, y, z = (
                gathered[16 * f : 16 * f + 16, lanes]
                for f in (base + (first + k) % 3 for k in range(3))
            )
            return jnp.where(axis == 0, x, jnp.where(axis == 1, y, z))

        m_ref[32 * half : 32 * half + 16, :] = tangential(0, 1) + s * tangential(3, 2)
        m_ref[32 * half + 16 : 32 * half + 32, :] = tangential(0, 2) - s * tangential(3, 1)
    lane = lax.broadcasted_iota(jnp.int32, (4, LANES), 1)
    row = lax.broadcasted_iota(jnp.int32, (4, LANES), 0)

    def weight(second, i, j):
        return jnp.where(second, float(adjoint[1][i, j]), float(adjoint[0][i, j]))

    project_a = [[weight(lane >= 64, i, j) for j in range(4)] for i in range(4)]
    project_b = [[weight(row >= 2, i, j) for j in range(4)] for i in range(4)]
    nodes = [[m_ref[pl.ds(4 * a + b, 4, stride=16), :] for b in range(4)] for a in range(4)]
    out = applied(turned(nodes, codes_ref[8:12, :]), project_a, project_b)
    for a in range(4):
        for b in range(4):
            m_ref[pl.ds(4 * a + b, 4, stride=16), :] = out[a][b]
    pieces = jnp.concatenate([m_ref[0:32, :], m_ref[32:64, :]], axis=1)
    both = jnp.concatenate(halves_of(pieces), axis=0)
    placed = lax.dot_general(
        both, place_ref[...], (((1,), (1,)), ((), ())), preferred_element_type=jnp.float32
    )
    placed = placed[0:32] + placed[32:64]
    for w in range(2):
        for at in range(6):
            rows = slice(96 * w + 16 * at, 96 * w + 16 * at + 16)
            g_ref[rows, :] = (
                g_ref[rows, :] + placed[16 * w : 16 * w + 16, 128 * at : 128 * at + 128]
            )


def add_lift(rate_ref, g_ref):
    for face in range(6):
        a = face // 2
        b, c = (a + 1) % 3, (a + 2) % 3
        s = 3.0 if face % 2 else -3.0
        p = g_ref[16 * face : 16 * face + 16, :]
        q = g_ref[96 + 16 * face : 96 + 16 * face + 16, :]
        for f, value in ((b, -3.0 * p), (c, -3.0 * q), (3 + b, s * q), (3 + c, -s * p)):
            base = 64 * f
            if a == 0:
                at = base + (48 if face % 2 else 0)
                rate_ref[at : at + 16, :] = rate_ref[at : at + 16, :] + value
            elif a == 1:
                for i in range(4):
                    at = base + 16 * i + (12 if face % 2 else 0)
                    rate_ref[at : at + 4, :] = rate_ref[at : at + 4, :] + value[4 * i : 4 * i + 4]
            else:
                at = pl.ds(base + (3 if face % 2 else 0), 16, stride=4)
                rate_ref[at, :] = rate_ref[at, :] + value


def section_kernel(section, *refs):
    refs = list(refs)
    core_ref, u_ref = refs[0:2]
    del refs[0:2]
    register_ref = refs.pop(0) if section else None
    rate_in_ref, part_ref, far_ref, shared_ref = refs[0:4]
    spread_ref, place_ref, codes_ref, scale_ref = refs[4:8]
    del refs[0:8]
    list_spread_ref = None if section else refs.pop(0)
    outs = refs[0:2]
    del refs[0:2]
    if section == 0:
        swap_ref, own_ref = refs[0:2]
        del refs[0:2]
        new_u_ref, new_register_ref = outs
    else:
        new_u_ref, new_register_ref, sems = refs[0:3]
        del refs[0:3]
    r_ref, g_ref, m_ref, rate_ref, t_ref = refs
    core = core_ref[0]
    write_far(core, far_ref, shared_ref, r_ref)
    gathered = part_ref[...] + picked(r_ref[...], spread_ref[NEAR_ROWS:ALL_ROWS, :])
    exterior(gathered, codes_ref, place_ref, g_ref, m_ref)
    rate_ref[...] = rate_in_ref[...]
    add_lift(rate_ref, g_ref)
    copies = []
    for half in range(2):
        rows = slice(192 * half, 192 * half + 192)
        register = scale_ref[half : half + 1, :] * rate_ref[rows, :]
        if section:
            register = register + SECTION_A[section] * register_ref[rows, :]
        new_register_ref[rows, :] = register
        new_u_ref[rows, :] = u_ref[rows, :] + SECTION_B[section] * register
        if section:
            for f in range(3 * half, 3 * half + 3):
                for which, ref in enumerate((new_u_ref, new_register_ref)):
                    rows = pl.ds(64 * f, 64)
                    copy = pltpu.make_async_copy(
                        ref.at[rows], outs[which].at[rows], sems.at[2 * f + which]
                    )
                    copy.start()
                    copies.append(copy)
    for copy in copies:
        copy.wait()
    if section == 0:
        write_table(new_u_ref, t_ref)
        write_lists(t_ref, list_spread_ref[...], swap_ref, own_ref)


def shaped(rows, columns=LANES, dtype=jnp.float32):
    return jax.ShapeDtypeStruct((rows, columns), dtype)


def called(kernel, core, operands, outputs, scratch, space=pltpu.VMEM, out=pltpu.VMEM):
    first = [] if core is None else [pl.BlockSpec(memory_space=pltpu.SMEM)]
    given = list(operands) if core is None else [core, *operands]
    return pl.pallas_call(
        kernel,
        in_specs=first + [pl.BlockSpec(memory_space=space)] * len(operands),
        out_specs=[pl.BlockSpec(memory_space=out)] * len(outputs),
        out_shape=outputs,
        scratch_shapes=[
            pltpu.VMEM(shape, jnp.float32) if isinstance(shape, tuple) else shape
            for shape in scratch
        ],
        compiler_params=pltpu.CompilerParams(vmem_limit_bytes=VMEM_LIMIT),
    )(*given)


LIST_OUTPUTS = [shaped(5 * UNIT), shaped(3 * UNIT)]


def exchanged(core, swap, own, gather_near):
    count = lax.axis_size("sfc")
    pairs = [[2 * chip, 2 * chip + 1] for chip in range(count // 2)]

    def ahead(chips):
        ends = [(i, i + 2 * chips if i % 2 == 0 else i - 2 * chips) for i in range(count)]
        return [(source, end) for source, end in ends if 0 <= end < count]

    swapped = lax.all_gather(swap, "sfc", axis_index_groups=pairs, tiled=True)
    theirs = lax.dynamic_slice_in_dim(swapped, (1 - core) * (5 * UNIT), 4 * UNIT)
    u = UNIT
    near = jnp.concatenate([own[0:u], theirs[0:u], own[u : 2 * u], theirs[u : 2 * u]])
    far = jnp.concatenate([own[2 * u : 3 * u], theirs[2 * u : 4 * u]])
    near = lax.ppermute(near, "sfc", ahead(1))
    far = lax.ppermute(far, "sfc", ahead(2))
    part, give = gather_near(swapped, near)
    (shared,) = called(join_kernel, None, [give, far], [shaped(3 * u)], [])
    shared = lax.all_gather(shared, "sfc", axis_index_groups=pairs, tiled=True)
    return part, far, shared


def local(
    fields,
    material,
    refinement,
    face_source,
    face_code,
    send_face,
    mortar_source,
    mortar_code,
    mortar_target,
):
    core = lax.rem(lax.axis_index("sfc"), 2).astype(jnp.int32)
    core_at = core.reshape(1)
    volume = jnp.asarray(volume_operand())
    solution = fields.reshape(384, LANES)
    refinement = refinement.reshape(1, LANES)
    target = mortar_target.reshape(1, 64)
    table = (96, 768)
    swap, own = called(
        lists_kernel,
        core_at,
        [
            pltpu.with_memory_space_constraint(operand, pltpu.HBM)
            for operand in (solution, send_face)
        ],
        LIST_OUTPUTS,
        [
            table,
            (384, LANES),
            pltpu.VMEM((8, 192), jnp.int32),
            pltpu.SemaphoreType.DMA,
            pltpu.SemaphoreType.DMA((6,)),
        ],
        space=pltpu.HBM,
    )
    register = None
    for section in range(2):
        if section == 0:
            rate, part, list_spread_made, *made = called(
                first_kernel,
                core_at,
                [
                    solution,
                    volume,
                    face_source,
                    mortar_source,
                    face_code,
                    mortar_code,
                    target,
                    material,
                    refinement,
                    send_face,
                ],
                [
                    shaped(384),
                    shaped(96, 1024),
                    shaped(768, 1536, jnp.bfloat16),
                    shaped(ALL_ROWS, 1024, jnp.bfloat16),
                    shaped(768, 256, jnp.bfloat16),
                    shaped(16, LANES, jnp.int32),
                    shaped(2, LANES),
                ],
                [table],
            )
        else:
            rate, part = called(
                local_part,
                None,
                [solution, volume, face_source, mortar_source],
                [shaped(384), shaped(96, 1024)],
                [table],
            )

        def gather_near(swapped, near, part=part):
            operands = [part, made[0], swapped, near]
            outputs = [shaped(96, 1024), shaped(2 * UNIT)]
            return called(near_kernel, core_at, operands, outputs, [(96, NEAR_ROWS)])

        part, far, shared = exchanged(core, swap, own, gather_near)
        operands = [solution] + ([register] if section else [])
        operands += [rate, part, far, shared, *made]
        outputs = [shaped(384), shaped(384)]
        scratch = [(96, ALL_ROWS - NEAR_ROWS), (192, LANES), (64, LANES), (384, LANES), table]
        if section:
            scratch = [(384, LANES), (384, LANES), pltpu.SemaphoreType.DMA((12,)), *scratch]
        if section == 0:
            operands.append(list_spread_made)
            outputs = outputs + LIST_OUTPUTS

        def kernel(*refs, section=section):
            section_kernel(section, *refs)

        results = called(
            kernel,
            core_at,
            operands,
            outputs,
            scratch,
            out=pltpu.HBM if section else pltpu.VMEM,
        )
        solution, register = results[0:2]
        if section == 0:
            swap, own = results[2:4]
    return (solution.reshape(6, 64, LANES), register.reshape(6, 64, LANES))


def solution(mesh):
    return jax.shard_map(
        local,
        mesh=mesh,
        in_specs=(
            P(None, None, "sfc"),
            P(None, "sfc"),
            P("sfc"),
            P(None, "sfc"),
            P(None, "sfc"),
            P(None, "sfc"),
            P(None, "sfc"),
            P(None, "sfc"),
            P("sfc"),
        ),
        out_specs=(P(None, None, "sfc"), P(None, None, "sfc")),
        check_vma=False,
    )
```

```python
import math

import jax
import jax.numpy as jnp
import numpy as np
from jax import lax
from jax.experimental import pallas as pl
from jax.experimental.pallas import tpu as pltpu
from jax.sharding import PartitionSpec as P

STEP_SIZE = 0.02
SECTION_A = (0.0, -567301805773.0 / 1357537059087.0)
SECTION_B = (1432997174477.0 / 9575080441755.0, 5161836677717.0 / 13612068292357.0)
UNIT = 144
LANES = 128
NEAR_ROWS = 640
ALL_ROWS = 1664
VMEM_LIMIT = 24 * 1024 * 1024


def gll_tables():
    points = np.array([-1.0, -1.0 / math.sqrt(5.0), 1.0 / math.sqrt(5.0), 1.0])
    weights = np.array([1.0, 5.0, 5.0, 1.0]) / 6.0

    def lagrange(where_at):
        values = np.ones((where_at.shape[0], 4))
        for column in range(4):
            for another in range(4):
                if another != column:
                    values[:, column] *= (where_at - points[another]) / (
                        points[column] - points[another]
                    )
        return values

    derivative = np.zeros((4, 4))
    for row_at in range(4):
        for column in range(4):
            summed = 0.0
            for another in range(4):
                if another == column:
                    continue
                factor = 1.0 / (points[column] - points[another])
                for further in range(4):
                    if further != column and further != another:
                        factor *= (points[row_at] - points[further]) / (
                            points[column] - points[further]
                        )
                summed += factor
            derivative[row_at, column] = summed
    halves = [lagrange((points - 1.0) / 2.0), lagrange((points + 1.0) / 2.0)]
    adjoint = [0.5 * halfway.T * weights[None, :] / weights[:, None] for halfway in halves]
    return derivative, halves, adjoint


def face_nodes(face):
    grid = np.arange(64).reshape(4, 4, 4)
    at = 3 if face % 2 else 0
    return [grid[at], grid[:, at], grid[:, :, at]][face // 2].reshape(16)


def volume_map():
    derivative, _, _ = gll_tables()
    eye = np.eye(4)
    along = [
        np.kron(np.kron(derivative, eye), eye),
        np.kron(np.kron(eye, derivative), eye),
        np.kron(np.kron(eye, eye), derivative),
    ]
    whole = np.zeros((6, 64, 6, 64))
    for a in range(3):
        b, c = (a + 1) % 3, (a + 2) % 3
        whole[a, :, 3 + c] += along[b]
        whole[a, :, 3 + b] -= along[c]
        whole[3 + a, :, c] -= along[b]
        whole[3 + a, :, b] += along[c]
    for face in range(6):
        a = face // 2
        b, c = (a + 1) % 3, (a + 2) % 3
        s = 1.0 if face % 2 else -1.0
        for n in face_nodes(face):
            whole[b, n, b, n] += 3.0
            whole[b, n, 3 + c, n] += 3.0 * s
            whole[c, n, c, n] += 3.0
            whole[c, n, 3 + b, n] -= 3.0 * s
            whole[3 + b, n, 3 + b, n] += 3.0
            whole[3 + b, n, c, n] -= 3.0 * s
            whole[3 + c, n, 3 + c, n] += 3.0
            whole[3 + c, n, b, n] += 3.0 * s
    return whole.reshape(384, 384)


def volume_operand():
    whole = volume_map().astype(np.float32)
    high = whole.astype(jnp.bfloat16)
    low = (whole - high.astype(np.float32)).astype(jnp.bfloat16)
    return np.concatenate([high, high, low], axis=1)


def halves_of(value):
    high = value.astype(jnp.bfloat16)
    low = (value - high.astype(jnp.float32)).astype(jnp.bfloat16)
    return high, low


def one_hot(rows, columns):
    at = lax.broadcasted_iota(jnp.int32, (rows, columns.shape[1]), 0)
    return jnp.where(at == columns, 1.0, 0.0).astype(jnp.bfloat16)


def picked(table, columns):
    rows = table.shape[0]
    both = jnp.concatenate(halves_of(table), axis=0)
    out = jnp.dot(both, columns, preferred_element_type=jnp.float32)
    return out[:rows] + out[rows:]


def write_table(u_ref, t_ref, fields=range(6)):
    for f in fields:
        base = 64 * f
        rows = slice(16 * f, 16 * f + 16)
        t_ref[rows, 0:128] = u_ref[base : base + 16, :]
        t_ref[rows, 128:256] = u_ref[base + 48 : base + 64, :]
        for side, at in ((2, 0), (3, 12)):
            for i in range(4):
                start = base + 16 * i + at
                t_ref[16 * f + 4 * i : 16 * f + 4 * i + 4, 128 * side : 128 * side + 128] = u_ref[
                    start : start + 4, :
                ]
        t_ref[rows, 512:640] = u_ref[pl.ds(base, 16, stride=4), :]
        t_ref[rows, 640:768] = u_ref[pl.ds(base + 3, 16, stride=4), :]


def list_spread(core, send_ref):
    def listed(k, lanes):
        return jnp.where(core == 0, send_ref[k : k + 1, lanes], send_ref[7 - k : 8 - k, lanes])

    columns = [listed(k, slice(0, 128)) for k in range(8)]
    for pair in range(4):
        rests = [listed(2 * pair + k, slice(128, 192)) for k in range(2)]
        columns.append(jnp.concatenate(rests, axis=1))
    return jnp.concatenate([one_hot(768, column) for column in columns], axis=1)


def write_lists(t_ref, spread, swap_ref, own_ref):
    out = picked(t_ref[...], spread)
    first = lax.broadcasted_iota(jnp.int32, (48, LANES), 1) < 64
    places = {4 - d: (swap_ref, d - 1) for d in range(1, 5)}
    places[4] = (swap_ref, 4)
    places.update({3 + d: (own_ref, d - 2) for d in range(2, 5)})
    for k in range(8):
        ref, place = places[k]
        ref[UNIT * place : UNIT * place + 96, :] = out[:, 128 * k : 128 * k + 128]
        at = 1024 + 128 * (k // 2)
        upper, lower = out[0:48, at : at + 128], out[48:96, at : at + 128]
        if k % 2 == 0:
            packed = jnp.where(first, upper, pltpu.roll(lower, 64, 1))
        else:
            packed = jnp.where(first, pltpu.roll(upper, 64, 1), lower)
        ref[UNIT * place + 96 : UNIT * place + UNIT, :] = packed


def lists_kernel(
    core_ref, u_hbm, send_hbm, swap_ref, own_ref, t_ref, u_ref, send_ref, send_sem, u_sem
):
    send_copy = pltpu.make_async_copy(send_hbm, send_ref, send_sem)
    send_copy.start()
    u_copy = pltpu.make_async_copy(u_hbm, u_ref, u_sem)
    u_copy.start()
    send_copy.wait()
    spread = list_spread(core_ref[0], send_ref)
    u_copy.wait()
    write_table(u_ref, t_ref)
    write_lists(t_ref, spread, swap_ref, own_ref)


def mortar_row(ref):
    return jnp.concatenate([ref[q : q + 1, :] for q in range(4)], axis=1)


def local_part(u_ref, volume_ref, face_ref, mortar_ref, rate_ref, part_ref, t_ref):
    high, low = halves_of(u_ref[...])
    rate_ref[...] = jnp.dot(
        volume_ref[...],
        jnp.concatenate([high, low, high], axis=0),
        preferred_element_type=jnp.float32,
    )
    write_table(u_ref, t_ref)
    columns = [face_ref[face : face + 1, :] for face in range(6)] + [mortar_row(mortar_ref)]
    spread = jnp.concatenate([one_hot(768, column) for column in columns], axis=1)
    part_ref[...] = picked(t_ref[...], spread)


def first_kernel(
    core_ref,
    u_ref,
    volume_ref,
    face_ref,
    mortar_ref,
    code_ref,
    mortar_code_ref,
    target_ref,
    material_ref,
    refinement_ref,
    send_ref,
    rate_ref,
    part_ref,
    list_spread_ref,
    spread_ref,
    place_ref,
    codes_ref,
    scale_ref,
    t_ref,
):
    local_part(u_ref, volume_ref, face_ref, mortar_ref, rate_ref, part_ref, t_ref)
    core = core_ref[0]
    list_spread_ref[...] = list_spread(core, send_ref)
    at = received_column(core, face_ref[...])
    columns = [at[face : face + 1, :] for face in range(6)]
    columns.append(received_column(core, mortar_row(mortar_ref)))
    spread_ref[...] = jnp.concatenate([one_hot(ALL_ROWS, column) for column in columns], axis=1)
    target = jnp.concatenate([target_ref[...]] * 4, axis=1)
    place_ref[...] = one_hot(768, target)
    face = jnp.zeros_like(target)
    for k in range(1, 6):
        face = face + jnp.where(target >= 128 * k, 1, 0)
    row = lax.broadcasted_iota(jnp.int32, (4, LANES), 0)
    codes = mortar_row(mortar_code_ref)
    codes_ref[0:6, :] = code_ref[...]
    codes_ref[6:8, :] = jnp.zeros((2, LANES), jnp.int32)
    codes_ref[8:12, :] = jnp.where(row >= 2, codes[:, 128:256], codes[:, 0:128])
    codes_ref[12:16, :] = jnp.where(row >= 2, face[:, 128:256], face[:, 0:128])
    level = refinement_ref[...]
    metric = jnp.where(level == 0, 1.0, jnp.where(level == 1, 2.0, 4.0))
    scale_ref[...] = STEP_SIZE * metric * material_ref[...]


def write_units(sources, r_ref):
    count = len(sources)
    first = lax.broadcasted_iota(jnp.int32, (48, LANES), 1) < 64
    none = jnp.zeros((48, LANES), jnp.float32)
    rests = []
    for k, (ref, start) in enumerate(sources):
        r_ref[:, 128 * k : 128 * k + 128] = ref[pl.ds(start, 96), :]
        rests.append(ref[pl.ds(start + 96, 48), :])
    for k in range(0, count, 2):
        even, odd = rests[k], rests[k + 1] if k + 1 < count else none
        at = 128 * count + 64 * k
        r_ref[0:48, at : at + 128] = jnp.where(first, even, pltpu.roll(odd, 64, 1))
        r_ref[48:96, at : at + 128] = jnp.where(first, pltpu.roll(even, 64, 1), odd)


def near_kernel(core_ref, part_ref, spread_ref, swapped_ref, near_ref, out_ref, give_ref, r_ref):
    swapped = pl.multiple_of((1 - core_ref[0]) * (5 * UNIT) + 4 * UNIT, 8)
    write_units([(swapped_ref, swapped), (near_ref, UNIT), (near_ref, 0)], r_ref)
    out_ref[...] = part_ref[...] + picked(r_ref[...], spread_ref[0:NEAR_ROWS, :])
    give_ref[...] = near_ref[2 * UNIT : 4 * UNIT, :]


def join_kernel(give_ref, far_ref, out_ref):
    out_ref[0 : 2 * UNIT, :] = give_ref[...]
    out_ref[2 * UNIT : 3 * UNIT, :] = far_ref[2 * UNIT : 3 * UNIT, :]


def write_far(core, far_ref, shared_ref, r_ref):
    shared = [pl.multiple_of((1 - core) * (3 * UNIT) + UNIT * place, 8) for place in range(3)]
    sources = [(shared_ref, shared[place]) for place in (2, 0, 1)]
    write_units(sources + [(far_ref, UNIT), (far_ref, 0)], r_ref)


def received_column(core, source):
    remote = source - 768
    list_at = jnp.zeros_like(source)
    for k in range(1, 8):
        list_at = list_at + jnp.where(remote >= 192 * k, 1, 0)
    slot = remote - 192 * list_at
    seen = list_at + core * (7 - 2 * list_at)
    near = (seen >= 3) & (seen < 6)
    place = jnp.where(seen < 3, seen, seen - 3)
    main = jnp.where(near, 0, NEAR_ROWS) + 128 * place + slot
    rest = jnp.where(near, 384, NEAR_ROWS + 640) + 64 * place + slot - 128
    return jnp.where(remote < 0, -1, jnp.where(slot < 128, main, rest))


def turned(nodes, code):
    swap = code >= 4
    flip_a = (code & 1) == 1
    flip_b = (code & 2) == 2
    out = [
        [nodes[a][b] if a == b else jnp.where(swap, nodes[b][a], nodes[a][b]) for b in range(4)]
        for a in range(4)
    ]
    out = [[jnp.where(flip_a, out[3 - a][b], out[a][b]) for b in range(4)] for a in range(4)]
    return [[jnp.where(flip_b, out[a][3 - b], out[a][b]) for b in range(4)] for a in range(4)]


def applied(nodes, along_a, along_b):
    def summed(terms):
        return (terms[0] + terms[1]) + (terms[2] + terms[3])

    half = [
        [summed([along_a[a][x] * nodes[x][b] for x in range(4)]) for b in range(4)]
        for a in range(4)
    ]
    return [
        [summed([along_b[b][y] * half[a][y] for y in range(4)]) for b in range(4)]
        for a in range(4)
    ]


def exterior(gathered, codes_ref, place_ref, g_ref, m_ref):
    _, halves, adjoint = gll_tables()
    for face in range(6):
        a = face // 2
        b, c = (a + 1) % 3, (a + 2) % 3
        s = 1.0 if face % 2 else -1.0
        boundary = (codes_ref[face : face + 1, :] >> 3) == 1
        sign = jnp.where(boundary, -1.0, 1.0)

        def field(index):
            return gathered[16 * index : 16 * index + 16, 128 * face : 128 * face + 128]

        g_ref[16 * face : 16 * face + 16, :] = sign * field(b) + s * field(3 + c)
        g_ref[96 + 16 * face : 96 + 16 * face + 16, :] = sign * field(c) - s * field(3 + b)
    code = codes_ref[0:6, :]
    kind = code >> 3
    quarter = kind - 2
    plain = kind < 2
    live = kind < 6

    def chosen(which, row, column):
        refined = jnp.where(
            which == 1, float(halves[1][row, column]), float(halves[0][row, column])
        )
        kept = jnp.where(plain, 1.0 if row == column else 0.0, refined)
        return jnp.where(live, kept, 0.0)

    along_a = [[chosen(quarter & 1, i, j) for j in range(4)] for i in range(4)]
    along_b = [[chosen(quarter >> 1, i, j) for j in range(4)] for i in range(4)]
    for w in range(2):
        nodes = [
            [g_ref[pl.ds(96 * w + 4 * a + b, 6, stride=16), :] for b in range(4)] for a in range(4)
        ]
        out = applied(turned(nodes, code & 7), along_a, along_b)
        for a in range(4):
            for b in range(4):
                g_ref[pl.ds(96 * w + 4 * a + b, 6, stride=16), :] = out[a][b]

    for half in range(2):
        face = codes_ref[13 + half : 14 + half, :]
        axis = face >> 1
        s = jnp.where((face & 1) == 1, 1.0, -1.0)
        lanes = slice(768 + 128 * half, 896 + 128 * half)

        def tangential(base, first):
            x, y, z = (
                gathered[16 * f : 16 * f + 16, lanes]
                for f in (base + (first + k) % 3 for k in range(3))
            )
            return jnp.where(axis == 0, x, jnp.where(axis == 1, y, z))

        m_ref[32 * half : 32 * half + 16, :] = tangential(0, 1) + s * tangential(3, 2)
        m_ref[32 * half + 16 : 32 * half + 32, :] = tangential(0, 2) - s * tangential(3, 1)
    lane = lax.broadcasted_iota(jnp.int32, (4, LANES), 1)
    row = lax.broadcasted_iota(jnp.int32, (4, LANES), 0)

    def weight(second, i, j):
        return jnp.where(second, float(adjoint[1][i, j]), float(adjoint[0][i, j]))

    project_a = [[weight(lane >= 64, i, j) for j in range(4)] for i in range(4)]
    project_b = [[weight(row >= 2, i, j) for j in range(4)] for i in range(4)]
    nodes = [[m_ref[pl.ds(4 * a + b, 4, stride=16), :] for b in range(4)] for a in range(4)]
    out = applied(turned(nodes, codes_ref[8:12, :]), project_a, project_b)
    for a in range(4):
        for b in range(4):
            m_ref[pl.ds(4 * a + b, 4, stride=16), :] = out[a][b]
    pieces = jnp.concatenate([m_ref[0:32, :], m_ref[32:64, :]], axis=1)
    both = jnp.concatenate(halves_of(pieces), axis=0)
    placed = lax.dot_general(
        both, place_ref[...], (((1,), (1,)), ((), ())), preferred_element_type=jnp.float32
    )
    placed = placed[0:32] + placed[32:64]
    for w in range(2):
        for at in range(6):
            rows = slice(96 * w + 16 * at, 96 * w + 16 * at + 16)
            g_ref[rows, :] = (
                g_ref[rows, :] + placed[16 * w : 16 * w + 16, 128 * at : 128 * at + 128]
            )


def add_lift(rate_ref, g_ref):
    for face in range(6):
        a = face // 2
        b, c = (a + 1) % 3, (a + 2) % 3
        s = 3.0 if face % 2 else -3.0
        p = g_ref[16 * face : 16 * face + 16, :]
        q = g_ref[96 + 16 * face : 96 + 16 * face + 16, :]
        for f, value in ((b, -3.0 * p), (c, -3.0 * q), (3 + b, s * q), (3 + c, -s * p)):
            base = 64 * f
            if a == 0:
                at = base + (48 if face % 2 else 0)
                rate_ref[at : at + 16, :] = rate_ref[at : at + 16, :] + value
            elif a == 1:
                for i in range(4):
                    at = base + 16 * i + (12 if face % 2 else 0)
                    rate_ref[at : at + 4, :] = rate_ref[at : at + 4, :] + value[4 * i : 4 * i + 4]
            else:
                at = pl.ds(base + (3 if face % 2 else 0), 16, stride=4)
                rate_ref[at, :] = rate_ref[at, :] + value


def section_kernel(section, *refs):
    refs = list(refs)
    core_ref, u_ref = refs[0:2]
    del refs[0:2]
    register_ref = refs.pop(0) if section else None
    rate_in_ref, part_ref, far_ref, shared_ref = refs[0:4]
    spread_ref, place_ref, codes_ref, scale_ref = refs[4:8]
    del refs[0:8]
    list_spread_ref = None if section else refs.pop(0)
    outs = refs[0:2]
    del refs[0:2]
    if section == 0:
        swap_ref, own_ref = refs[0:2]
        del refs[0:2]
        new_u_ref, new_register_ref = outs
    else:
        new_u_ref, new_register_ref, sems = refs[0:3]
        del refs[0:3]
    r_ref, g_ref, m_ref, rate_ref, t_ref = refs
    core = core_ref[0]
    write_far(core, far_ref, shared_ref, r_ref)
    gathered = part_ref[...] + picked(r_ref[...], spread_ref[NEAR_ROWS:ALL_ROWS, :])
    exterior(gathered, codes_ref, place_ref, g_ref, m_ref)
    rate_ref[...] = rate_in_ref[...]
    add_lift(rate_ref, g_ref)
    copies = []
    for half in range(2):
        rows = slice(192 * half, 192 * half + 192)
        register = scale_ref[half : half + 1, :] * rate_ref[rows, :]
        if section:
            register = register + SECTION_A[section] * register_ref[rows, :]
        new_register_ref[rows, :] = register
        new_u_ref[rows, :] = u_ref[rows, :] + SECTION_B[section] * register
        if section:
            for which, ref in enumerate((new_u_ref, new_register_ref)):
                rows = pl.ds(192 * half, 192)
                copy = pltpu.make_async_copy(
                    ref.at[rows], outs[which].at[rows], sems.at[2 * half + which]
                )
                copy.start()
                copies.append(copy)
    for copy in copies:
        copy.wait()
    if section == 0:
        write_table(new_u_ref, t_ref)
        write_lists(t_ref, list_spread_ref[...], swap_ref, own_ref)


def shaped(rows, columns=LANES, dtype=jnp.float32):
    return jax.ShapeDtypeStruct((rows, columns), dtype)


def called(kernel, core, operands, outputs, scratch, space=pltpu.VMEM, out=pltpu.VMEM):
    first = [] if core is None else [pl.BlockSpec(memory_space=pltpu.SMEM)]
    given = list(operands) if core is None else [core, *operands]
    return pl.pallas_call(
        kernel,
        in_specs=first + [pl.BlockSpec(memory_space=space)] * len(operands),
        out_specs=[pl.BlockSpec(memory_space=out)] * len(outputs),
        out_shape=outputs,
        scratch_shapes=[
            pltpu.VMEM(shape, jnp.float32) if isinstance(shape, tuple) else shape
            for shape in scratch
        ],
        compiler_params=pltpu.CompilerParams(vmem_limit_bytes=VMEM_LIMIT),
    )(*given)


LIST_OUTPUTS = [shaped(5 * UNIT), shaped(3 * UNIT)]


def exchanged(core, swap, own, gather_near):
    count = lax.axis_size("sfc")
    pairs = [[2 * chip, 2 * chip + 1] for chip in range(count // 2)]

    def ahead(chips):
        ends = [(i, i + 2 * chips if i % 2 == 0 else i - 2 * chips) for i in range(count)]
        return [(source, end) for source, end in ends if 0 <= end < count]

    swapped = lax.all_gather(swap, "sfc", axis_index_groups=pairs, tiled=True)
    theirs = lax.dynamic_slice_in_dim(swapped, (1 - core) * (5 * UNIT), 4 * UNIT)
    u = UNIT
    near = jnp.concatenate([own[0:u], theirs[0:u], own[u : 2 * u], theirs[u : 2 * u]])
    far = jnp.concatenate([own[2 * u : 3 * u], theirs[2 * u : 4 * u]])
    near = lax.ppermute(near, "sfc", ahead(1))
    far = lax.ppermute(far, "sfc", ahead(2))
    part, give = gather_near(swapped, near)
    (shared,) = called(join_kernel, None, [give, far], [shaped(3 * u)], [])
    shared = lax.all_gather(shared, "sfc", axis_index_groups=pairs, tiled=True)
    return part, far, shared


def local(
    fields,
    material,
    refinement,
    face_source,
    face_code,
    send_face,
    mortar_source,
    mortar_code,
    mortar_target,
):
    core = lax.rem(lax.axis_index("sfc"), 2).astype(jnp.int32)
    core_at = core.reshape(1)
    volume = jnp.asarray(volume_operand())
    solution = fields.reshape(384, LANES)
    refinement = refinement.reshape(1, LANES)
    target = mortar_target.reshape(1, 64)
    table = (96, 768)
    swap, own = called(
        lists_kernel,
        core_at,
        [
            pltpu.with_memory_space_constraint(operand, pltpu.HBM)
            for operand in (solution, send_face)
        ],
        LIST_OUTPUTS,
        [
            table,
            (384, LANES),
            pltpu.VMEM((8, 192), jnp.int32),
            pltpu.SemaphoreType.DMA,
            pltpu.SemaphoreType.DMA,
        ],
        space=pltpu.HBM,
    )
    register = None
    for section in range(2):
        if section == 0:
            rate, part, list_spread_made, *made = called(
                first_kernel,
                core_at,
                [
                    solution,
                    volume,
                    face_source,
                    mortar_source,
                    face_code,
                    mortar_code,
                    target,
                    material,
                    refinement,
                    send_face,
                ],
                [
                    shaped(384),
                    shaped(96, 1024),
                    shaped(768, 1536, jnp.bfloat16),
                    shaped(ALL_ROWS, 1024, jnp.bfloat16),
                    shaped(768, 256, jnp.bfloat16),
                    shaped(16, LANES, jnp.int32),
                    shaped(2, LANES),
                ],
                [table],
            )
        else:
            rate, part = called(
                local_part,
                None,
                [solution, volume, face_source, mortar_source],
                [shaped(384), shaped(96, 1024)],
                [table],
            )

        def gather_near(swapped, near, part=part):
            operands = [part, made[0], swapped, near]
            outputs = [shaped(96, 1024), shaped(2 * UNIT)]
            return called(near_kernel, core_at, operands, outputs, [(96, NEAR_ROWS)])

        part, far, shared = exchanged(core, swap, own, gather_near)
        operands = [solution] + ([register] if section else [])
        operands += [rate, part, far, shared, *made]
        outputs = [shaped(384), shaped(384)]
        scratch = [(96, ALL_ROWS - NEAR_ROWS), (192, LANES), (64, LANES), (384, LANES), table]
        if section:
            scratch = [(384, LANES), (384, LANES), pltpu.SemaphoreType.DMA((4,)), *scratch]
        if section == 0:
            operands.append(list_spread_made)
            outputs = outputs + LIST_OUTPUTS

        def kernel(*refs, section=section):
            section_kernel(section, *refs)

        results = called(
            kernel,
            core_at,
            operands,
            outputs,
            scratch,
            out=pltpu.HBM if section else pltpu.VMEM,
        )
        solution, register = results[0:2]
        if section == 0:
            swap, own = results[2:4]
    return (solution.reshape(6, 64, LANES), register.reshape(6, 64, LANES))


def solution(mesh):
    return jax.shard_map(
        local,
        mesh=mesh,
        in_specs=(
            P(None, None, "sfc"),
            P(None, "sfc"),
            P("sfc"),
            P(None, "sfc"),
            P(None, "sfc"),
            P(None, "sfc"),
            P(None, "sfc"),
            P(None, "sfc"),
            P("sfc"),
        ),
        out_specs=(P(None, None, "sfc"), P(None, None, "sfc")),
        check_vma=False,
    )
```

```python
import math

import jax
import jax.numpy as jnp
import numpy as np
from jax import lax
from jax.experimental import pallas as pl
from jax.experimental.pallas import tpu as pltpu
from jax.sharding import PartitionSpec as P

STEP_SIZE = 0.02
SECTION_A = (0.0, -567301805773.0 / 1357537059087.0)
SECTION_B = (1432997174477.0 / 9575080441755.0, 5161836677717.0 / 13612068292357.0)
UNIT = 144
LANES = 128
EARLY_ROWS = 1024
ALL_ROWS = 1664
VMEM_LIMIT = 24 * 1024 * 1024


def gll_tables():
    points = np.array([-1.0, -1.0 / math.sqrt(5.0), 1.0 / math.sqrt(5.0), 1.0])
    weights = np.array([1.0, 5.0, 5.0, 1.0]) / 6.0

    def lagrange(where_at):
        values = np.ones((where_at.shape[0], 4))
        for column in range(4):
            for another in range(4):
                if another != column:
                    values[:, column] *= (where_at - points[another]) / (
                        points[column] - points[another]
                    )
        return values

    derivative = np.zeros((4, 4))
    for row_at in range(4):
        for column in range(4):
            summed = 0.0
            for another in range(4):
                if another == column:
                    continue
                factor = 1.0 / (points[column] - points[another])
                for further in range(4):
                    if further != column and further != another:
                        factor *= (points[row_at] - points[further]) / (
                            points[column] - points[further]
                        )
                summed += factor
            derivative[row_at, column] = summed
    halves = [lagrange((points - 1.0) / 2.0), lagrange((points + 1.0) / 2.0)]
    adjoint = [0.5 * halfway.T * weights[None, :] / weights[:, None] for halfway in halves]
    return derivative, halves, adjoint


def face_nodes(face):
    grid = np.arange(64).reshape(4, 4, 4)
    at = 3 if face % 2 else 0
    return [grid[at], grid[:, at], grid[:, :, at]][face // 2].reshape(16)


def volume_map():
    derivative, _, _ = gll_tables()
    eye = np.eye(4)
    along = [
        np.kron(np.kron(derivative, eye), eye),
        np.kron(np.kron(eye, derivative), eye),
        np.kron(np.kron(eye, eye), derivative),
    ]
    whole = np.zeros((6, 64, 6, 64))
    for a in range(3):
        b, c = (a + 1) % 3, (a + 2) % 3
        whole[a, :, 3 + c] += along[b]
        whole[a, :, 3 + b] -= along[c]
        whole[3 + a, :, c] -= along[b]
        whole[3 + a, :, b] += along[c]
    for face in range(6):
        a = face // 2
        b, c = (a + 1) % 3, (a + 2) % 3
        s = 1.0 if face % 2 else -1.0
        for n in face_nodes(face):
            whole[b, n, b, n] += 3.0
            whole[b, n, 3 + c, n] += 3.0 * s
            whole[c, n, c, n] += 3.0
            whole[c, n, 3 + b, n] -= 3.0 * s
            whole[3 + b, n, 3 + b, n] += 3.0
            whole[3 + b, n, c, n] -= 3.0 * s
            whole[3 + c, n, 3 + c, n] += 3.0
            whole[3 + c, n, b, n] += 3.0 * s
    return whole.reshape(384, 384)


def volume_operand():
    whole = volume_map().astype(np.float32)
    high = whole.astype(jnp.bfloat16)
    low = (whole - high.astype(np.float32)).astype(jnp.bfloat16)
    return np.concatenate([high, high, low], axis=1)


def halves_of(value):
    high = value.astype(jnp.bfloat16)
    low = (value - high.astype(jnp.float32)).astype(jnp.bfloat16)
    return high, low


def one_hot(rows, columns):
    at = lax.broadcasted_iota(jnp.int32, (rows, columns.shape[1]), 0)
    return jnp.where(at == columns, 1.0, 0.0).astype(jnp.bfloat16)


def picked(table, columns):
    rows = table.shape[0]
    both = jnp.concatenate(halves_of(table), axis=0)
    out = jnp.dot(both, columns, preferred_element_type=jnp.float32)
    return out[:rows] + out[rows:]


def write_table(u_ref, t_ref, fields=range(6)):
    for f in fields:
        base = 64 * f
        rows = slice(16 * f, 16 * f + 16)
        t_ref[rows, 0:128] = u_ref[base : base + 16, :]
        t_ref[rows, 128:256] = u_ref[base + 48 : base + 64, :]
        for side, at in ((2, 0), (3, 12)):
            for i in range(4):
                start = base + 16 * i + at
                t_ref[16 * f + 4 * i : 16 * f + 4 * i + 4, 128 * side : 128 * side + 128] = u_ref[
                    start : start + 4, :
                ]
        t_ref[rows, 512:640] = u_ref[pl.ds(base, 16, stride=4), :]
        t_ref[rows, 640:768] = u_ref[pl.ds(base + 3, 16, stride=4), :]


def list_spread(core, send_ref):
    def listed(k, lanes):
        return jnp.where(core == 0, send_ref[k : k + 1, lanes], send_ref[7 - k : 8 - k, lanes])

    columns = [listed(k, slice(0, 128)) for k in range(8)]
    for pair in range(4):
        rests = [listed(2 * pair + k, slice(128, 192)) for k in range(2)]
        columns.append(jnp.concatenate(rests, axis=1))
    return jnp.concatenate([one_hot(768, column) for column in columns], axis=1)


def write_lists(t_ref, spread, swap_ref, own_ref):
    out = picked(t_ref[...], spread)
    first = lax.broadcasted_iota(jnp.int32, (48, LANES), 1) < 64
    places = {4 - d: (swap_ref, d - 1) for d in range(1, 5)}
    places[4] = (swap_ref, 4)
    places.update({3 + d: (own_ref, d - 2) for d in range(2, 5)})
    for k in range(8):
        ref, place = places[k]
        ref[UNIT * place : UNIT * place + 96, :] = out[:, 128 * k : 128 * k + 128]
        at = 1024 + 128 * (k // 2)
        upper, lower = out[0:48, at : at + 128], out[48:96, at : at + 128]
        if k % 2 == 0:
            packed = jnp.where(first, upper, pltpu.roll(lower, 64, 1))
        else:
            packed = jnp.where(first, pltpu.roll(upper, 64, 1), lower)
        ref[UNIT * place + 96 : UNIT * place + UNIT, :] = packed


def lists_kernel(
    core_ref, u_hbm, send_hbm, swap_ref, own_ref, t_ref, u_ref, send_ref, send_sem, u_sem
):
    send_copy = pltpu.make_async_copy(send_hbm, send_ref, send_sem)
    send_copy.start()
    u_copy = pltpu.make_async_copy(u_hbm, u_ref, u_sem)
    u_copy.start()
    send_copy.wait()
    spread = list_spread(core_ref[0], send_ref)
    u_copy.wait()
    write_table(u_ref, t_ref)
    write_lists(t_ref, spread, swap_ref, own_ref)


def mortar_row(ref):
    return jnp.concatenate([ref[q : q + 1, :] for q in range(4)], axis=1)


def local_part(u_ref, volume_ref, face_ref, mortar_ref, rate_ref, part_ref, t_ref):
    high, low = halves_of(u_ref[...])
    rate_ref[...] = jnp.dot(
        volume_ref[...],
        jnp.concatenate([high, low, high], axis=0),
        preferred_element_type=jnp.float32,
    )
    write_table(u_ref, t_ref)
    columns = [face_ref[face : face + 1, :] for face in range(6)] + [mortar_row(mortar_ref)]
    spread = jnp.concatenate([one_hot(768, column) for column in columns], axis=1)
    part_ref[...] = picked(t_ref[...], spread)


def first_kernel(
    core_ref,
    u_ref,
    volume_ref,
    face_ref,
    mortar_ref,
    code_ref,
    mortar_code_ref,
    target_ref,
    material_ref,
    refinement_ref,
    send_ref,
    rate_ref,
    part_ref,
    list_spread_ref,
    spread_ref,
    place_ref,
    codes_ref,
    scale_ref,
    t_ref,
):
    local_part(u_ref, volume_ref, face_ref, mortar_ref, rate_ref, part_ref, t_ref)
    core = core_ref[0]
    list_spread_ref[...] = list_spread(core, send_ref)
    at = received_column(core, face_ref[...])
    columns = [at[face : face + 1, :] for face in range(6)]
    columns.append(received_column(core, mortar_row(mortar_ref)))
    spread_ref[...] = jnp.concatenate([one_hot(ALL_ROWS, column) for column in columns], axis=1)
    target = jnp.concatenate([target_ref[...]] * 4, axis=1)
    place_ref[...] = one_hot(768, target)
    face = jnp.zeros_like(target)
    for k in range(1, 6):
        face = face + jnp.where(target >= 128 * k, 1, 0)
    row = lax.broadcasted_iota(jnp.int32, (4, LANES), 0)
    codes = mortar_row(mortar_code_ref)
    codes_ref[0:6, :] = code_ref[...]
    codes_ref[6:8, :] = jnp.zeros((2, LANES), jnp.int32)
    codes_ref[8:12, :] = jnp.where(row >= 2, codes[:, 128:256], codes[:, 0:128])
    codes_ref[12:16, :] = jnp.where(row >= 2, face[:, 128:256], face[:, 0:128])
    level = refinement_ref[...]
    metric = jnp.where(level == 0, 1.0, jnp.where(level == 1, 2.0, 4.0))
    scale_ref[...] = STEP_SIZE * metric * material_ref[...]


def write_units(sources, r_ref):
    count = len(sources)
    first = lax.broadcasted_iota(jnp.int32, (48, LANES), 1) < 64
    none = jnp.zeros((48, LANES), jnp.float32)
    rests = []
    for k, (ref, start) in enumerate(sources):
        r_ref[:, 128 * k : 128 * k + 128] = ref[pl.ds(start, 96), :]
        rests.append(ref[pl.ds(start + 96, 48), :])
    for k in range(0, count, 2):
        even, odd = rests[k], rests[k + 1] if k + 1 < count else none
        at = 128 * count + 64 * k
        r_ref[0:48, at : at + 128] = jnp.where(first, even, pltpu.roll(odd, 64, 1))
        r_ref[48:96, at : at + 128] = jnp.where(first, pltpu.roll(even, 64, 1), odd)


def early_kernel(
    core_ref, part_ref, spread_ref, swapped_ref, near_ref, shared_ref, out_ref, r_ref
):
    other = 1 - core_ref[0]
    swapped = pl.multiple_of(other * (5 * UNIT) + 4 * UNIT, 8)
    shared = [pl.multiple_of(other * (2 * UNIT) + UNIT * place, 8) for place in range(2)]
    sources = [(shared_ref, shared[0]), (shared_ref, shared[1]), (swapped_ref, swapped)]
    write_units(sources + [(near_ref, UNIT), (near_ref, 0)], r_ref)
    out_ref[...] = part_ref[...] + picked(r_ref[...], spread_ref[0:EARLY_ROWS, :])


def give_kernel(part_ref, far_ref, out_ref):
    out_ref[...] = far_ref[2 * UNIT : 3 * UNIT, :]


def write_late(core, far_ref, shared_ref, r_ref):
    shared = pl.multiple_of((1 - core) * UNIT, 8)
    write_units([(shared_ref, shared), (far_ref, UNIT), (far_ref, 0)], r_ref)


def received_column(core, source):
    remote = source - 768
    list_at = jnp.zeros_like(source)
    for k in range(1, 8):
        list_at = list_at + jnp.where(remote >= 192 * k, 1, 0)
    slot = remote - 192 * list_at
    seen = list_at + core * (7 - 2 * list_at)
    early = (seen >= 1) & (seen < 6)
    place = jnp.where(early, seen - 1, jnp.maximum(seen - 5, 0))
    main = jnp.where(early, 0, EARLY_ROWS) + 128 * place + slot
    rest = jnp.where(early, 640, EARLY_ROWS + 384) + 64 * place + slot - 128
    return jnp.where(remote < 0, -1, jnp.where(slot < 128, main, rest))


def turned(nodes, code):
    swap = code >= 4
    flip_a = (code & 1) == 1
    flip_b = (code & 2) == 2
    out = [
        [nodes[a][b] if a == b else jnp.where(swap, nodes[b][a], nodes[a][b]) for b in range(4)]
        for a in range(4)
    ]
    out = [[jnp.where(flip_a, out[3 - a][b], out[a][b]) for b in range(4)] for a in range(4)]
    return [[jnp.where(flip_b, out[a][3 - b], out[a][b]) for b in range(4)] for a in range(4)]


def applied(nodes, along_a, along_b):
    def summed(terms):
        return (terms[0] + terms[1]) + (terms[2] + terms[3])

    half = [
        [summed([along_a[a][x] * nodes[x][b] for x in range(4)]) for b in range(4)]
        for a in range(4)
    ]
    return [
        [summed([along_b[b][y] * half[a][y] for y in range(4)]) for b in range(4)]
        for a in range(4)
    ]


def exterior(gathered, codes_ref, place_ref, g_ref, m_ref):
    _, halves, adjoint = gll_tables()
    for face in range(6):
        a = face // 2
        b, c = (a + 1) % 3, (a + 2) % 3
        s = 1.0 if face % 2 else -1.0
        boundary = (codes_ref[face : face + 1, :] >> 3) == 1
        sign = jnp.where(boundary, -1.0, 1.0)

        def field(index):
            return gathered[16 * index : 16 * index + 16, 128 * face : 128 * face + 128]

        g_ref[16 * face : 16 * face + 16, :] = sign * field(b) + s * field(3 + c)
        g_ref[96 + 16 * face : 96 + 16 * face + 16, :] = sign * field(c) - s * field(3 + b)
    code = codes_ref[0:6, :]
    kind = code >> 3
    quarter = kind - 2
    plain = kind < 2
    live = kind < 6

    def chosen(which, row, column):
        refined = jnp.where(
            which == 1, float(halves[1][row, column]), float(halves[0][row, column])
        )
        kept = jnp.where(plain, 1.0 if row == column else 0.0, refined)
        return jnp.where(live, kept, 0.0)

    along_a = [[chosen(quarter & 1, i, j) for j in range(4)] for i in range(4)]
    along_b = [[chosen(quarter >> 1, i, j) for j in range(4)] for i in range(4)]
    for w in range(2):
        nodes = [
            [g_ref[pl.ds(96 * w + 4 * a + b, 6, stride=16), :] for b in range(4)] for a in range(4)
        ]
        out = applied(turned(nodes, code & 7), along_a, along_b)
        for a in range(4):
            for b in range(4):
                g_ref[pl.ds(96 * w + 4 * a + b, 6, stride=16), :] = out[a][b]

    for half in range(2):
        face = codes_ref[13 + half : 14 + half, :]
        axis = face >> 1
        s = jnp.where((face & 1) == 1, 1.0, -1.0)
        lanes = slice(768 + 128 * half, 896 + 128 * half)

        def tangential(base, first):
            x, y, z = (
                gathered[16 * f : 16 * f + 16, lanes]
                for f in (base + (first + k) % 3 for k in range(3))
            )
            return jnp.where(axis == 0, x, jnp.where(axis == 1, y, z))

        m_ref[32 * half : 32 * half + 16, :] = tangential(0, 1) + s * tangential(3, 2)
        m_ref[32 * half + 16 : 32 * half + 32, :] = tangential(0, 2) - s * tangential(3, 1)
    lane = lax.broadcasted_iota(jnp.int32, (4, LANES), 1)
    row = lax.broadcasted_iota(jnp.int32, (4, LANES), 0)

    def weight(second, i, j):
        return jnp.where(second, float(adjoint[1][i, j]), float(adjoint[0][i, j]))

    project_a = [[weight(lane >= 64, i, j) for j in range(4)] for i in range(4)]
    project_b = [[weight(row >= 2, i, j) for j in range(4)] for i in range(4)]
    nodes = [[m_ref[pl.ds(4 * a + b, 4, stride=16), :] for b in range(4)] for a in range(4)]
    out = applied(turned(nodes, codes_ref[8:12, :]), project_a, project_b)
    for a in range(4):
        for b in range(4):
            m_ref[pl.ds(4 * a + b, 4, stride=16), :] = out[a][b]
    pieces = jnp.concatenate([m_ref[0:32, :], m_ref[32:64, :]], axis=1)
    both = jnp.concatenate(halves_of(pieces), axis=0)
    placed = lax.dot_general(
        both, place_ref[...], (((1,), (1,)), ((), ())), preferred_element_type=jnp.float32
    )
    placed = placed[0:32] + placed[32:64]
    for w in range(2):
        for at in range(6):
            rows = slice(96 * w + 16 * at, 96 * w + 16 * at + 16)
            g_ref[rows, :] = (
                g_ref[rows, :] + placed[16 * w : 16 * w + 16, 128 * at : 128 * at + 128]
            )


def add_lift(rate_ref, g_ref):
    for face in range(6):
        a = face // 2
        b, c = (a + 1) % 3, (a + 2) % 3
        s = 3.0 if face % 2 else -3.0
        p = g_ref[16 * face : 16 * face + 16, :]
        q = g_ref[96 + 16 * face : 96 + 16 * face + 16, :]
        for f, value in ((b, -3.0 * p), (c, -3.0 * q), (3 + b, s * q), (3 + c, -s * p)):
            base = 64 * f
            if a == 0:
                at = base + (48 if face % 2 else 0)
                rate_ref[at : at + 16, :] = rate_ref[at : at + 16, :] + value
            elif a == 1:
                for i in range(4):
                    at = base + 16 * i + (12 if face % 2 else 0)
                    rate_ref[at : at + 4, :] = rate_ref[at : at + 4, :] + value[4 * i : 4 * i + 4]
            else:
                at = pl.ds(base + (3 if face % 2 else 0), 16, stride=4)
                rate_ref[at, :] = rate_ref[at, :] + value


def section_kernel(section, *refs):
    refs = list(refs)
    core_ref, u_ref = refs[0:2]
    del refs[0:2]
    register_ref = refs.pop(0) if section else None
    rate_in_ref, part_ref, far_ref, shared_ref = refs[0:4]
    spread_ref, place_ref, codes_ref, scale_ref = refs[4:8]
    del refs[0:8]
    list_spread_ref = None if section else refs.pop(0)
    outs = refs[0:2]
    del refs[0:2]
    if section == 0:
        swap_ref, own_ref = refs[0:2]
        del refs[0:2]
        new_u_ref, new_register_ref = outs
    else:
        new_u_ref, new_register_ref, sems = refs[0:3]
        del refs[0:3]
    r_ref, g_ref, m_ref, rate_ref, t_ref = refs
    core = core_ref[0]
    write_late(core, far_ref, shared_ref, r_ref)
    gathered = part_ref[...] + picked(r_ref[...], spread_ref[EARLY_ROWS:ALL_ROWS, :])
    exterior(gathered, codes_ref, place_ref, g_ref, m_ref)
    rate_ref[...] = rate_in_ref[...]
    add_lift(rate_ref, g_ref)
    copies = []
    for half in range(2):
        rows = slice(192 * half, 192 * half + 192)
        register = scale_ref[half : half + 1, :] * rate_ref[rows, :]
        if section:
            register = register + SECTION_A[section] * register_ref[rows, :]
        new_register_ref[rows, :] = register
        new_u_ref[rows, :] = u_ref[rows, :] + SECTION_B[section] * register
        if section:
            for which, ref in enumerate((new_u_ref, new_register_ref)):
                rows = pl.ds(192 * half, 192)
                copy = pltpu.make_async_copy(
                    ref.at[rows], outs[which].at[rows], sems.at[2 * half + which]
                )
                copy.start()
                copies.append(copy)
    for copy in copies:
        copy.wait()
    if section == 0:
        write_table(new_u_ref, t_ref)
        write_lists(t_ref, list_spread_ref[...], swap_ref, own_ref)


def shaped(rows, columns=LANES, dtype=jnp.float32):
    return jax.ShapeDtypeStruct((rows, columns), dtype)


def called(kernel, core, operands, outputs, scratch, space=pltpu.VMEM, out=pltpu.VMEM):
    first = [] if core is None else [pl.BlockSpec(memory_space=pltpu.SMEM)]
    given = list(operands) if core is None else [core, *operands]
    return pl.pallas_call(
        kernel,
        in_specs=first + [pl.BlockSpec(memory_space=space)] * len(operands),
        out_specs=[pl.BlockSpec(memory_space=out)] * len(outputs),
        out_shape=outputs,
        scratch_shapes=[
            pltpu.VMEM(shape, jnp.float32) if isinstance(shape, tuple) else shape
            for shape in scratch
        ],
        compiler_params=pltpu.CompilerParams(vmem_limit_bytes=VMEM_LIMIT),
    )(*given)


LIST_OUTPUTS = [shaped(5 * UNIT), shaped(3 * UNIT)]


def exchanged(core, swap, own, gather_early):
    count = lax.axis_size("sfc")
    pairs = [[2 * chip, 2 * chip + 1] for chip in range(count // 2)]

    def ahead(chips):
        ends = [(i, i + 2 * chips if i % 2 == 0 else i - 2 * chips) for i in range(count)]
        return [(source, end) for source, end in ends if 0 <= end < count]

    swapped = lax.all_gather(swap, "sfc", axis_index_groups=pairs, tiled=True)
    theirs = lax.dynamic_slice_in_dim(swapped, (1 - core) * (5 * UNIT), 4 * UNIT)
    u = UNIT
    near = jnp.concatenate([own[0:u], theirs[0:u], own[u : 2 * u], theirs[u : 2 * u]])
    far = jnp.concatenate([own[2 * u : 3 * u], theirs[2 * u : 4 * u]])
    near = lax.ppermute(near, "sfc", ahead(1))
    far = lax.ppermute(far, "sfc", ahead(2))

    def shared(given):
        return lax.all_gather(given, "sfc", axis_index_groups=pairs, tiled=True)

    part = gather_early(swapped, near, shared(near[2 * u : 4 * u]))
    (given,) = called(give_kernel, None, [part, far], [shaped(u)], [])
    return part, far, shared(given)


def local(
    fields,
    material,
    refinement,
    face_source,
    face_code,
    send_face,
    mortar_source,
    mortar_code,
    mortar_target,
):
    core = lax.rem(lax.axis_index("sfc"), 2).astype(jnp.int32)
    core_at = core.reshape(1)
    volume = jnp.asarray(volume_operand())
    solution = fields.reshape(384, LANES)
    refinement = refinement.reshape(1, LANES)
    target = mortar_target.reshape(1, 64)
    table = (96, 768)
    swap, own = called(
        lists_kernel,
        core_at,
        [
            pltpu.with_memory_space_constraint(operand, pltpu.HBM)
            for operand in (solution, send_face)
        ],
        LIST_OUTPUTS,
        [
            table,
            (384, LANES),
            pltpu.VMEM((8, 192), jnp.int32),
            pltpu.SemaphoreType.DMA,
            pltpu.SemaphoreType.DMA,
        ],
        space=pltpu.HBM,
    )
    register = None
    for section in range(2):
        if section == 0:
            rate, part, list_spread_made, *made = called(
                first_kernel,
                core_at,
                [
                    solution,
                    volume,
                    face_source,
                    mortar_source,
                    face_code,
                    mortar_code,
                    target,
                    material,
                    refinement,
                    send_face,
                ],
                [
                    shaped(384),
                    shaped(96, 1024),
                    shaped(768, 1536, jnp.bfloat16),
                    shaped(ALL_ROWS, 1024, jnp.bfloat16),
                    shaped(768, 256, jnp.bfloat16),
                    shaped(16, LANES, jnp.int32),
                    shaped(2, LANES),
                ],
                [table],
            )
        else:
            rate, part = called(
                local_part,
                None,
                [solution, volume, face_source, mortar_source],
                [shaped(384), shaped(96, 1024)],
                [table],
            )

        def gather_early(swapped, near, shared, part=part):
            operands = [part, made[0], swapped, near, shared]
            outputs = [shaped(96, 1024)]
            return called(early_kernel, core_at, operands, outputs, [(96, EARLY_ROWS)])[0]

        part, far, shared = exchanged(core, swap, own, gather_early)
        operands = [solution] + ([register] if section else [])
        operands += [rate, part, far, shared, *made]
        outputs = [shaped(384), shaped(384)]
        scratch = [(96, ALL_ROWS - EARLY_ROWS), (192, LANES), (64, LANES), (384, LANES), table]
        if section:
            scratch = [(384, LANES), (384, LANES), pltpu.SemaphoreType.DMA((4,)), *scratch]
        if section == 0:
            operands.append(list_spread_made)
            outputs = outputs + LIST_OUTPUTS

        def kernel(*refs, section=section):
            section_kernel(section, *refs)

        results = called(
            kernel,
            core_at,
            operands,
            outputs,
            scratch,
            out=pltpu.HBM if section else pltpu.VMEM,
        )
        solution, register = results[0:2]
        if section == 0:
            swap, own = results[2:4]
    return (solution.reshape(6, 64, LANES), register.reshape(6, 64, LANES))


def solution(mesh):
    return jax.shard_map(
        local,
        mesh=mesh,
        in_specs=(
            P(None, None, "sfc"),
            P(None, "sfc"),
            P("sfc"),
            P(None, "sfc"),
            P(None, "sfc"),
            P(None, "sfc"),
            P(None, "sfc"),
            P(None, "sfc"),
            P("sfc"),
        ),
        out_specs=(P(None, None, "sfc"), P(None, None, "sfc")),
        check_vma=False,
    )
```

```python
import math

import jax
import jax.numpy as jnp
import numpy as np
from jax import lax
from jax.experimental import pallas as pl
from jax.experimental.pallas import tpu as pltpu
from jax.sharding import PartitionSpec as P

STEP_SIZE = 0.02
SECTION_A = (0.0, -567301805773.0 / 1357537059087.0)
SECTION_B = (1432997174477.0 / 9575080441755.0, 5161836677717.0 / 13612068292357.0)
UNIT = 144
LANES = 128
EARLY_ROWS = 1024
ALL_ROWS = 1664
VMEM_LIMIT = 24 * 1024 * 1024


def gll_tables():
    points = np.array([-1.0, -1.0 / math.sqrt(5.0), 1.0 / math.sqrt(5.0), 1.0])
    weights = np.array([1.0, 5.0, 5.0, 1.0]) / 6.0

    def lagrange(where_at):
        values = np.ones((where_at.shape[0], 4))
        for column in range(4):
            for another in range(4):
                if another != column:
                    values[:, column] *= (where_at - points[another]) / (
                        points[column] - points[another]
                    )
        return values

    derivative = np.zeros((4, 4))
    for row_at in range(4):
        for column in range(4):
            summed = 0.0
            for another in range(4):
                if another == column:
                    continue
                factor = 1.0 / (points[column] - points[another])
                for further in range(4):
                    if further != column and further != another:
                        factor *= (points[row_at] - points[further]) / (
                            points[column] - points[further]
                        )
                summed += factor
            derivative[row_at, column] = summed
    halves = [lagrange((points - 1.0) / 2.0), lagrange((points + 1.0) / 2.0)]
    adjoint = [0.5 * halfway.T * weights[None, :] / weights[:, None] for halfway in halves]
    return derivative, halves, adjoint


def face_nodes(face):
    grid = np.arange(64).reshape(4, 4, 4)
    at = 3 if face % 2 else 0
    return [grid[at], grid[:, at], grid[:, :, at]][face // 2].reshape(16)


def volume_map():
    derivative, _, _ = gll_tables()
    eye = np.eye(4)
    along = [
        np.kron(np.kron(derivative, eye), eye),
        np.kron(np.kron(eye, derivative), eye),
        np.kron(np.kron(eye, eye), derivative),
    ]
    whole = np.zeros((6, 64, 6, 64))
    for a in range(3):
        b, c = (a + 1) % 3, (a + 2) % 3
        whole[a, :, 3 + c] += along[b]
        whole[a, :, 3 + b] -= along[c]
        whole[3 + a, :, c] -= along[b]
        whole[3 + a, :, b] += along[c]
    for face in range(6):
        a = face // 2
        b, c = (a + 1) % 3, (a + 2) % 3
        s = 1.0 if face % 2 else -1.0
        for n in face_nodes(face):
            whole[b, n, b, n] += 3.0
            whole[b, n, 3 + c, n] += 3.0 * s
            whole[c, n, c, n] += 3.0
            whole[c, n, 3 + b, n] -= 3.0 * s
            whole[3 + b, n, 3 + b, n] += 3.0
            whole[3 + b, n, c, n] -= 3.0 * s
            whole[3 + c, n, 3 + c, n] += 3.0
            whole[3 + c, n, b, n] += 3.0 * s
    return whole.reshape(384, 384)


def volume_operand():
    whole = volume_map().astype(np.float32)
    high = whole.astype(jnp.bfloat16)
    low = (whole - high.astype(np.float32)).astype(jnp.bfloat16)
    return np.concatenate([high, high, low], axis=1)


def halves_of(value):
    high = value.astype(jnp.bfloat16)
    low = (value - high.astype(jnp.float32)).astype(jnp.bfloat16)
    return high, low


def one_hot(rows, columns):
    at = lax.broadcasted_iota(jnp.int32, (rows, columns.shape[1]), 0)
    return jnp.where(at == columns, 1.0, 0.0).astype(jnp.bfloat16)


def picked(table, columns):
    rows = table.shape[0]
    both = jnp.concatenate(halves_of(table), axis=0)
    out = jnp.dot(both, columns, preferred_element_type=jnp.float32)
    return out[:rows] + out[rows:]


def write_table(u_ref, t_ref, fields=range(6)):
    for f in fields:
        base = 64 * f
        rows = slice(16 * f, 16 * f + 16)
        t_ref[rows, 0:128] = u_ref[base : base + 16, :]
        t_ref[rows, 128:256] = u_ref[base + 48 : base + 64, :]
        for side, at in ((2, 0), (3, 12)):
            for i in range(4):
                start = base + 16 * i + at
                t_ref[16 * f + 4 * i : 16 * f + 4 * i + 4, 128 * side : 128 * side + 128] = u_ref[
                    start : start + 4, :
                ]
        t_ref[rows, 512:640] = u_ref[pl.ds(base, 16, stride=4), :]
        t_ref[rows, 640:768] = u_ref[pl.ds(base + 3, 16, stride=4), :]


def list_spread(core, send_ref):
    def listed(k, lanes):
        return jnp.where(core == 0, send_ref[k : k + 1, lanes], send_ref[7 - k : 8 - k, lanes])

    columns = [listed(k, slice(0, 128)) for k in range(8)]
    for pair in range(4):
        rests = [listed(2 * pair + k, slice(128, 192)) for k in range(2)]
        columns.append(jnp.concatenate(rests, axis=1))
    return jnp.concatenate([one_hot(768, column) for column in columns], axis=1)


def write_lists(t_ref, spread, swap_ref, own_ref):
    out = picked(t_ref[...], spread)
    first = lax.broadcasted_iota(jnp.int32, (48, LANES), 1) < 64
    places = {4 - d: (swap_ref, d - 1) for d in range(1, 5)}
    places[4] = (swap_ref, 4)
    places.update({3 + d: (own_ref, d - 2) for d in range(2, 5)})
    for k in range(8):
        ref, place = places[k]
        ref[UNIT * place : UNIT * place + 96, :] = out[:, 128 * k : 128 * k + 128]
        at = 1024 + 128 * (k // 2)
        upper, lower = out[0:48, at : at + 128], out[48:96, at : at + 128]
        if k % 2 == 0:
            packed = jnp.where(first, upper, pltpu.roll(lower, 64, 1))
        else:
            packed = jnp.where(first, pltpu.roll(upper, 64, 1), lower)
        ref[UNIT * place + 96 : UNIT * place + UNIT, :] = packed


def lists_kernel(
    core_ref, u_hbm, send_hbm, swap_ref, own_ref, t_ref, u_ref, send_ref, send_sem, u_sem
):
    send_copy = pltpu.make_async_copy(send_hbm, send_ref, send_sem)
    send_copy.start()
    u_copy = pltpu.make_async_copy(u_hbm, u_ref, u_sem)
    u_copy.start()
    send_copy.wait()
    spread = list_spread(core_ref[0], send_ref)
    u_copy.wait()
    write_table(u_ref, t_ref)
    write_lists(t_ref, spread, swap_ref, own_ref)


def mortar_row(ref):
    return jnp.concatenate([ref[q : q + 1, :] for q in range(4)], axis=1)


def local_part(u_ref, volume_ref, face_ref, mortar_ref, rate_ref, part_ref, t_ref):
    high, low = halves_of(u_ref[...])
    rate_ref[...] = jnp.dot(
        volume_ref[...],
        jnp.concatenate([high, low, high], axis=0),
        preferred_element_type=jnp.float32,
    )
    write_table(u_ref, t_ref)
    columns = [face_ref[face : face + 1, :] for face in range(6)] + [mortar_row(mortar_ref)]
    spread = jnp.concatenate([one_hot(768, column) for column in columns], axis=1)
    part_ref[...] = picked(t_ref[...], spread)


def first_kernel(
    core_ref,
    u_ref,
    volume_ref,
    face_ref,
    mortar_ref,
    code_ref,
    mortar_code_ref,
    target_ref,
    material_ref,
    refinement_ref,
    rate_ref,
    part_ref,
    spread_ref,
    place_ref,
    codes_ref,
    scale_ref,
    t_ref,
):
    local_part(u_ref, volume_ref, face_ref, mortar_ref, rate_ref, part_ref, t_ref)
    core = core_ref[0]
    at = received_column(core, face_ref[...])
    columns = [at[face : face + 1, :] for face in range(6)]
    columns.append(received_column(core, mortar_row(mortar_ref)))
    spread_ref[...] = jnp.concatenate([one_hot(ALL_ROWS, column) for column in columns], axis=1)
    target = jnp.concatenate([target_ref[...]] * 4, axis=1)
    place_ref[...] = one_hot(768, target)
    face = jnp.zeros_like(target)
    for k in range(1, 6):
        face = face + jnp.where(target >= 128 * k, 1, 0)
    row = lax.broadcasted_iota(jnp.int32, (4, LANES), 0)
    codes = mortar_row(mortar_code_ref)
    codes_ref[0:6, :] = code_ref[...]
    codes_ref[6:8, :] = jnp.zeros((2, LANES), jnp.int32)
    codes_ref[8:12, :] = jnp.where(row >= 2, codes[:, 128:256], codes[:, 0:128])
    codes_ref[12:16, :] = jnp.where(row >= 2, face[:, 128:256], face[:, 0:128])
    level = refinement_ref[...]
    metric = jnp.where(level == 0, 1.0, jnp.where(level == 1, 2.0, 4.0))
    scale_ref[...] = STEP_SIZE * metric * material_ref[...]


def write_units(sources, r_ref):
    count = len(sources)
    first = lax.broadcasted_iota(jnp.int32, (48, LANES), 1) < 64
    none = jnp.zeros((48, LANES), jnp.float32)
    rests = []
    for k, (ref, start) in enumerate(sources):
        r_ref[:, 128 * k : 128 * k + 128] = ref[pl.ds(start, 96), :]
        rests.append(ref[pl.ds(start + 96, 48), :])
    for k in range(0, count, 2):
        even, odd = rests[k], rests[k + 1] if k + 1 < count else none
        at = 128 * count + 64 * k
        r_ref[0:48, at : at + 128] = jnp.where(first, even, pltpu.roll(odd, 64, 1))
        r_ref[48:96, at : at + 128] = jnp.where(first, pltpu.roll(even, 64, 1), odd)


def early_kernel(
    core_ref, part_ref, spread_ref, swapped_ref, near_ref, shared_ref, out_ref, r_ref
):
    other = 1 - core_ref[0]
    swapped = pl.multiple_of(other * (5 * UNIT) + 4 * UNIT, 8)
    shared = [pl.multiple_of(other * (2 * UNIT) + UNIT * place, 8) for place in range(2)]
    sources = [(shared_ref, shared[0]), (shared_ref, shared[1]), (swapped_ref, swapped)]
    write_units(sources + [(near_ref, UNIT), (near_ref, 0)], r_ref)
    out_ref[...] = part_ref[...] + picked(r_ref[...], spread_ref[0:EARLY_ROWS, :])


def give_kernel(part_ref, far_ref, out_ref):
    out_ref[...] = far_ref[2 * UNIT : 3 * UNIT, :]


def write_late(core, far_ref, shared_ref, r_ref):
    shared = pl.multiple_of((1 - core) * UNIT, 8)
    write_units([(shared_ref, shared), (far_ref, UNIT), (far_ref, 0)], r_ref)


def received_column(core, source):
    remote = source - 768
    list_at = jnp.zeros_like(source)
    for k in range(1, 8):
        list_at = list_at + jnp.where(remote >= 192 * k, 1, 0)
    slot = remote - 192 * list_at
    seen = list_at + core * (7 - 2 * list_at)
    early = (seen >= 1) & (seen < 6)
    place = jnp.where(early, seen - 1, jnp.maximum(seen - 5, 0))
    main = jnp.where(early, 0, EARLY_ROWS) + 128 * place + slot
    rest = jnp.where(early, 640, EARLY_ROWS + 384) + 64 * place + slot - 128
    return jnp.where(remote < 0, -1, jnp.where(slot < 128, main, rest))


def turned(nodes, code):
    swap = code >= 4
    flip_a = (code & 1) == 1
    flip_b = (code & 2) == 2
    out = [
        [nodes[a][b] if a == b else jnp.where(swap, nodes[b][a], nodes[a][b]) for b in range(4)]
        for a in range(4)
    ]
    out = [[jnp.where(flip_a, out[3 - a][b], out[a][b]) for b in range(4)] for a in range(4)]
    return [[jnp.where(flip_b, out[a][3 - b], out[a][b]) for b in range(4)] for a in range(4)]


def applied(nodes, along_a, along_b):
    def summed(terms):
        return (terms[0] + terms[1]) + (terms[2] + terms[3])

    half = [
        [summed([along_a[a][x] * nodes[x][b] for x in range(4)]) for b in range(4)]
        for a in range(4)
    ]
    return [
        [summed([along_b[b][y] * half[a][y] for y in range(4)]) for b in range(4)]
        for a in range(4)
    ]


def exterior(gathered, codes_ref, place_ref, g_ref, m_ref):
    _, halves, adjoint = gll_tables()
    for face in range(6):
        a = face // 2
        b, c = (a + 1) % 3, (a + 2) % 3
        s = 1.0 if face % 2 else -1.0
        boundary = (codes_ref[face : face + 1, :] >> 3) == 1
        sign = jnp.where(boundary, -1.0, 1.0)

        def field(index):
            return gathered[16 * index : 16 * index + 16, 128 * face : 128 * face + 128]

        g_ref[16 * face : 16 * face + 16, :] = sign * field(b) + s * field(3 + c)
        g_ref[96 + 16 * face : 96 + 16 * face + 16, :] = sign * field(c) - s * field(3 + b)
    code = codes_ref[0:6, :]
    kind = code >> 3
    quarter = kind - 2
    plain = kind < 2
    live = kind < 6

    def chosen(which, row, column):
        refined = jnp.where(
            which == 1, float(halves[1][row, column]), float(halves[0][row, column])
        )
        kept = jnp.where(plain, 1.0 if row == column else 0.0, refined)
        return jnp.where(live, kept, 0.0)

    along_a = [[chosen(quarter & 1, i, j) for j in range(4)] for i in range(4)]
    along_b = [[chosen(quarter >> 1, i, j) for j in range(4)] for i in range(4)]
    for w in range(2):
        nodes = [
            [g_ref[pl.ds(96 * w + 4 * a + b, 6, stride=16), :] for b in range(4)] for a in range(4)
        ]
        out = applied(turned(nodes, code & 7), along_a, along_b)
        for a in range(4):
            for b in range(4):
                g_ref[pl.ds(96 * w + 4 * a + b, 6, stride=16), :] = out[a][b]

    for half in range(2):
        face = codes_ref[13 + half : 14 + half, :]
        axis = face >> 1
        s = jnp.where((face & 1) == 1, 1.0, -1.0)
        lanes = slice(768 + 128 * half, 896 + 128 * half)

        def tangential(base, first):
            x, y, z = (
                gathered[16 * f : 16 * f + 16, lanes]
                for f in (base + (first + k) % 3 for k in range(3))
            )
            return jnp.where(axis == 0, x, jnp.where(axis == 1, y, z))

        m_ref[32 * half : 32 * half + 16, :] = tangential(0, 1) + s * tangential(3, 2)
        m_ref[32 * half + 16 : 32 * half + 32, :] = tangential(0, 2) - s * tangential(3, 1)
    lane = lax.broadcasted_iota(jnp.int32, (4, LANES), 1)
    row = lax.broadcasted_iota(jnp.int32, (4, LANES), 0)

    def weight(second, i, j):
        return jnp.where(second, float(adjoint[1][i, j]), float(adjoint[0][i, j]))

    project_a = [[weight(lane >= 64, i, j) for j in range(4)] for i in range(4)]
    project_b = [[weight(row >= 2, i, j) for j in range(4)] for i in range(4)]
    nodes = [[m_ref[pl.ds(4 * a + b, 4, stride=16), :] for b in range(4)] for a in range(4)]
    out = applied(turned(nodes, codes_ref[8:12, :]), project_a, project_b)
    for a in range(4):
        for b in range(4):
            m_ref[pl.ds(4 * a + b, 4, stride=16), :] = out[a][b]
    pieces = jnp.concatenate([m_ref[0:32, :], m_ref[32:64, :]], axis=1)
    both = jnp.concatenate(halves_of(pieces), axis=0)
    placed = lax.dot_general(
        both, place_ref[...], (((1,), (1,)), ((), ())), preferred_element_type=jnp.float32
    )
    placed = placed[0:32] + placed[32:64]
    for w in range(2):
        for at in range(6):
            rows = slice(96 * w + 16 * at, 96 * w + 16 * at + 16)
            g_ref[rows, :] = (
                g_ref[rows, :] + placed[16 * w : 16 * w + 16, 128 * at : 128 * at + 128]
            )


def add_lift(rate_ref, g_ref):
    for face in range(6):
        a = face // 2
        b, c = (a + 1) % 3, (a + 2) % 3
        s = 3.0 if face % 2 else -3.0
        p = g_ref[16 * face : 16 * face + 16, :]
        q = g_ref[96 + 16 * face : 96 + 16 * face + 16, :]
        for f, value in ((b, -3.0 * p), (c, -3.0 * q), (3 + b, s * q), (3 + c, -s * p)):
            base = 64 * f
            if a == 0:
                at = base + (48 if face % 2 else 0)
                rate_ref[at : at + 16, :] = rate_ref[at : at + 16, :] + value
            elif a == 1:
                for i in range(4):
                    at = base + 16 * i + (12 if face % 2 else 0)
                    rate_ref[at : at + 4, :] = rate_ref[at : at + 4, :] + value[4 * i : 4 * i + 4]
            else:
                at = pl.ds(base + (3 if face % 2 else 0), 16, stride=4)
                rate_ref[at, :] = rate_ref[at, :] + value


def section_kernel(section, *refs):
    refs = list(refs)
    core_ref, u_ref = refs[0:2]
    del refs[0:2]
    register_ref = refs.pop(0) if section else None
    rate_in_ref, part_ref, far_ref, shared_ref = refs[0:4]
    spread_ref, place_ref, codes_ref, scale_ref = refs[4:8]
    del refs[0:8]
    send_ref = None if section else refs.pop(0)
    outs = refs[0:2]
    del refs[0:2]
    if section == 0:
        swap_ref, own_ref = refs[0:2]
        del refs[0:2]
        new_u_ref, new_register_ref = outs
    else:
        new_u_ref, new_register_ref, sems = refs[0:3]
        del refs[0:3]
    r_ref, g_ref, m_ref, rate_ref, t_ref = refs
    core = core_ref[0]
    write_late(core, far_ref, shared_ref, r_ref)
    gathered = part_ref[...] + picked(r_ref[...], spread_ref[EARLY_ROWS:ALL_ROWS, :])
    exterior(gathered, codes_ref, place_ref, g_ref, m_ref)
    rate_ref[...] = rate_in_ref[...]
    add_lift(rate_ref, g_ref)
    copies = []
    for half in range(2):
        rows = slice(192 * half, 192 * half + 192)
        register = scale_ref[half : half + 1, :] * rate_ref[rows, :]
        if section:
            register = register + SECTION_A[section] * register_ref[rows, :]
        new_register_ref[rows, :] = register
        new_u_ref[rows, :] = u_ref[rows, :] + SECTION_B[section] * register
        if section:
            for which, ref in enumerate((new_u_ref, new_register_ref)):
                rows = pl.ds(192 * half, 192)
                copy = pltpu.make_async_copy(
                    ref.at[rows], outs[which].at[rows], sems.at[2 * half + which]
                )
                copy.start()
                copies.append(copy)
    for copy in copies:
        copy.wait()
    if section == 0:
        write_table(new_u_ref, t_ref)
        write_lists(t_ref, list_spread(core, send_ref), swap_ref, own_ref)


def shaped(rows, columns=LANES, dtype=jnp.float32):
    return jax.ShapeDtypeStruct((rows, columns), dtype)


def called(kernel, core, operands, outputs, scratch, space=pltpu.VMEM, out=pltpu.VMEM):
    first = [] if core is None else [pl.BlockSpec(memory_space=pltpu.SMEM)]
    given = list(operands) if core is None else [core, *operands]
    return pl.pallas_call(
        kernel,
        in_specs=first + [pl.BlockSpec(memory_space=space)] * len(operands),
        out_specs=[pl.BlockSpec(memory_space=out)] * len(outputs),
        out_shape=outputs,
        scratch_shapes=[
            pltpu.VMEM(shape, jnp.float32) if isinstance(shape, tuple) else shape
            for shape in scratch
        ],
        compiler_params=pltpu.CompilerParams(vmem_limit_bytes=VMEM_LIMIT),
    )(*given)


LIST_OUTPUTS = [shaped(5 * UNIT), shaped(3 * UNIT)]


def exchanged(core, swap, own, gather_early):
    count = lax.axis_size("sfc")
    pairs = [[2 * chip, 2 * chip + 1] for chip in range(count // 2)]

    def ahead(chips):
        ends = [(i, i + 2 * chips if i % 2 == 0 else i - 2 * chips) for i in range(count)]
        return [(source, end) for source, end in ends if 0 <= end < count]

    swapped = lax.all_gather(swap, "sfc", axis_index_groups=pairs, tiled=True)
    theirs = lax.dynamic_slice_in_dim(swapped, (1 - core) * (5 * UNIT), 4 * UNIT)
    u = UNIT
    near = jnp.concatenate([own[0:u], theirs[0:u], own[u : 2 * u], theirs[u : 2 * u]])
    far = jnp.concatenate([own[2 * u : 3 * u], theirs[2 * u : 4 * u]])
    near = lax.ppermute(near, "sfc", ahead(1))
    far = lax.ppermute(far, "sfc", ahead(2))

    def shared(given):
        return lax.all_gather(given, "sfc", axis_index_groups=pairs, tiled=True)

    part = gather_early(swapped, near, shared(near[2 * u : 4 * u]))
    (given,) = called(give_kernel, None, [part, far], [shaped(u)], [])
    return part, far, shared(given)


def local(
    fields,
    material,
    refinement,
    face_source,
    face_code,
    send_face,
    mortar_source,
    mortar_code,
    mortar_target,
):
    core = lax.rem(lax.axis_index("sfc"), 2).astype(jnp.int32)
    core_at = core.reshape(1)
    volume = jnp.asarray(volume_operand())
    solution = fields.reshape(384, LANES)
    refinement = refinement.reshape(1, LANES)
    target = mortar_target.reshape(1, 64)
    table = (96, 768)
    swap, own = called(
        lists_kernel,
        core_at,
        [
            pltpu.with_memory_space_constraint(operand, pltpu.HBM)
            for operand in (solution, send_face)
        ],
        LIST_OUTPUTS,
        [
            table,
            (384, LANES),
            pltpu.VMEM((8, 192), jnp.int32),
            pltpu.SemaphoreType.DMA,
            pltpu.SemaphoreType.DMA,
        ],
        space=pltpu.HBM,
    )
    register = None
    for section in range(2):
        if section == 0:
            rate, part, *made = called(
                first_kernel,
                core_at,
                [
                    solution,
                    volume,
                    face_source,
                    mortar_source,
                    face_code,
                    mortar_code,
                    target,
                    material,
                    refinement,
                ],
                [
                    shaped(384),
                    shaped(96, 1024),
                    shaped(ALL_ROWS, 1024, jnp.bfloat16),
                    shaped(768, 256, jnp.bfloat16),
                    shaped(16, LANES, jnp.int32),
                    shaped(2, LANES),
                ],
                [table],
            )
        else:
            rate, part = called(
                local_part,
                None,
                [solution, volume, face_source, mortar_source],
                [shaped(384), shaped(96, 1024)],
                [table],
            )

        def gather_early(swapped, near, shared, part=part):
            operands = [part, made[0], swapped, near, shared]
            outputs = [shaped(96, 1024)]
            return called(early_kernel, core_at, operands, outputs, [(96, EARLY_ROWS)])[0]

        part, far, shared = exchanged(core, swap, own, gather_early)
        operands = [solution] + ([register] if section else [])
        operands += [rate, part, far, shared, *made]
        outputs = [shaped(384), shaped(384)]
        scratch = [(96, ALL_ROWS - EARLY_ROWS), (192, LANES), (64, LANES), (384, LANES), table]
        if section:
            scratch = [(384, LANES), (384, LANES), pltpu.SemaphoreType.DMA((4,)), *scratch]
        if section == 0:
            operands.append(send_face)
            outputs = outputs + LIST_OUTPUTS

        def kernel(*refs, section=section):
            section_kernel(section, *refs)

        results = called(
            kernel,
            core_at,
            operands,
            outputs,
            scratch,
            out=pltpu.HBM if section else pltpu.VMEM,
        )
        solution, register = results[0:2]
        if section == 0:
            swap, own = results[2:4]
    return (solution.reshape(6, 64, LANES), register.reshape(6, 64, LANES))


def solution(mesh):
    return jax.shard_map(
        local,
        mesh=mesh,
        in_specs=(
            P(None, None, "sfc"),
            P(None, "sfc"),
            P("sfc"),
            P(None, "sfc"),
            P(None, "sfc"),
            P(None, "sfc"),
            P(None, "sfc"),
            P(None, "sfc"),
            P("sfc"),
        ),
        out_specs=(P(None, None, "sfc"), P(None, None, "sfc")),
        check_vma=False,
    )
```
